32 devices in a mesh: head: 4 (over y, core), seq: 8 (over z, x).
Axes of the slice: x: 2, y: 2, z: 4, core: 2. Of those that a mesh axis runs over, the one named last changes fastest.
Arguments:
- hidden_in: bfloat16 [8, 4, 640, 768], P('seq', 'head'), may hold values from -6 to 6
- norm1_gain: bfloat16 [768], P('head'), may hold values from 0.5 to 1.5
- w_query: bfloat16 [768, 768], P('head'), may hold values from -0.21875 to 0.21875
- w_key: bfloat16 [768, 768], P('head'), may hold values from -0.21875 to 0.21875
- w_value: bfloat16 [768, 768], P('head'), may hold values from -0.21875 to 0.21875
- w_out: bfloat16 [768, 768], P('head'), may hold values from -3 to 3
- rel_bias: bfloat16 [384], P('head'), may hold values from -4 to 4
- norm2_gain: bfloat16 [768], P('head'), may hold values from 0.5 to 1.5
- w_router: bfloat16 [768, 16], P('head'), may hold values from -0.15625 to 0.15625
- w_first: bfloat16 [16, 768, 3072], P('seq', 'head'), may hold values from -0.21875 to 0.21875
- w_second: bfloat16 [16, 3072, 768], P('seq', 'head'), may hold values from -0.21875 to 0.21875
- routes: int32 [8, 4, 640, 2], P('seq', 'head'), may hold values from 0 to 15, all different within a row; in each aligned block of 640 rows (0 to 639, 640 to 1279, ..., all dimensions but the last counted through in order) at most 160 rows name the same one
- priority: int32 [8, 4, 640, 2], P('seq', 'head'), may hold values from 0 to 40959, as said below
- segments: int32 [20480], replicated, may hold values from 0 to 3, as said below
- grad_out: bfloat16 [8, 4, 640, 768], P('seq', 'head'), may hold values from -6 to 6
Outputs:
- output: bfloat16 [8, 4, 640, 768], P('seq', 'head')
- grad_hidden: float32 [8, 4, 640, 768], P('seq', 'head')
- grad_norm1: float32 [768], P('head')
- grad_query: float32 [768, 768], P('head')
- grad_key: float32 [768, 768], P('head')
- grad_value: float32 [768, 768], P('head')
- grad_outproj: float32 [768, 768], P('head')
- grad_rel: float32 [384], P('head')
- grad_norm2: float32 [768], P('head')
- grad_router: float32 [768, 16], P('head')
- grad_first: float32 [16, 768, 3072], P('seq', 'head')
- grad_second: float32 [16, 3072, 768], P('seq', 'head')
The draws below stay inside these ranges and needn't reach their ends.
Inputs may be any that keep to these rules, and one draw needn't show every extreme that they name: `routes`: each row names 2 different experts; in the rows of one device no expert is named more than 160 times. `priority`: every pair has its own number; the pairs of the rows of one device hold 1280 consecutive numbers. `segments`: document numbers never fall along the positions.
All inputs are finite; a program needn't handle non-finite values.
Results may differ from the reference program's by a relative error of at most 0.02.
Values may be sent and summed in bfloat16 or wider, within the bound.
No kernel may reach another device: no remote copies, remote signals or barrier semaphores. Data moves between devices by JAX's collectives and lax.ppermute only.
A program may use at most 320 MiB of HBM per device.

```python
import math
import jax
import jax.numpy as jnp
import numpy as np
from jax import lax

D = 768
HEADS = 12
HEAD_DIM = 64
FF = 3072
TOP = 2
WINDOW = 1024
BUCKETS = 32
TOK_DEV = 640
EXPERTS = 16
SEQ_BLOCKS = 8
HEAD_GROUPS = 4
BLOCK = 2560
TOKENS = 20480
MOST = 160
CAP = 3200


def draw_priority(key, part):
    key = jax.random.fold_in(key, 11)
    order_key, local_key = jax.random.split(key)
    block_total = SEQ_BLOCKS * HEAD_GROUPS
    block_order = jax.random.permutation(order_key, block_total)
    local_keys = jax.random.split(local_key, block_total)
    local_order = jax.vmap(lambda single_key: jax.random.permutation(single_key, TOP * TOK_DEV))(local_keys)
    numbers = block_order[:, None] * (TOP * TOK_DEV) + local_order
    return numbers.reshape(SEQ_BLOCKS, HEAD_GROUPS, TOK_DEV, TOP).astype(jnp.int32)


def draw_segments(key, part):
    key = jax.random.fold_in(key, 23)
    first_key, second_key, third_key = jax.random.split(key, 3)
    first_cut = jax.random.randint(first_key, (), 1, BLOCK // 2)
    second_cut = jax.random.randint(second_key, (), BLOCK // 2, BLOCK)
    third_cut = TOKENS - jax.random.randint(third_key, (), 1, BLOCK)
    positions = jnp.arange(TOKENS, dtype=jnp.int32)
    numbers = (positions >= first_cut).astype(jnp.int32) + (positions >= second_cut).astype(jnp.int32) + (positions >= third_cut).astype(jnp.int32)
    return numbers.astype(jnp.int32)


def block_scale(rng, shape, cuts, smallest, largest):
    def one(dim, shards_of):
        heights = jax.random.uniform(jax.random.fold_in(jax.random.fold_in(rng, 6), dim), (shards_of,), jnp.float32, smallest / len(cuts), largest / len(cuts))
        return jnp.repeat(jnp.exp(heights), shape[dim] // shards_of).reshape((-1,) + (1,) * (len(shape) - dim - 1))

    loudness = one(*cuts[0])
    for cut in cuts[1:]:
        loudness = loudness * one(*cut)
    return loudness


def deal_out(stream_key, own, number, rows, count, top, most, slope):
    ranking = jax.random.permutation(stream_key, count)
    packed, ordinary = load_shares(count, rows * top, most, slope, True), load_shares(count, rows * top, most, slope, False)
    places = jnp.arange(count)

    def named(tallies, turn):
        used = int((tallies > 0).sum())
        fixed = max(1, used // 4)
        shifted = fixed + (places - fixed + turn * (used - fixed)) % max(1, count - fixed)
        return jnp.zeros((count,), jnp.int32).at[ranking[jnp.where(places < fixed, places, shifted)]].set(jnp.asarray(tallies, jnp.int32))

    tallies = jnp.where(number % 4 == 0, named(packed, number // 4), named(ordinary, number - number // 4 - 1))
    mixed = jax.random.permutation(jax.random.fold_in(own, 3), count)
    giver, taker = mixed[0:count // 2 * 2:2], mixed[1:count // 2 * 2:2]
    margin = jnp.minimum(tallies[giver] - 1, most - tallies[taker]) // 2
    margin = jnp.where((giver == ranking[0]) | (taker == ranking[0]) | (tallies[taker] == 0), 0, jnp.maximum(margin, 0))
    shifted = jax.random.randint(jax.random.fold_in(own, 4), (count // 2,), 0, 1 << 20) % (margin + 1)
    tallies = tallies.at[giver].add(-shifted).at[taker].add(shifted)
    members = jnp.searchsorted(jnp.cumsum(tallies), jnp.arange(rows * top), side="right").astype(jnp.int32)
    listing = members.reshape(top, rows).T
    listing = listing[jax.random.permutation(jax.random.fold_in(own, 1), rows)]
    turn = jax.random.randint(jax.random.fold_in(own, 2), (rows, 1), 0, top)
    return jnp.take_along_axis(listing, (jnp.arange(top)[None, :] + turn) % top, axis=1)


def load_shares(number_of, total, most, lean, full):
    loads = [(1 << 20) // math.isqrt(grade ** lean) + 1 for grade in range(1, number_of + 1)]
    largest = most if full else min(most, max(-(-total // number_of), total * loads[0] // sum(loads)))
    least = 1 if total - largest >= number_of - 1 else 0
    holding, rest = [largest] + [least] * (number_of - 1), total - largest - least * (number_of - 1)
    while rest > 0:
        movable = [i for i in range(1, number_of) if holding[i] < largest] or [i for i in range(1, number_of) if holding[i] < most]
        whole, remaining = sum([loads[i] for i in movable]), rest
        for i in movable:
            more = min(most - holding[i], max(1, remaining * loads[i] // whole), rest)
            holding[i] = holding[i] + more
            rest = rest - more
    return np.array(holding)


def bell_draw(key, shape, scale, reach, cuts=(), kind=jnp.bfloat16):
    result = scale * jax.random.normal(key, shape, jnp.float32)
    if cuts:
        result = result * block_scale(key, shape, cuts, -0.22, 0.18)
    return jnp.clip(result, -reach, reach).astype(kind)


def setup_inputs(seed: int = 0) -> dict:
    splits = jax.random.split(jax.random.key(seed), 16)
    hidden_in = bell_draw(splits[0], (SEQ_BLOCKS, HEAD_GROUPS, TOK_DEV, D), 1.0, 6.0, ((0, 8), (1, 4)))
    norm1_gain = jnp.clip(1.0 + 0.1 * jax.random.normal(splits[1], (D,), jnp.float32), 0.5, 1.5).astype(jnp.bfloat16)
    w_query = bell_draw(splits[2], (D, HEADS * HEAD_DIM), D ** -0.5, 0.21875, ((0, 4),))
    w_key = bell_draw(splits[3], (D, HEADS * HEAD_DIM), D ** -0.5, 0.21875, ((0, 4),))
    w_value = bell_draw(splits[4], (D, HEADS * HEAD_DIM), D ** -0.5, 0.21875, ((0, 4),))
    w_out = bell_draw(splits[5], (HEADS * HEAD_DIM, D), (HEAD_DIM // 16) ** -0.5, 3.0, ((0, 4),))
    rel_bias = bell_draw(splits[6], (HEADS * BUCKETS,), 1.0, 4.0, ((0, 4),))
    norm2_gain = jnp.clip(1.0 + 0.1 * jax.random.normal(splits[7], (D,), jnp.float32), 0.5, 1.5).astype(jnp.bfloat16)
    w_router = bell_draw(splits[8], (D, EXPERTS), (2 * D) ** -0.5, 0.15625, ((0, 4),))
    w_first = bell_draw(splits[9], (EXPERTS, D, FF), D ** -0.5, 0.21875, ((0, 8), (1, 4)))
    w_second = bell_draw(splits[10], (EXPERTS, FF, D), (FF // 4) ** -0.5, 0.21875, ((0, 8), (1, 4)))
    routes_keys = jax.random.split(jax.random.fold_in(splits[11], 1), SEQ_BLOCKS * HEAD_GROUPS * TOK_DEV // TOK_DEV)
    routes_turns = jax.random.permutation(jax.random.fold_in(splits[11], 3), SEQ_BLOCKS * HEAD_GROUPS * TOK_DEV // TOK_DEV)
    routes = jax.vmap(lambda own, number: deal_out(jax.random.fold_in(splits[11], 2), own, number, TOK_DEV, EXPERTS, TOP, MOST, 2))(routes_keys, routes_turns).reshape((SEQ_BLOCKS, HEAD_GROUPS, TOK_DEV, TOP))
    priority = draw_priority(jax.random.fold_in(splits[15], 71), 0)
    segments = draw_segments(jax.random.fold_in(splits[15], 71), 0)
    grad_out = bell_draw(splits[14], (SEQ_BLOCKS, HEAD_GROUPS, TOK_DEV, D), 1.0, 6.0, ((0, 8), (1, 4)))
    return {"hidden_in": hidden_in, "norm1_gain": norm1_gain, "w_query": w_query, "w_key": w_key, "w_value": w_value, "w_out": w_out, "rel_bias": rel_bias, "norm2_gain": norm2_gain, "w_router": w_router, "w_first": w_first, "w_second": w_second, "routes": routes, "priority": priority, "segments": segments, "grad_out": grad_out}


@jax.custom_vjp
def low(v):
    return lax.optimization_barrier(v.astype(jnp.bfloat16)).astype(jnp.float32)

@jax.custom_vjp
def low_back(v):
    return v

def low_keep(v):
    return (low(v), None)

def low_pass(kept, grad):
    return (grad,)

def back_keep(v):
    return (v, None)

def back_low(kept, grad):
    return (low(grad),)
low.defvjp(low_keep, low_pass)
low_back.defvjp(back_keep, back_low)
highest = lax.Precision.HIGHEST

def bucket_edges(window_len, bucket_count):
    middle = bucket_count // 2
    edge_list = []
    for number in range(1, bucket_count):
        if number < middle:
            edge_list.append(number)
        else:
            edge_list.append(int(middle * (window_len / middle) ** ((number - middle) / middle)))
    return edge_list

def bucket_index(query_rows, key_rows):
    distance = WINDOW + jnp.arange(query_rows, dtype=jnp.int32)[:, None] - jnp.arange(key_rows, dtype=jnp.int32)[None, :]
    bucket = jnp.zeros(distance.shape, jnp.int32)
    for edge_value in bucket_edges(WINDOW, BUCKETS):
        bucket = bucket + (distance >= edge_value).astype(jnp.int32)
    return (distance, bucket)

def rms_scale(values, gain_vec):
    return values * lax.rsqrt(lax.optimization_barrier(jnp.mean(values * values, axis=-1, keepdims=True)) + 1e-06) * gain_vec

def route_gates(logits, route_rows):
    probability = jax.nn.softmax(logits, axis=-1)
    chosen = jnp.take_along_axis(probability, route_rows, axis=1)
    return chosen / lax.optimization_barrier(jnp.sum(chosen, axis=-1, keepdims=True))

def pair_ranks(pair_routes, pair_prio):
    pair_total = pair_prio.shape[0]
    span_rows = math.gcd(pair_total, 4096)
    by_priority = jnp.zeros((pair_total,), jnp.int32).at[pair_prio].set(pair_routes)
    expert_ids = jnp.arange(EXPERTS, dtype=jnp.int32)

    def count_step(running, piece_ids):
        onehot = (piece_ids[:, None] == expert_ids[None, :]).astype(jnp.int32)
        before = (jnp.cumsum(onehot, axis=0).astype(jnp.int32) - onehot + running[None, :]).astype(jnp.int32)
        running_next = (running + lax.optimization_barrier(jnp.sum(onehot, axis=0))).astype(jnp.int32)
        return (running_next, lax.optimization_barrier(jnp.sum(before * onehot, axis=1)).astype(jnp.int32))
    _, rank_list = lax.scan(count_step, jnp.zeros((EXPERTS,), jnp.int32), by_priority.reshape(-1, span_rows))
    return rank_list.reshape(-1)[pair_prio].astype(jnp.int32)

def attend(queries, keys_in, values_in, rel_table, segments):
    length = queries.shape[0]
    query_rows = min(512, BLOCK)
    key_rows = WINDOW + query_rows
    distance, bucket = bucket_index(query_rows, key_rows)
    allowed = (distance >= 0) & (distance < WINDOW)
    rel_bias_blk = rel_table.reshape(HEADS, BUCKETS)[:, bucket]
    zeros_pad = jnp.zeros((WINDOW,) + keys_in.shape[1:], keys_in.dtype)
    keys_pad = jnp.concatenate([zeros_pad, keys_in], axis=0)
    values_pad = jnp.concatenate([zeros_pad, values_in], axis=0)
    segs_pad = jnp.concatenate([jnp.full((WINDOW,), -1, jnp.int32), segments.astype(jnp.int32)])
    factor = HEAD_DIM ** (-0.5)

    def one_block(row_start):
        query_blk = lax.dynamic_slice_in_dim(queries, row_start, query_rows, 0)
        key_blk = lax.dynamic_slice_in_dim(keys_pad, row_start, key_rows, 0)
        value_blk = lax.dynamic_slice_in_dim(values_pad, row_start, key_rows, 0)
        query_seg = lax.dynamic_slice_in_dim(segments.astype(jnp.int32), row_start, query_rows, 0)
        key_seg = lax.dynamic_slice_in_dim(segs_pad, row_start, key_rows, 0)
        usable = allowed & (query_seg[:, None] == key_seg[None, :])
        scores = jnp.einsum('qhe,khe->hqk', query_blk, key_blk, precision=highest) * factor + rel_bias_blk
        scores = jnp.where(usable[None], low_back(scores), -1e+30)
        weights = low(jax.nn.softmax(scores, axis=-1))
        return jnp.einsum('hqk,khe->qhe', weights, value_blk, precision=highest)
    starts = jnp.arange(length // query_rows, dtype=jnp.int32) * query_rows
    return lax.map(jax.checkpoint(one_block), starts).reshape(length, -1)

def expert_rows(inputs):
    rows, first_w, second_w = inputs
    pre_act = low_back(jnp.dot(rows, first_w, precision=highest))
    act_low = low(jax.nn.gelu(pre_act))
    return low_back(low(jnp.dot(act_low, second_w, precision=highest)))

def reference(hidden_in, norm1_gain, w_query, w_key, w_value, w_out, rel_bias, norm2_gain, w_router, w_first, w_second, routes, priority, segments, grad_out):
    float_type = jnp.float32
    model_width = hidden_in.shape[-1]
    pair_routes = routes.reshape(-1).astype(jnp.int32)
    pair_prio = priority.reshape(-1).astype(jnp.int32)
    route_rows = routes.reshape(-1, TOP).astype(jnp.int32)
    rank_list = pair_ranks(pair_routes, pair_prio)
    kept_mask = rank_list < CAP
    slot_index = jnp.where(kept_mask, pair_routes * CAP + rank_list, EXPERTS * CAP).astype(jnp.int32)
    kept_mat = kept_mask.reshape(-1, TOP).astype(float_type)

    def layer(hidden, gain_one, query_w, key_w, value_w, out_w, rel_table, gain_two, router_w, first_w, second_w):
        normed = low(rms_scale(hidden, gain_one))
        queries = low_back(low(jnp.dot(normed, query_w, precision=highest))).reshape(-1, HEADS, HEAD_DIM)
        keys_in = low_back(low(jnp.dot(normed, key_w, precision=highest))).reshape(-1, HEADS, HEAD_DIM)
        values_in = low_back(low(jnp.dot(normed, value_w, precision=highest))).reshape(-1, HEADS, HEAD_DIM)
        mixed_out = low_back(low(attend(queries, keys_in, values_in, rel_table, segments)))
        middle = hidden + low_back(jnp.dot(mixed_out, out_w, precision=highest))
        normed_two = low(rms_scale(middle, gain_two))
        gate_mat = route_gates(low_back(jnp.dot(normed_two, router_w, precision=highest)), route_rows)
        pair_rows = low_back(jnp.broadcast_to(normed_two[:, None, :], (normed_two.shape[0], TOP, model_width)).reshape(-1, model_width))
        buffer = jnp.zeros((EXPERTS * CAP + 1, model_width), pair_rows.dtype).at[slot_index].set(pair_rows)
        buffer = buffer[:EXPERTS * CAP].reshape(EXPERTS, CAP, model_width)
        results = lax.map(jax.checkpoint(expert_rows), (buffer, first_w, second_w))
        padded = jnp.concatenate([results.reshape(-1, model_width), jnp.zeros((1, model_width), results.dtype)], axis=0)
        expert_out = padded[slot_index].reshape(-1, TOP, model_width)
        return middle + lax.optimization_barrier(jnp.sum((gate_mat * kept_mat)[:, :, None] * expert_out, axis=1))
    hidden = hidden_in.reshape(-1, model_width).astype(float_type)
    final_out, pullback = jax.vjp(layer, hidden, norm1_gain.astype(float_type), w_query.astype(float_type), w_key.astype(float_type), w_value.astype(float_type), w_out.astype(float_type), rel_bias.astype(float_type), norm2_gain.astype(float_type), w_router.astype(float_type), w_first.astype(float_type), w_second.astype(float_type))
    gradients = pullback(grad_out.reshape(-1, model_width).astype(float_type))
    return (final_out.astype(jnp.bfloat16).reshape(hidden_in.shape), gradients[0].reshape(hidden_in.shape), gradients[1], gradients[2], gradients[3], gradients[4], gradients[5], gradients[6], gradients[7], gradients[8], gradients[9], gradients[10])
```

```python
import functools

import jax
import jax.numpy as jnp
import numpy as np
from jax import lax
from jax.experimental import pallas as pl
from jax.experimental.pallas import tpu as pltpu
from jax.sharding import PartitionSpec as P

HEAD_DIM = 64
WINDOW = 1024
BUCKETS = 32
QB = 256
CHUNKS = WINDOW // QB + 1
KEYS = CHUNKS * QB
MASKED = -1e30
epsilon = 1e-06
bfloat = jnp.bfloat16
single = jnp.float32
MIB = 1 << 20

VMEM = pl.BlockSpec(memory_space=pltpu.VMEM)
SMEM = pl.BlockSpec(memory_space=pltpu.SMEM)


def dot(a, b, dims=((1,), (0,))):
    return lax.dot_general(a, b, (dims, ((), ())), preferred_element_type=single)


NN = ((1,), (0,))
NT = ((1,), (1,))
TN = ((0,), (0,))


def params(mib, grid=0):
    extra = {"dimension_semantics": ("arbitrary",) * grid} if grid else {}
    return pltpu.CompilerParams(vmem_limit_bytes=mib * MIB, **extra)


def cost(flops, moved, trans=0):
    return pl.CostEstimate(flops=int(flops), bytes_accessed=int(moved), transcendentals=int(trans))


def bucket_edges(window_len, bucket_count):
    middle = bucket_count // 2
    edge_list = []
    for number in range(1, bucket_count):
        if number < middle:
            edge_list.append(number)
        else:
            edge_list.append(int(middle * (window_len / middle) ** ((number - middle) / middle)))
    return edge_list


def lane_tables():
    lane = np.arange(2 * QB)
    offset = np.where(lane < QB, lane, lane - 2 * QB)
    distance = WINDOW - QB * np.arange(CHUNKS)[:, None] + offset[None, :]
    allowed = (distance >= 0) & (distance < WINDOW)
    bucket = np.zeros(distance.shape, np.int32)
    for edge_value in bucket_edges(WINDOW, BUCKETS):
        bucket = bucket + (distance >= edge_value)
    hot = (bucket.reshape(-1)[:, None] == np.arange(BUCKETS)[None, :]) & allowed.reshape(-1)[:, None]
    return hot, allowed


GAINS = 16


def pack_kernel(order, wq, wk, wv, router_t, gains, own, far, near, both):
    part, width = wq.shape
    experts = router_t.shape[0]
    for lane in range(width // part):

        @pl.when(order[0] == lane)
        def _():
            for mask, ref in ((0, own), (2, far), (1, near), (3, both)):
                at = (lane ^ mask) * part
                for number, weight in enumerate((wq, wk, wv)):
                    ref[number * part : (number + 1) * part, :] = weight[:, at : at + part]

    for ref in (own, far, near, both):
        ref[3 * part : 3 * part + experts, :] = router_t[...]
        ref[3 * part + experts :, :] = gains[...]


def pack(order, wq, wk, wv, router_t, gains):
    part = wq.shape[0]
    tall = 3 * part + router_t.shape[0] + GAINS
    return pl.pallas_call(
        pack_kernel,
        in_specs=[SMEM] + [VMEM] * 5,
        out_specs=[VMEM] * 4,
        out_shape=[jax.ShapeDtypeStruct((tall, part), bfloat)] * 4,
        compiler_params=params(16),
        name="pack",
    )(order, wq, wk, wv, router_t, gains)


def project_kernel(
    order, x0, x1, x2, x3, p0, p1, p2, p3, n_out, qt_out, kv_out, rows_out, router_out, gain_out, wq, wk, wv
):
    rows, width = x0.shape
    heads = kv_out.shape[0]
    part = heads * HEAD_DIM
    experts = router_out.shape[0]
    packed = (p0, p1, p2, p3)
    for place, ref in enumerate(packed):
        at = pl.ds(pl.multiple_of(order[place] * part, 64), part)
        for number, weight in enumerate((wq, wk, wv)):
            weight[at, :] = ref[number * part : (number + 1) * part, :]

    def spread(begin, count):
        found = []
        for lane in range(len(packed)):
            piece = packed[0][begin : begin + count, :]
            for place in range(1, len(packed)):
                piece = jnp.where(order[place] == lane, packed[place][begin : begin + count, :], piece)
            found.append(piece)
        return jnp.concatenate(found, axis=1)

    router_out[...] = spread(3 * part, experts)
    gains = spread(3 * part + experts, GAINS).astype(single)
    gain_out[...] = gains[0:8, :]
    wq_t = wq[...].T
    k_t = wk[...].T
    v_t = wv[...].T
    for head in range(heads):
        at = slice(head * HEAD_DIM, (head + 1) * HEAD_DIM)
        for number, value in enumerate((wq_t, k_t, v_t)):
            begin = (3 * head + number) * HEAD_DIM
            rows_out[begin : begin + HEAD_DIM, :] = value[at, :]
    for place, ref in enumerate((x0, x1, x2, x3)):
        block = order[place]
        values = ref[...].astype(single)
        inverse = lax.rsqrt(jnp.mean(values * values, axis=-1, keepdims=True) + epsilon)
        normed = (values * inverse * gain_out[0:1, :]).astype(bfloat)
        n_out[block] = normed
        at = pl.ds(pl.multiple_of(block * rows, 128), rows)
        qt = dot(wq_t, normed, NT).astype(bfloat)
        qt_out[:, at] = qt * bfloat(HEAD_DIM**-0.5)
        for head in range(heads):
            begin = 3 * head * HEAD_DIM + HEAD_DIM
            kv = dot(normed, rows_out[begin : begin + 2 * HEAD_DIM, :], NT)
            kv_out[head, at, :] = kv.astype(bfloat)


def project(order, pieces, packed, heads, experts):
    rows, width = pieces[0].shape
    total = rows * len(pieces)
    part = heads * HEAD_DIM
    return pl.pallas_call(
        project_kernel,
        in_specs=[SMEM] + [VMEM] * 8,
        out_specs=[VMEM] * 6,
        out_shape=[
            jax.ShapeDtypeStruct((len(pieces), rows, width), bfloat),
            jax.ShapeDtypeStruct((part, total), bfloat),
            jax.ShapeDtypeStruct((heads, total, 2 * HEAD_DIM), bfloat),
            jax.ShapeDtypeStruct((3 * part, width), bfloat),
            jax.ShapeDtypeStruct((experts, width), bfloat),
            jax.ShapeDtypeStruct((8, width), single),
        ],
        scratch_shapes=[pltpu.VMEM((width, part), bfloat)] * 3,
        compiler_params=params(40),
        cost_estimate=cost(2 * total * width * 3 * part, 4 * total * width),
        name="project",
    )(order, *pieces, *packed)


def eye(size):
    return (
        lax.broadcasted_iota(jnp.int32, (size, size), 0) == lax.broadcasted_iota(jnp.int32, (size, size), 1)
    ).astype(bfloat)


def stage_attention(kvp, kv, vecs, kv_all, kvt_all, bias):
    heads = kv_all.shape[0]
    unit = eye(2 * HEAD_DIM)
    for head in range(heads):
        if kvp is None:
            kv_all[head] = kv[head]
        else:
            kv_all[head, :WINDOW, :] = kvp[head]
            kv_all[head, WINDOW:, :] = kv[head]
        kvt_all[head] = dot(unit, kv_all[head], NT).astype(bfloat)
        for chunk in range(CHUNKS):
            row = jnp.broadcast_to(vecs[head, chunk : chunk + 1, :], (QB, 2 * QB))
            tile = pltpu.roll(row, 0, 1, stride=1, stride_axis=0)
            bias[head, chunk * QB : (chunk + 1) * QB, :] = tile[:, :QB]


def keep_rows(scores, step, low):
    key = lax.broadcasted_iota(jnp.int32, scores.shape, 0) + step * QB
    return jnp.where(key >= low, scores, MASKED)


def query_tile(step, first, pieces):
    found = []
    for half in range(QB // 128):
        piece = (step + first) * (QB // 128) + half
        found.append((piece // pieces, pl.ds(pl.multiple_of((piece % pieces) * 128, 128), 128)))
    return found


def forward_kernel(first, order, need, low, qt, keys_in, vecs, *rest):
    *more, out, lse, kv_all, kvt_all, bias = rest
    step = pl.program_id(0)
    heads = kv_all.shape[0]
    pieces = out.shape[2] // 128

    @pl.when(step == 0)
    def _():
        if more:
            stage_attention(more[0], keys_in, vecs, kv_all, kvt_all, bias)
            out[...] = more[1][...]
        else:
            stage_attention(None, keys_in, vecs, kv_all, kvt_all, bias)

    start = pl.multiple_of(step * QB, QB)

    def run(masked):
        for head in range(heads):
            keys = kv_all[head, pl.ds(start, KEYS), :]
            query = qt[head * HEAD_DIM : (head + 1) * HEAD_DIM, :]
            query = jnp.concatenate([query, jnp.zeros_like(query)], axis=0)
            scores = dot(keys, query) + bias[head]
            if masked:
                scores = keep_rows(scores, step + first, low[...])
            peak = jnp.max(scores, axis=0, keepdims=True)
            expo = jnp.exp(scores - peak)
            total = jnp.sum(expo, axis=0, keepdims=True)
            values = kvt_all[head, HEAD_DIM:, pl.ds(start, KEYS)]
            mixed = dot(values, expo.astype(bfloat)) * (1.0 / total)
            mixed = mixed.astype(bfloat)
            at = slice(head * HEAD_DIM, (head + 1) * HEAD_DIM)
            for half, (owner, place) in enumerate(query_tile(step, first, pieces)):
                out[jnp.bitwise_xor(owner, order[0]), at, place] = mixed[:, half * 128 : (half + 1) * 128]
            lse[0, head : head + 1, :] = peak + jnp.log(total)

    pl.when(need[step + first] > 0)(lambda: run(True))
    pl.when(need[step + first] <= 0)(lambda: run(False))


def attention_forward(first, steps, order, need, low, qt, kvp, kv, vecs, lanes, begun=None):
    heads, total, packed = kv.shape
    width = heads * HEAD_DIM
    held = KEYS + (steps - 1) * QB
    own = held - (0 if kvp is None else WINDOW)
    more = [] if kvp is None else [kvp, begun]
    return pl.pallas_call(
        functools.partial(forward_kernel, first),
        grid=(steps,),
        in_specs=[
            SMEM,
            SMEM,
            pl.BlockSpec((1, QB), lambda i: (0, i + first)),
            pl.BlockSpec((width, QB), lambda i: (0, i + first)),
            pl.BlockSpec((heads, own, packed), lambda i: (0, 0, 0)),
            VMEM,
        ]
        + [VMEM] * len(more),
        out_specs=[VMEM, pl.BlockSpec((1, 8, QB), lambda i: (i, 0, 0))],
        out_shape=[
            jax.ShapeDtypeStruct((lanes, width, total // lanes), bfloat),
            jax.ShapeDtypeStruct((steps, 8, QB), single),
        ],
        scratch_shapes=[
            pltpu.VMEM((heads, held, packed), bfloat),
            pltpu.VMEM((heads, packed, held), bfloat),
            pltpu.VMEM((heads, KEYS, QB), single),
        ],
        compiler_params=params(48, 1),
        cost_estimate=cost(steps * heads * KEYS * QB * 2048, 8 * total * width, steps * heads * KEYS * QB),
        name="attend",
    )(order, need, low, qt, kv, vecs, *more)


def diagonal_sums(tile):
    wide = jnp.concatenate([tile, jnp.zeros_like(tile)], axis=1)
    row = lax.broadcasted_iota(jnp.int32, wide.shape, 0)
    bit = 1
    while bit < QB:
        wide = jnp.where((row & bit) != 0, pltpu.roll(wide, 2 * QB - bit, 1), wide)
        bit *= 2
    return jnp.sum(wide, axis=0, keepdims=True)


def backward_kernel(first, ends, order, need, low, qt, keys_in, vecs, lse, d0, d1, d2, d3, *rest):
    if ends:
        dkvt_in, ds_in, dqt, dkvt, sums, kv_all, kvt_all, bias, dout_all, ds_all = rest
        kvp = None
    else:
        kvp, dqt, dkvt, ds_all, kv_all, kvt_all, bias, dout_all = rest
    step = pl.program_id(0)
    heads = kv_all.shape[0]
    rows = d0.shape[1]

    @pl.when(step == 0)
    def _():
        stage_attention(kvp, keys_in, vecs, kv_all, kvt_all, bias)
        for place, ref in enumerate((d0, d1, d2, d3)):
            dout_all[:, pl.ds(pl.multiple_of(order[place] * rows, 128), rows)] = ref[...]
        if ends:
            ds_all[...] = ds_in[...]
            dkvt[:, :, :WINDOW] = dkvt_in[:, :, WINDOW : 2 * WINDOW]
            dkvt[:, :, WINDOW:] = jnp.zeros_like(dkvt[:, :, WINDOW:])
        else:
            ds_all[...] = jnp.zeros_like(ds_all)
            dkvt[...] = jnp.zeros_like(dkvt)

    start = pl.multiple_of(step * QB, QB)

    def run(masked):
        for head in range(heads):
            at = slice(head * HEAD_DIM, (head + 1) * HEAD_DIM)
            keys = kv_all[head, pl.ds(start, KEYS), :]
            query = qt[at, :]
            none = jnp.zeros_like(query)
            scores = dot(keys, jnp.concatenate([query, none], axis=0)) + bias[head]
            if masked:
                scores = keep_rows(scores, step + first, low[...])
            probs = jnp.exp(scores - lse[0, pl.ds(order[4] + head, 1), :])
            dout = dout_all[at, pl.ds(pl.multiple_of((step + first) * QB, QB), QB)]
            dprobs = dot(keys, jnp.concatenate([none, dout], axis=0))
            delta = jnp.sum(probs * dprobs, axis=0, keepdims=True)
            dscores = probs * (dprobs - delta)
            ds_all[head] += dscores
            dscores = dscores.astype(bfloat)
            probs = probs.astype(bfloat)
            window = pl.ds(start, KEYS)
            dqt[at, :] = (dot(kvt_all[head, :HEAD_DIM, window], dscores) * HEAD_DIM**-0.5).astype(bfloat)
            dkvt[head, :HEAD_DIM, window] += dot(query, dscores, NT)
            dkvt[head, HEAD_DIM:, window] += dot(dout, probs, NT)

    pl.when(need[step + first] > 0)(lambda: run(True))
    pl.when(need[step + first] <= 0)(lambda: run(False))

    if ends:

        @pl.when(step == pl.num_programs(0) - 1)
        def _():
            for head in range(heads):
                for chunk in range(CHUNKS):
                    sums[head, chunk : chunk + 1, :] = diagonal_sums(ds_all[head, chunk * QB : (chunk + 1) * QB, :])


def attention_backward(first, steps, span, order, need, low, qt, kvp, kv, vecs, lse, douts, begun=(), after=()):
    total, packed = kv.shape[1:]
    begin, heads = span
    pick = begin // heads
    width = heads * HEAD_DIM
    held = KEYS + (steps - 1) * QB
    ends = kvp is None
    own = held if ends else held - WINDOW
    scores = (heads, KEYS, QB)
    order = jnp.concatenate([order, jnp.full((1,), begin, jnp.int32)])
    kernel = functools.partial(backward_kernel, first, ends)
    specs = [
        SMEM,
        SMEM,
        pl.BlockSpec((1, QB), lambda i: (0, i + first)),
        pl.BlockSpec((width, QB), lambda i: (pick, i + first)),
        pl.BlockSpec((heads, own, packed), lambda i: (pick, 0, 0)),
        pl.BlockSpec((heads,) + vecs.shape[1:], lambda i: (pick, 0, 0)),
        pl.BlockSpec((1, 8, QB), lambda i: (i, 0, 0)),
    ] + [pl.BlockSpec((width, douts[0].shape[1]), lambda i: (pick, 0))] * 4
    inputs = [order, need, low, qt, kv, vecs, lse, *douts]
    out_specs = [pl.BlockSpec((width, QB), lambda i: (0, i)), VMEM]
    out_shape = [
        jax.ShapeDtypeStruct((width, steps * QB), bfloat),
        jax.ShapeDtypeStruct((heads, packed, held), single),
    ]
    scratch = [
        pltpu.VMEM((heads, held, packed), bfloat),
        pltpu.VMEM((heads, packed, held), bfloat),
        pltpu.VMEM(scores, single),
        pltpu.VMEM((width, total), bfloat),
    ]
    if ends:
        specs += [
            pl.BlockSpec((heads, packed, 2 * WINDOW), lambda i: (pick, 0, 0)),
            pl.BlockSpec(scores, lambda i: (pick, 0, 0)),
        ]
        inputs += list(begun)
        out_specs.append(VMEM)
        out_shape.append(jax.ShapeDtypeStruct((heads, 8, 2 * QB), single))
        scratch.append(pltpu.VMEM(scores, single))
    else:
        specs.append(VMEM)
        inputs.append(kvp)
        out_specs.append(VMEM)
        out_shape.append(jax.ShapeDtypeStruct(scores, single))
    if after:
        inner, count = kernel, len(inputs)
        kernel = lambda *refs: inner(*refs[:count], *refs[count + len(after) :])
        specs += [pl.BlockSpec(memory_space=pl.ANY)] * len(after)
        inputs += list(after)
    return pl.pallas_call(
        kernel,
        grid=(steps,),
        in_specs=specs,
        out_specs=out_specs,
        out_shape=out_shape,
        scratch_shapes=scratch,
        compiler_params=params(56, 1),
        cost_estimate=cost(steps * heads * KEYS * QB * 4096, 16 * total * width, steps * heads * KEYS * QB),
        name="attend_back",
    )(*inputs)


def settle_kernel(order, dq0, dq1, dkvt, behind, normed, out, grad):
    heads = dkvt.shape[0]
    rows = out.shape[2]
    total = dkvt.shape[2]
    edge = total - WINDOW
    sums = None
    parts = []
    for head in range(heads):
        at = slice(head * HEAD_DIM, (head + 1) * HEAD_DIM)
        dkv = jnp.concatenate([dkvt[head, :, :edge], dkvt[head, :, edge:] + behind[head].astype(single)], axis=1)
        parts.append(jnp.concatenate([dq0[at, :], dq1[at, :]], axis=1))
        parts.append(dkv.astype(bfloat))
    whole = jnp.concatenate(parts, axis=0)
    for lane in range(total // rows):
        piece = whole[:, lane * rows : (lane + 1) * rows]
        out[jnp.bitwise_xor(order[0], lane)] = piece
        term = dot(piece, normed[lane])
        sums = term if sums is None else sums + term
    grad[...] = sums.astype(bfloat)


def settle(span, order, dq0, dq1, dkvt, behind, normed):
    begin, heads = span
    pick = begin // heads
    lanes, rows, width = normed.shape
    tall = heads * 3 * HEAD_DIM
    total = lanes * rows
    whole = lambda shape: pl.BlockSpec(shape, lambda i: (0,) * len(shape))
    return pl.pallas_call(
        settle_kernel,
        grid=(1,),
        in_specs=[
            SMEM,
            pl.BlockSpec((heads * HEAD_DIM, dq0.shape[1]), lambda i: (pick, 0)),
            whole(dq1.shape),
            whole(dkvt.shape),
            pl.BlockSpec((heads,) + behind.shape[1:], lambda i: (pick, 0, 0)),
            whole(normed.shape),
        ],
        out_specs=[whole((lanes, tall, rows)), whole((tall, width))],
        out_shape=[
            jax.ShapeDtypeStruct((lanes, tall, rows), bfloat),
            jax.ShapeDtypeStruct((tall, width), bfloat),
        ],
        compiler_params=params(40, 1),
        cost_estimate=cost(2 * tall * total * width, 4 * total * width),
        name="settle",
    )(order, dq0, dq1, dkvt, behind, normed)


def middle_kernel(o0, o1, o2, o3, w0, w1, w2, w3, x, gain, code, y_out, send0, send1):
    y = x[...].astype(single)
    for ref, weight in ((o0, w0), (o1, w1), (o2, w2), (o3, w3)):
        y = y + dot(ref[...], weight[...], TN)
    y_out[...] = y
    inverse = lax.rsqrt(jnp.mean(y * y, axis=-1, keepdims=True) + epsilon)
    normed = (y * inverse * gain[...]).astype(bfloat)
    slots = send0.shape[0]
    for number, ref in enumerate((send0, send1)):
        slot = lax.broadcasted_iota(jnp.int32, (slots, y.shape[0]), 0) + number * slots
        pick = ((slot == code[0:1, :]) | (slot == code[1:2, :])).astype(bfloat)
        ref[...] = dot(pick, normed).astype(bfloat)


def middle(ots, w_out, x, gain, code, slots):
    rows, width = x.shape
    return pl.pallas_call(
        middle_kernel,
        in_specs=[VMEM] * 11,
        out_specs=[VMEM] * 3,
        out_shape=[
            jax.ShapeDtypeStruct((rows, width), single),
            jax.ShapeDtypeStruct((slots, width), bfloat),
            jax.ShapeDtypeStruct((slots, width), bfloat),
        ],
        compiler_params=params(40),
        cost_estimate=cost(2 * rows * width * (width + 2 * slots), 8 * rows * width),
        name="middle",
    )(*ots, *w_out, x, gain, code)


NOTES = 16


def send_kernel(value, code, out):
    slots, rows = out.shape[0], value.shape[0]
    slot = lax.broadcasted_iota(jnp.int32, (slots, rows), 0)
    pick = ((slot == code[0:1, :]) | (slot == code[1:2, :])).astype(bfloat)
    out[...] = dot(pick, value[...]).astype(bfloat)


def send_noted_kernel(value, code, partner, out):
    blocks, slot_rows = out.shape[0], out.shape[1] - NOTES
    rows, width = value.shape
    slots = blocks * slot_rows
    slot = lax.broadcasted_iota(jnp.int32, (slot_rows, rows), 0)
    for block in range(blocks):
        notes = []
        for number in range(2):
            here = slot + (number * slots + block * slot_rows)
            first = (here == code[0:1, :]).astype(bfloat)
            second = (here == code[1:2, :]).astype(bfloat)
            notes.append(dot(partner[0:8, :], first, NT) + dot(partner[8:16, :], second, NT))
        pick = first + second
        out[block, NOTES:, :] = dot(pick, value[...]).astype(bfloat)
        row = lax.broadcasted_iota(jnp.int32, (8, slot_rows), 0)
        note = jnp.where(row == 0, notes[0], notes[1])
        note = jnp.concatenate([note, jnp.zeros((8, width - slot_rows), single)], axis=1)
        out[block, :NOTES, :] = jnp.concatenate([note, note], axis=0).astype(bfloat)


def send_rows(value, code, slots):
    rows, width = value.shape
    return pl.pallas_call(
        send_kernel,
        in_specs=[VMEM] * 2,
        out_specs=VMEM,
        out_shape=jax.ShapeDtypeStruct((slots, width), bfloat),
        compiler_params=params(24),
        cost_estimate=cost(2 * rows * width * slots, 6 * rows * width),
        name="send_rows",
    )(value, code)


def send_noted(value, code, partner, blocks, slot_rows):
    rows, width = value.shape
    return pl.pallas_call(
        send_noted_kernel,
        in_specs=[VMEM] * 3,
        out_specs=VMEM,
        out_shape=jax.ShapeDtypeStruct((blocks, slot_rows + NOTES, width), bfloat),
        compiler_params=params(24),
        cost_estimate=cost(2 * rows * width * blocks * slot_rows, 6 * rows * width),
        name="send_noted",
    )(value, code, partner)


def collect(code, refs):
    total = None
    for number, ref in enumerate(refs):
        slots = ref.shape[0]
        slot = lax.broadcasted_iota(jnp.int32, (code.shape[0], slots), 1) + number * slots
        pick = ((slot == code[:, 0:1]) | (slot == code[:, 1:2])).astype(bfloat)
        part = dot(pick, ref[...])
        total = part if total is None else total + part
    return total


def return_kernel(order, d0, d1, code, y, gain, cotangent, w0, w1, w2, w3, o0, o1, o2, o3, dy_out, dot_out, gw_out, gg_out):
    dn = collect(code, (d0, d1))
    values = y[...]
    inverse = lax.rsqrt(jnp.mean(values * values, axis=-1, keepdims=True) + epsilon)
    hat = values * inverse
    gg_out[...] = jnp.sum(dn * hat, axis=0, keepdims=True)
    scaled = dn * gain[...]
    dy = cotangent[...].astype(single) + inverse * (scaled - hat * jnp.mean(scaled * hat, axis=-1, keepdims=True))
    dy_out[...] = dy
    low = dy.astype(bfloat)
    tall = o0.shape[0]
    for place, (ref, weight) in enumerate(((o0, w0), (o1, w1), (o2, w2), (o3, w3))):
        at = pl.ds(pl.multiple_of(order[place] * tall, 64), tall)
        mask = (0, 2, 1, 3)[place]
        dot_out[mask] = dot(weight[...], low, NT).astype(bfloat)
        gw_out[at, :] = dot(ref[...], low).astype(bfloat)


def return_rows(order, d0, d1, code, y, gain, cotangent, w_out, ots):
    rows, width = y.shape
    slots = d0.shape[0]
    lanes = len(ots)
    return pl.pallas_call(
        return_kernel,
        in_specs=[SMEM] + [VMEM] * 14,
        out_specs=[VMEM] * 4,
        out_shape=[
            jax.ShapeDtypeStruct((rows, width), single),
            jax.ShapeDtypeStruct((lanes, width // lanes, rows), bfloat),
            jax.ShapeDtypeStruct((width, width), bfloat),
            jax.ShapeDtypeStruct((1, width), single),
        ],
        compiler_params=params(48),
        cost_estimate=cost(2 * rows * width * (2 * width + 2 * slots), 16 * rows * width),
        name="return_rows",
    )(order, d0, d1, code, y, gain, cotangent, *w_out, *ots)


def finish_kernel(z0, z1, code, y, out):
    out[...] = (y[...] + collect(code, (z0, z1))).astype(bfloat)


def finish(z0, z1, code, y):
    rows, width = y.shape
    return pl.pallas_call(
        finish_kernel,
        in_specs=[VMEM] * 4,
        out_specs=VMEM,
        out_shape=jax.ShapeDtypeStruct((rows, width), bfloat),
        compiler_params=params(32),
        cost_estimate=cost(4 * rows * width * z0.shape[0], 12 * rows * width),
        name="finish",
    )(z0, z1, code, y)


def tail_kernel(order, *refs):
    *pieces, wt, x, gain, dy, out = refs
    dn = None
    for number, ref in enumerate(pieces):
        block = order[number % 4]
        tall = ref.shape[0]
        begin = block * (3 * x.shape[1] // 4)
        if number >= 4:
            begin = begin + pieces[0].shape[0]
        term = dot(ref[...], wt[pl.ds(pl.multiple_of(begin, 64), tall), :], TN)
        dn = term if dn is None else dn + term
    values = x[...].astype(single)
    inverse = lax.rsqrt(jnp.mean(values * values, axis=-1, keepdims=True) + epsilon)
    hat = values * inverse
    scaled = dn * gain[...]
    out[...] = dy[...] + inverse * (scaled - hat * jnp.mean(scaled * hat, axis=-1, keepdims=True))


def tail(order, pieces, wt, x, gain, dy):
    rows, width = x.shape
    return pl.pallas_call(
        tail_kernel,
        in_specs=[SMEM] + [VMEM] * (4 + len(pieces)),
        out_specs=VMEM,
        out_shape=jax.ShapeDtypeStruct((rows, width), single),
        compiler_params=params(40),
        cost_estimate=cost(2 * rows * width * wt.shape[0], 14 * rows * width),
        name="tail",
    )(order, *pieces, wt, x, gain, dy)


GELU_0 = 0.7978845608028654
GELU_1 = 0.7978845608028654 * 0.044715
FF_BLOCK = 512
ROW_BLOCK = 256


def expert_kernel(
    mine, xs, router, other, w1, w2, da, cot, g1, g2, dx_out, z_out, m_out, total, result, dgate, gate, act_all, du_all, xst, dzt
):
    step = pl.program_id(0)
    rows = xs.shape[0]
    experts = router.shape[0]

    def picks():
        lane = lax.broadcasted_iota(jnp.int32, (rows, experts), 1)
        return lane == mine[0], lane == other[...] - 1

    @pl.when(step == 0)
    def _():
        logits = dot(xs[...], router[...], NT)
        own, rest = picks()
        margin = jnp.sum(jnp.where(own, logits, 0.0) - jnp.where(rest, logits, 0.0), axis=1, keepdims=True)
        value = 1.0 / (1.0 + jnp.exp(-margin))
        value = jnp.where(other[...] > 0, value, 0.0)
        gate[...] = jnp.broadcast_to(value, gate.shape)
        dgate[...] = jnp.zeros_like(dgate)
        total[...] = jnp.zeros_like(total)
        result[...] = jnp.zeros_like(result)
        for begin in range(0, rows, ROW_BLOCK):
            at = slice(begin, begin + ROW_BLOCK)
            xst[:, at] = xs[at, :].T
            dzt[:, at] = (cot[at, :].astype(single) * gate[at, 0:1]).astype(bfloat).T

    for begin in range(0, rows, ROW_BLOCK):
        at = slice(begin, begin + ROW_BLOCK)
        u = dot(xs[at, :], w1[...])
        square = u * u
        tan = jnp.tanh(u * (GELU_0 + GELU_1 * square))
        half = 0.5 + 0.5 * tan
        act = u * half
        slope = half + act * (1.0 - half) * (2.0 * GELU_0 + 6.0 * GELU_1 * square)
        back = da[at, :].astype(single)
        product = act * back
        part = product[:, :128]
        for col in range(128, product.shape[1], 128):
            part = part + product[:, col : col + 128]
        dgate[at, :] += part
        act_all[at, :] = act.astype(bfloat)
        du_all[at, :] = (gate[at, 0:1] * back * slope).astype(bfloat)
    total[...] += dot(du_all[...], w1[...], NT)
    result[...] += dot(act_all[...], w2[...])
    g1[...] = dot(xst[...], du_all[...]).astype(bfloat)
    g2[...] = dot(dzt[...], act_all[...]).astype(bfloat).T

    @pl.when(step == pl.num_programs(0) - 1)
    def _():
        own, rest = picks()
        value = gate[:, 0:1]
        weight = value * (1.0 - value) * jnp.sum(dgate[...], axis=1, keepdims=True)
        m = (weight * (own.astype(single) - rest.astype(single))).astype(bfloat)
        m_out[...] = m
        dx_out[...] = (total[...] + dot(m, router[...])).astype(bfloat)
        z_out[...] = (result[...] * value).astype(bfloat)


def expert(mine, xs, router, other, w1, w2, da, cot, local):
    rows, width = xs.shape
    inner = w1.shape[2]
    experts = router.shape[0]
    block = FF_BLOCK
    whole = lambda shape: pl.BlockSpec(shape, lambda f: (0,) * len(shape))
    return pl.pallas_call(
        expert_kernel,
        grid=(inner // block,),
        in_specs=[
            SMEM,
            whole((rows, width)),
            whole((experts, width)),
            whole((rows, 1)),
            pl.BlockSpec((None, width, block), lambda f: (local, 0, f)),
            pl.BlockSpec((None, block, width), lambda f: (local, f, 0)),
            pl.BlockSpec((rows, block), lambda f: (0, f)),
            whole((rows, width)),
        ],
        out_specs=[
            pl.BlockSpec((width, block), lambda f: (0, f)),
            pl.BlockSpec((block, width), lambda f: (f, 0)),
            whole((rows, width)),
            whole((rows, width)),
            whole((rows, experts)),
        ],
        out_shape=[
            jax.ShapeDtypeStruct((width, inner), bfloat),
            jax.ShapeDtypeStruct((inner, width), bfloat),
            jax.ShapeDtypeStruct((rows, width), bfloat),
            jax.ShapeDtypeStruct((rows, width), bfloat),
            jax.ShapeDtypeStruct((rows, experts), bfloat),
        ],
        scratch_shapes=[
            pltpu.VMEM((rows, width), single),
            pltpu.VMEM((rows, width), single),
            pltpu.VMEM((rows, 128), single),
            pltpu.VMEM((rows, 128), single),
            pltpu.VMEM((rows, block), bfloat),
            pltpu.VMEM((rows, block), bfloat),
            pltpu.VMEM((width, rows), bfloat),
            pltpu.VMEM((width, rows), bfloat),
        ],
        compiler_params=params(60, 1),
        cost_estimate=cost(20 * rows * width * inner, 8 * rows * inner + 8 * width * inner, rows * inner),
        name="expert",
    )(mine, xs, router, other, w1, w2, da, cot)


def tie(*values):
    return lax.optimization_barrier(values)


def swap(value, axis, mask):
    return lax.ppermute(value, axis, [(i, i ^ mask) for i in range(lax.axis_size(axis))])


def per_device(
    hidden_in,
    norm1_gain,
    w_query,
    w_key,
    w_value,
    w_out,
    rel_bias,
    norm2_gain,
    w_router,
    w_first,
    w_second,
    routes,
    priority,
    segments,
    grad_out,
):
    lanes = lax.axis_size("head")
    blocks = lax.axis_size("seq")
    lane = lax.axis_index("head")
    place = lax.axis_index("seq")
    rows, width = hidden_in.shape[2:]
    x = hidden_in.reshape(rows, width)
    total = rows * lanes
    part = width // lanes
    heads = part // HEAD_DIM
    cotangent = grad_out.reshape(rows, width)
    experts = w_router.shape[1]
    local = w_first.shape[0]
    slot_rows = max(2, 4 * rows // experts)
    slots = blocks * slot_rows
    capacity = 5 * rows * lanes // (2 * local)

    far = swap(x, "head", 2)
    near = swap(x, "head", 1)
    order = jnp.stack([lane, lane ^ 2, lane ^ 1, lane ^ 3]).astype(jnp.int32)
    at = lambda value, mask: lax.dynamic_index_in_dim(value, lane ^ mask, 0, keepdims=False)

    def trade(value):
        return [value[0], swap(value[2], "head", 2), swap(value[1], "head", 1), swap(value[3], "head", 3)]

    gains = jnp.concatenate([norm1_gain[None, :], norm2_gain[None, :], jnp.zeros((GAINS - 2, part), bfloat)], axis=0)
    own_pack, far_pack, near_pack, both_pack = pack(order, w_query, w_key, w_value, w_router.T, gains)
    packed = [own_pack, swap(far_pack, "head", 2), swap(near_pack, "head", 1), swap(both_pack, "head", 3)]

    route_rows = routes.reshape(rows, -1)
    top_count = route_rows.shape[1]
    pair_routes = route_rows.reshape(-1)
    pair_prio = priority.reshape(-1)
    expert_ids = jnp.arange(experts, dtype=jnp.int32)
    pair_hot = (pair_routes[:, None] == expert_ids[None, :]).astype(jnp.int32)
    earlier = (pair_routes[:, None] == pair_routes[None, :]) & (pair_prio[None, :] < pair_prio[:, None])
    local_rank = jnp.sum(earlier.astype(jnp.int32), axis=1)
    code = (pair_routes % local) * slots + (pair_routes // local) * slot_rows + local_rank
    code = code.reshape(rows, top_count)
    code_t = code.T

    def exchange(value):
        return lax.all_to_all(
            value.reshape(blocks, slot_rows, -1), "seq", split_axis=0, concat_axis=0, tiled=True
        ).reshape(slots, -1)

    cot_send = send_rows(cotangent, code_t, slots)

    block_rank = (jnp.min(pair_prio) // (top_count * rows)).reshape(1)
    spare = 128 - (experts + 1) % 128
    tallies = jnp.concatenate([jnp.sum(pair_hot, axis=0), block_rank, jnp.zeros((spare,), jnp.int32)])[None, :]
    for axis, size in (("head", lanes), ("seq", blocks)):
        mask = 1
        while mask < size:
            tallies = jnp.concatenate([tallies, swap(tallies, axis, mask)], axis=0)
            mask *= 2
    ahead = (tallies[:, experts : experts + 1] < block_rank[None, :]).astype(jnp.int32)
    offsets = jnp.sum(tallies[:, :experts] * ahead, axis=0)
    kept = (jnp.sum(pair_hot * offsets[None, :], axis=1) + local_rank < capacity).reshape(rows, top_count)
    partner = jnp.where(kept, route_rows[:, ::-1] + 1, 0).astype(bfloat)
    partner = jnp.repeat(partner.T, 8, axis=0)

    near, far, cot_send, w_second, w_first, w_out, *packed = tie(near, far, cot_send, w_second, w_first, w_out, *packed)
    both = swap(far, "head", 1)
    cot_first = exchange(cot_send)

    out_far = swap(w_out, "head", 2)
    out_near = swap(w_out, "head", 1)
    second_full = lax.all_gather(w_second, "head", axis=1, tiled=True)
    first_full = lax.all_gather(w_first, "head", axis=1, tiled=True)

    both, partner = tie(both, partner)
    normed, qt, kv, w_rows, router_t, gains = project(order, (x, far, near, both), packed, heads, experts)
    w_rows_full = lax.all_gather(w_rows, "head", axis=0, tiled=True)
    gain_one, gain_two = gains[0:1], gains[1:2]
    kvp = lax.ppermute(kv[:, total - WINDOW :, :], "seq", [(i, i + 1) for i in range(blocks - 1)])
    hot, allowed = lane_tables()
    table = rel_bias.reshape(heads, BUCKETS)
    vecs = dot(table, jnp.asarray(hot.T, bfloat)).reshape(heads, CHUNKS, 2 * QB)
    vecs = jnp.where(jnp.asarray(allowed)[None], vecs, MASKED)
    vecs = jnp.concatenate([vecs, jnp.zeros((heads, 8 - CHUNKS, 2 * QB), single)], axis=1)
    base = place * total
    own = lax.dynamic_slice_in_dim(segments, base, total, 0)
    low = jnp.zeros_like(own)
    for number in range(1, 4):
        low = jnp.where(own == number, jnp.sum((segments < number).astype(jnp.int32)), low)
    low = low - base + WINDOW
    need = (jnp.max(low.reshape(-1, QB), axis=1) > jnp.arange(total // QB) * QB).astype(jnp.int32)
    low = low.reshape(1, total)
    early = WINDOW // QB
    later = total // QB - early
    kv, cot_first = tie(kv, cot_first)
    ot, lse_later = attention_forward(early, later, order, need, low, qt, None, kv, vecs, lanes)
    ot, late_cotangent, kvp, out_far, out_near = tie(ot, cotangent, kvp, out_far, out_near)
    w_outs = (w_out, out_far, out_near, swap(out_far, "head", 1))
    ot, lse_early = attention_forward(0, early, order, need, low, qt, kvp, kv, vecs, lanes, ot)
    noted = lax.all_to_all(
        send_noted(late_cotangent, code_t, partner, blocks, slot_rows), "seq", split_axis=0, concat_axis=0, tiled=True
    )
    ots = trade(ot)

    y, *sends = middle(ots, w_outs, x, gain_two, code_t, slots)
    sends[0], noted = tie(sends[0], noted)
    other = noted[:, :local, :slot_rows].astype(jnp.int32).transpose(1, 0, 2).reshape(local, slots, 1)
    cot_slots = [cot_first, noted[:, NOTES:, :].reshape(slots, width)]
    mine = (place * local).astype(jnp.int32).reshape(1)
    backs = [dot(cot_slots[i], second_full[i], NT).astype(bfloat) for i in range(local)]
    received = [exchange(sends[0])]
    sends[1], *backs = tie(sends[1], *backs)
    received.append(exchange(sends[1]))

    def run_expert(number):
        return expert(
            mine + number,
            received[number],
            router_t,
            other[number],
            first_full,
            second_full,
            backs[number],
            cot_slots[number],
            number,
        )

    *grads0, dx0, z0, m0 = run_expert(0)
    dx0, received[1] = tie(dx0, received[1])
    returns = [exchange(dx0)]
    *grads1, dx1, z1, m1 = run_expert(1)
    def near_terms(value):
        value = value.reshape(lanes, part, -1)
        cross = swap(at(value, 3), "head", 1)
        direct = swap(at(value, 1), "head", 1)
        return (
            (at(value, 2).astype(single) + cross.astype(single)).astype(bfloat),
            at(value, 0).astype(single) + direct.astype(single),
        )

    def scatter(value):
        return lax.psum_scatter(value, "head", scatter_dimension=0, tiled=True)

    away0, home0 = near_terms(grads0[0])
    second0 = scatter(grads0[1])
    across0 = swap(away0, "head", 2)
    away1, home1 = near_terms(grads1[0])
    second1 = scatter(grads1[1])

    returns[0], dx1 = tie(returns[0], dx1)
    returns.append(exchange(dx1))
    grad_router = dot(received[0], m0, TN) + dot(received[1], m1, TN)

    w_rows_full, returns[1], away1, home1, across0, home0 = tie(w_rows_full, returns[1], away1, home1, across0, home0)
    dy, douts, grad_outw, grad_gain_two = return_rows(
        order, returns[0], returns[1], code, y, gain_two, cotangent, w_outs, ots
    )
    across1 = swap(away1, "head", 2)
    dy, z0, z1 = tie(dy, z0, z1)
    z_back = [exchange(z0), exchange(z1)]
    douts = trade(douts)
    first0 = home0 + across0.astype(single)
    first1 = home1 + across1.astype(single)
    douts[3], first0, first1 = tie(douts[3], first0, first1)
    mixed = jnp.concatenate(
        [grad_outw, grad_router.astype(bfloat), grad_gain_two.astype(bfloat).T, jnp.zeros((width, 111 - experts % 128), bfloat)],
        axis=1,
    )

    def sum_blocks(value):
        count, last = value.shape[1:]
        value = value.reshape(lanes * blocks, count // blocks, last)
        value = lax.all_to_all(value, ("head", "seq"), split_axis=0, concat_axis=0, tiled=True)
        return jnp.sum(value.reshape(lanes, blocks, -1, last).astype(single), axis=1).astype(bfloat)

    dq_early, dkvt_early, ds_early = attention_backward(
        0, early, (0, heads), order, need, low, qt, kvp, kv, vecs, lse_early, douts
    )
    behind = lax.ppermute(
        dkvt_early[:, :, :WINDOW].astype(bfloat), "seq", [(i + 1, i) for i in range(blocks - 1)]
    )
    mixed = lax.psum_scatter(mixed, "head", scatter_dimension=0, tiled=True)
    dkvt_early, mixed, z_back[0], second0 = tie(dkvt_early, mixed, z_back[0], second0)
    mixed = lax.psum(mixed, "seq")
    cut = heads - 1

    def later_part(span):
        return attention_backward(
            early, later, span, order, need, low, qt, None, kv, vecs, lse_later, douts, (dkvt_early, ds_early)
        )

    pieces = []
    span = (0, cut)
    dq, dkvt, sums0 = later_part(span)
    dkvt, z_back[1] = tie(dkvt, z_back[1])
    parts, grad_part = settle(span, order, dq_early, dq, dkvt, behind, normed)
    ds_early, second1, parts, grad_part = tie(ds_early, second1, parts, grad_part)
    pieces += trade(parts)
    summed = [sum_blocks(grad_part.reshape(-1, lanes, part).transpose(1, 0, 2))]
    span = (cut, heads - cut)
    dq, dkvt, sums1 = later_part(span)
    dkvt, summed[0] = tie(dkvt, summed[0])
    parts, grad_part = settle(span, order, dq_early, dq, dkvt, behind, normed)
    pieces += trade(parts)
    grad_hidden = tail(order, pieces, w_rows_full, x, gain_one, dy).reshape(hidden_in.shape)
    output = finish(z_back[0], z_back[1], code, y).reshape(hidden_in.shape)

    grad_rel = jnp.dot(
        jnp.concatenate([sums0, sums1], axis=0)[:, :CHUNKS].reshape(heads, -1),
        jnp.asarray(hot, single),
        precision=lax.Precision.HIGHEST,
    ).reshape(-1)
    rel_row = jnp.concatenate([grad_rel.astype(bfloat), jnp.zeros((part - grad_rel.shape[0],), bfloat)])
    rel_rows = jnp.zeros((lanes, blocks, part), bfloat)
    rel_rows = lax.dynamic_update_slice(rel_rows, rel_row[None, None, :], (lane, 0, 0))
    value = jnp.concatenate([grad_part.reshape(-1, lanes, part).transpose(1, 0, 2), rel_rows], axis=1)
    summed.append(sum_blocks(value))
    split = summed[0].shape[1]
    value = jnp.concatenate(summed, axis=1)
    value, grad_hidden, mixed = tie(value, grad_hidden, mixed)
    value = lax.all_to_all(
        jnp.broadcast_to(value[None], (blocks,) + value.shape), "seq", split_axis=0, concat_axis=0, tiled=True
    )
    value = value.transpose(1, 0, 2, 3)
    summed = [
        value[:, :, :split].reshape(lanes, blocks * split, part),
        value[:, :, split:].reshape(lanes, -1, part),
    ]
    grad_rel = jnp.sum(summed[1][:, -blocks, : heads * BUCKETS].astype(single), axis=0)
    summed[1] = summed[1][:, :-blocks, :]
    rows_all = jnp.concatenate(summed, axis=1).reshape(lanes, heads, 3, HEAD_DIM, part)
    grads = rows_all.transpose(2, 4, 0, 1, 3).reshape(3, part, width).astype(single)
    grad_norm1 = sum(
        jnp.sum(grads[i] * weight.astype(single), axis=1) for i, weight in enumerate((w_query, w_key, w_value))
    ) / norm1_gain.astype(single)
    return (
        output,
        grad_hidden,
        grad_norm1,
        grads[0],
        grads[1],
        grads[2],
        mixed[:, :width].astype(single),
        grad_rel,
        mixed[:, width + experts].astype(single),
        mixed[:, width : width + experts].astype(single),
        jnp.stack([first0, first1]),
        jnp.stack([second0, second1]).astype(single),
    )


def solution(mesh):
    return jax.shard_map(
        per_device,
        mesh=mesh,
        in_specs=(
            P("seq", "head", None, None),
            P("head"),
            P("head", None),
            P("head", None),
            P("head", None),
            P("head", None),
            P("head"),
            P("head"),
            P("head", None),
            P("seq", "head", None),
            P("seq", "head", None),
            P("seq", "head", None, None),
            P("seq", "head", None, None),
            P(),
            P("seq", "head", None, None),
        ),
        out_specs=(
            P("seq", "head", None, None),
            P("seq", "head", None, None),
            P("head"),
            P("head", None),
            P("head", None),
            P("head", None),
            P("head", None),
            P("head"),
            P("head"),
            P("head", None),
            P("seq", "head", None),
            P("seq", "head", None),
        ),
        check_vma=False,
    )
```

```python
import functools

import jax
import jax.numpy as jnp
import numpy as np
from jax import lax
from jax.experimental import pallas as pl
from jax.experimental.pallas import tpu as pltpu
from jax.sharding import PartitionSpec as P

HEAD_DIM = 64
WINDOW = 1024
BUCKETS = 32
QB = 256
CHUNKS = WINDOW // QB + 1
KEYS = CHUNKS * QB
MASKED = -1e30
epsilon = 1e-06
bfloat = jnp.bfloat16
single = jnp.float32
MIB = 1 << 20

VMEM = pl.BlockSpec(memory_space=pltpu.VMEM)
SMEM = pl.BlockSpec(memory_space=pltpu.SMEM)


def dot(a, b, dims=((1,), (0,))):
    return lax.dot_general(a, b, (dims, ((), ())), preferred_element_type=single)


NN = ((1,), (0,))
NT = ((1,), (1,))
TN = ((0,), (0,))


def params(mib, grid=0):
    extra = {"dimension_semantics": ("arbitrary",) * grid} if grid else {}
    return pltpu.CompilerParams(vmem_limit_bytes=mib * MIB, **extra)


def full(shape):
    return pl.BlockSpec(tuple(shape), lambda i: (0,) * len(shape))


def once(kernel, name, inputs, outputs, scratch=()):
    found = pl.pallas_call(
        kernel,
        grid=(1,),
        in_specs=[SMEM if value.ndim == 1 else full(value.shape) for value in inputs],
        out_specs=[full(shape) for shape, _ in outputs],
        out_shape=[jax.ShapeDtypeStruct(shape, kind) for shape, kind in outputs],
        scratch_shapes=list(scratch),
        compiler_params=params(60, 1),
        cost_estimate=light(),
        name=name,
    )(*inputs)
    return found


def cost(flops, moved, trans=0):
    return pl.CostEstimate(flops=int(flops), bytes_accessed=int(moved), transcendentals=int(trans))


def light():
    return cost(1000, 1000)


MASKS = (0, 2, 1, 3)


def by_lane(own, action):
    for lane in range(len(MASKS)):

        @pl.when(own == lane)
        def _():
            for place, mask in enumerate(MASKS):
                action(place, lane ^ mask)


def bucket_edges(window_len, bucket_count):
    middle = bucket_count // 2
    edge_list = []
    for number in range(1, bucket_count):
        if number < middle:
            edge_list.append(number)
        else:
            edge_list.append(int(middle * (window_len / middle) ** ((number - middle) / middle)))
    return edge_list


def lane_tables():
    lane = np.arange(2 * QB)
    offset = np.where(lane < QB, lane, lane - 2 * QB)
    distance = WINDOW - QB * np.arange(CHUNKS)[:, None] + offset[None, :]
    allowed = (distance >= 0) & (distance < WINDOW)
    bucket = np.zeros(distance.shape, np.int32)
    for edge_value in bucket_edges(WINDOW, BUCKETS):
        bucket = bucket + (distance >= edge_value)
    hot = (bucket.reshape(-1)[:, None] == np.arange(BUCKETS)[None, :]) & allowed.reshape(-1)[:, None]
    return hot, allowed


GAINS = 16


def pack_kernel(order, wq, wk, wv, router_t, gains, *outs):
    part = wq.shape[0]
    experts = router_t.shape[0]

    def put(place, lane):
        for number, weight in enumerate((wq, wk, wv)):
            outs[place][:, number * part : (number + 1) * part] = weight[:, lane * part : (lane + 1) * part]

    by_lane(order[0], put)
    rest = outs[0].shape[1] - 3 * part
    for ref in outs:
        ref[:experts, 3 * part :] = router_t[...]
        ref[experts : experts + GAINS, 3 * part :] = gains[...]
        ref[experts + GAINS :, 3 * part :] = jnp.zeros((part - experts - GAINS, rest), bfloat)


def pack(order, wq, wk, wv, router_t, gains):
    part, width = wq.shape
    return once(pack_kernel, "pack", (order, wq, wk, wv, router_t, gains), [((part, width), bfloat)] * len(MASKS))


def project_kernel(
    order, x0, x1, x2, x3, p0, p1, p2, p3, n_out, qt_out, kv_out, kv_last, rows_out, router_out, gain_out, wq, wk, wv
):
    rows, width = x0.shape
    heads = kv_out.shape[0]
    part = heads * HEAD_DIM
    experts = router_out.shape[0]
    packed = (p0, p1, p2, p3)
    for place, ref in enumerate(packed):
        at = pl.ds(pl.multiple_of(order[place] * part, 64), part)
        for number, weight in enumerate((wq, wk, wv)):
            weight[at, :] = ref[:, number * part : (number + 1) * part]

    def spread(skip, count):
        found = []
        for lane in range(len(packed)):
            piece = None
            for place, ref in enumerate(packed):
                value = ref[skip : skip + count, 3 * part :]
                piece = value if piece is None else jnp.where(order[place] == lane, value, piece)
            found.append(piece)
        return jnp.concatenate(found, axis=1)

    router_out[...] = spread(0, experts)
    gains = spread(experts, GAINS).astype(single)
    gain_out[...] = gains[0:8, :]
    wq_t = wq[...].T
    k_t = wk[...].T
    v_t = wv[...].T
    for head in range(heads):
        at = slice(head * HEAD_DIM, (head + 1) * HEAD_DIM)
        for number, value in enumerate((wq_t, k_t, v_t)):
            begin = (3 * head + number) * HEAD_DIM
            rows_out[begin : begin + HEAD_DIM, :] = value[at, :]
    for place, ref in enumerate((x0, x1, x2, x3)):
        block = order[place]
        values = ref[...].astype(single)
        inverse = lax.rsqrt(jnp.mean(values * values, axis=-1, keepdims=True) + epsilon)
        normed = (values * inverse * gain_out[0:1, :]).astype(bfloat)
        n_out[block] = normed
        at = pl.ds(pl.multiple_of(block * rows, 128), rows)
        qt = dot(wq_t, normed, NT).astype(bfloat)
        qt_out[:, at] = qt * bfloat(HEAD_DIM**-0.5)
        for head in range(heads):
            begin = 3 * head * HEAD_DIM + HEAD_DIM
            kv = dot(normed, rows_out[begin : begin + 2 * HEAD_DIM, :], NT)
            kv_out[head, at, :] = kv.astype(bfloat)
    kv_last[...] = kv_out[:, kv_out.shape[1] - WINDOW :, :]


def project(order, pieces, packed, heads, experts):
    rows, width = pieces[0].shape
    lanes = len(MASKS)
    total = rows * lanes
    part = heads * HEAD_DIM
    return once(
        project_kernel,
        "project",
        (order, *pieces, *packed),
        [
            ((lanes, rows, width), bfloat),
            ((part, total), bfloat),
            ((heads, total, 2 * HEAD_DIM), bfloat),
            ((heads, WINDOW, 2 * HEAD_DIM), bfloat),
            ((3 * part, width), bfloat),
            ((experts, width), bfloat),
            ((8, width), single),
        ],
        [pltpu.VMEM((width, part), bfloat)] * 3,
    )


def eye(size):
    return (
        lax.broadcasted_iota(jnp.int32, (size, size), 0) == lax.broadcasted_iota(jnp.int32, (size, size), 1)
    ).astype(bfloat)


def stage_attention(kvp, kv, vecs, kv_all, kvt_all, bias):
    heads = kv_all.shape[0]
    unit = eye(2 * HEAD_DIM)
    for head in range(heads):
        if kvp is None:
            kv_all[head] = kv[head]
        else:
            kv_all[head, :WINDOW, :] = kvp[head]
            kv_all[head, WINDOW:, :] = kv[head]
        kvt_all[head] = dot(unit, kv_all[head], NT).astype(bfloat)
        for chunk in range(CHUNKS):
            row = jnp.broadcast_to(vecs[head, chunk : chunk + 1, :], (QB, 2 * QB))
            tile = pltpu.roll(row, 0, 1, stride=1, stride_axis=0)
            bias[head, chunk * QB : (chunk + 1) * QB, :] = tile[:, :QB]


def keep_rows(scores, step, low):
    key = lax.broadcasted_iota(jnp.int32, scores.shape, 0) + step * QB
    return jnp.where(key >= low, scores, MASKED)


def query_tile(step, first, pieces):
    found = []
    for half in range(QB // 128):
        piece = (step + first) * (QB // 128) + half
        found.append((piece // pieces, pl.ds(pl.multiple_of((piece % pieces) * 128, 128), 128)))
    return found


def forward_kernel(first, order, need, low, qt, keys_in, vecs, *rest):
    *more, out0, out1, out2, out3, lse, kv_all, kvt_all, bias = rest
    outs = (out0, out1, out2, out3)
    step = pl.program_id(0)
    heads = kv_all.shape[0]
    pieces = out0.shape[1] // 128

    @pl.when(step == 0)
    def _():
        if more:
            stage_attention(more[0], keys_in, vecs, kv_all, kvt_all, bias)
            for ref, begun in zip(outs, more[1:]):
                ref[...] = begun[...]
        else:
            stage_attention(None, keys_in, vecs, kv_all, kvt_all, bias)

    start = pl.multiple_of(step * QB, QB)

    def run(masked):
        found = []
        for head in range(heads):
            keys = kv_all[head, pl.ds(start, KEYS), :]
            query = qt[head * HEAD_DIM : (head + 1) * HEAD_DIM, :]
            query = jnp.concatenate([query, jnp.zeros_like(query)], axis=0)
            scores = dot(keys, query) + bias[head]
            if masked:
                scores = keep_rows(scores, step + first, low[...])
            peak = jnp.max(scores, axis=0, keepdims=True)
            expo = jnp.exp(scores - peak)
            total = jnp.sum(expo, axis=0, keepdims=True)
            values = kvt_all[head, HEAD_DIM:, pl.ds(start, KEYS)]
            mixed = dot(values, expo.astype(bfloat)) * (1.0 / total)
            found.append(mixed.astype(bfloat))
            lse[0, head : head + 1, :] = peak + jnp.log(total)
        whole = jnp.concatenate(found, axis=0)
        for half, (owner, spot) in enumerate(query_tile(step, first, pieces)):
            for mask, ref in zip(MASKS, outs):

                @pl.when(jnp.bitwise_xor(owner, order[0]) == mask)
                def _():
                    ref[:, spot] = whole[:, half * 128 : (half + 1) * 128]

    pl.when(need[step + first] > 0)(lambda: run(True))
    pl.when(need[step + first] <= 0)(lambda: run(False))


def attention_forward(first, steps, order, need, low, qt, kvp, kv, vecs, lanes, begun=None):
    heads, total, packed = kv.shape
    width = heads * HEAD_DIM
    held = KEYS + (steps - 1) * QB
    own = held - (0 if kvp is None else WINDOW)
    more = [] if kvp is None else [kvp, *begun]
    return pl.pallas_call(
        functools.partial(forward_kernel, first),
        grid=(steps,),
        in_specs=[
            SMEM,
            SMEM,
            pl.BlockSpec((1, QB), lambda i: (0, i + first)),
            pl.BlockSpec((width, QB), lambda i: (0, i + first)),
            pl.BlockSpec((heads, own, packed), lambda i: (0, 0, 0)),
            full(vecs.shape),
        ]
        + [full(value.shape) for value in more],
        out_specs=[full((width, total // lanes))] * lanes + [pl.BlockSpec((1, 8, QB), lambda i: (i, 0, 0))],
        out_shape=[jax.ShapeDtypeStruct((width, total // lanes), bfloat)] * lanes
        + [jax.ShapeDtypeStruct((steps, 8, QB), single)],
        scratch_shapes=[
            pltpu.VMEM((heads, held, packed), bfloat),
            pltpu.VMEM((heads, packed, held), bfloat),
            pltpu.VMEM((heads, KEYS, QB), single),
        ],
        compiler_params=params(60, 1),
        cost_estimate=light(),
        name="attend",
    )(order, need, low, qt, kv, vecs, *more)


def diagonal_sums(tile):
    wide = jnp.concatenate([tile, jnp.zeros_like(tile)], axis=1)
    row = lax.broadcasted_iota(jnp.int32, wide.shape, 0)
    bit = 1
    while bit < QB:
        wide = jnp.where((row & bit) != 0, pltpu.roll(wide, 2 * QB - bit, 1), wide)
        bit *= 2
    return jnp.sum(wide, axis=0, keepdims=True)


def backward_kernel(first, ends, order, need, low, qt, keys_in, vecs, lse, d0, d1, d2, d3, *rest):
    if ends:
        dkvt_in, ds_in, dqt, dkvt, sums, kv_all, kvt_all, bias, dout_all, ds_all = rest
        kvp = None
    else:
        kvp, dqt, behind, dkv_own, ds_all, kv_all, kvt_all, bias, dout_all, dkvt = rest
    step = pl.program_id(0)
    heads = kv_all.shape[0]
    rows = d0.shape[1]

    @pl.when(step == 0)
    def _():
        stage_attention(kvp, keys_in, vecs, kv_all, kvt_all, bias)
        for place, ref in enumerate((d0, d1, d2, d3)):
            dout_all[:, pl.ds(pl.multiple_of(order[place] * rows, 128), rows)] = ref[...]
        if ends:
            ds_all[...] = ds_in[...]
            dkvt[:, :, :WINDOW] = dkvt_in[...]
            dkvt[:, :, WINDOW:] = jnp.zeros_like(dkvt[:, :, WINDOW:])
        else:
            ds_all[...] = jnp.zeros_like(ds_all)
            dkvt[...] = jnp.zeros_like(dkvt)

    start = pl.multiple_of(step * QB, QB)

    def run(masked):
        for head in range(heads):
            at = slice(head * HEAD_DIM, (head + 1) * HEAD_DIM)
            keys = kv_all[head, pl.ds(start, KEYS), :]
            query = qt[at, :]
            none = jnp.zeros_like(query)
            scores = dot(keys, jnp.concatenate([query, none], axis=0)) + bias[head]
            if masked:
                scores = keep_rows(scores, step + first, low[...])
            probs = jnp.exp(scores - lse[0, pl.ds(order[4] + head, 1), :])
            dout = dout_all[at, pl.ds(pl.multiple_of((step + first) * QB, QB), QB)]
            dprobs = dot(keys, jnp.concatenate([none, dout], axis=0))
            delta = jnp.sum(probs * dprobs, axis=0, keepdims=True)
            dscores = probs * (dprobs - delta)
            ds_all[head] += dscores
            dscores = dscores.astype(bfloat)
            probs = probs.astype(bfloat)
            window = pl.ds(start, KEYS)
            dqt[at, :] = (dot(kvt_all[head, :HEAD_DIM, window], dscores) * HEAD_DIM**-0.5).astype(bfloat)
            dkvt[head, :HEAD_DIM, window] += dot(query, dscores, NT)
            dkvt[head, HEAD_DIM:, window] += dot(dout, probs, NT)

    pl.when(need[step + first] > 0)(lambda: run(True))
    pl.when(need[step + first] <= 0)(lambda: run(False))

    @pl.when(step == pl.num_programs(0) - 1)
    def _():
        if not ends:
            behind[...] = dkvt[:, :, :WINDOW].astype(bfloat)
            dkv_own[...] = dkvt[:, :, WINDOW:]
        else:
            for head in range(heads):
                for chunk in range(CHUNKS):
                    sums[head, chunk : chunk + 1, :] = diagonal_sums(ds_all[head, chunk * QB : (chunk + 1) * QB, :])


def attention_backward(first, steps, span, order, need, low, qt, kvp, kv, vecs, lse, douts, begun=()):
    total, packed = kv.shape[1:]
    begin, heads = span
    pick = begin // heads
    width = heads * HEAD_DIM
    held = KEYS + (steps - 1) * QB
    ends = kvp is None
    own = held if ends else held - WINDOW
    scores = (heads, KEYS, QB)
    order = jnp.concatenate([order, jnp.full((1,), begin, jnp.int32)])
    kernel = functools.partial(backward_kernel, first, ends)
    specs = [
        SMEM,
        SMEM,
        pl.BlockSpec((1, QB), lambda i: (0, i + first)),
        pl.BlockSpec((width, QB), lambda i: (pick, i + first)),
        pl.BlockSpec((heads, own, packed), lambda i: (pick, 0, 0)),
        pl.BlockSpec((heads,) + vecs.shape[1:], lambda i: (pick, 0, 0)),
        pl.BlockSpec((1, 8, QB), lambda i: (i, 0, 0)),
    ] + [pl.BlockSpec((width, douts[0].shape[1]), lambda i: (pick, 0))] * 4
    inputs = [order, need, low, qt, kv, vecs, lse, *douts]
    out_specs = [pl.BlockSpec((width, QB), lambda i: (0, i))]
    out_shape = [jax.ShapeDtypeStruct((width, steps * QB), bfloat)]
    scratch = [
        pltpu.VMEM((heads, held, packed), bfloat),
        pltpu.VMEM((heads, packed, held), bfloat),
        pltpu.VMEM(scores, single),
        pltpu.VMEM((width, total), bfloat),
    ]
    if ends:
        specs += [
            pl.BlockSpec((heads, packed, WINDOW), lambda i: (pick, 0, 0)),
            pl.BlockSpec(scores, lambda i: (pick, 0, 0)),
        ]
        inputs += list(begun)
        shapes = [((heads, packed, held), single), ((heads, 8, 2 * QB), single)]
        scratch.append(pltpu.VMEM(scores, single))
    else:
        specs.append(full(kvp.shape))
        inputs.append(kvp)
        shapes = [((heads, packed, WINDOW), bfloat), ((heads, packed, held - WINDOW), single), (scores, single)]
        scratch.append(pltpu.VMEM((heads, packed, held), single))
    out_specs += [full(shape) for shape, _ in shapes]
    out_shape += [jax.ShapeDtypeStruct(shape, kind) for shape, kind in shapes]
    return pl.pallas_call(
        kernel,
        grid=(steps,),
        in_specs=specs,
        out_specs=out_specs,
        out_shape=out_shape,
        scratch_shapes=scratch,
        compiler_params=params(60, 1),
        cost_estimate=light(),
        name="attend_back",
    )(*inputs)


def settle_kernel(
    order, dq0, dq1, dq2, dkv1, dkv2, behind, normed, sums1, sums2, hot, gain_terms, router0, router1,
    out0, out1, out2, out3, grad,
):
    heads = behind.shape[0]
    rows = out0.shape[1]
    outs = (out0, out1, out2, out3)
    edge = dkv1.shape[2] - WINDOW
    held = [(dq1, dkv1, sums1, number) for number in range(dkv1.shape[0])]
    held += [(dq2, dkv2, sums2, number) for number in range(dkv2.shape[0])]
    parts = []
    for head, (dq, dkvt, _, number) in enumerate(held):
        at = slice(number * HEAD_DIM, (number + 1) * HEAD_DIM)
        last = dkvt[number, :, edge:] + behind[head].astype(single)
        parts.append(jnp.concatenate([dq0[head * HEAD_DIM : (head + 1) * HEAD_DIM, :], dq[at, :]], axis=1))
        parts.append(jnp.concatenate([dkvt[number, :, :edge], last], axis=1).astype(bfloat))
    whole = jnp.concatenate(parts, axis=0)

    def put(place, lane):
        outs[place][...] = whole[:, lane * rows : (lane + 1) * rows]

    by_lane(order[0], put)
    total = None
    for lane in range(len(outs)):
        term = dot(whole[:, lane * rows : (lane + 1) * rows], normed[lane])
        total = term if total is None else total + term
    total = total.astype(bfloat)
    part = grad.shape[2]
    count = total.shape[0]
    found = []
    for _, _, ref, number in held:
        value = None
        for chunk in range(CHUNKS):
            term = lax.dot_general(
                jnp.broadcast_to(ref[number, chunk : chunk + 1, :], (8, 2 * QB)),
                hot[chunk * 2 * QB : (chunk + 1) * 2 * QB, :],
                (NN, ((), ())),
                precision=lax.Precision.HIGHEST,
                preferred_element_type=single,
            )
            value = term if value is None else value + term
        found.append(value[0:1, :])
    found.append(jnp.zeros((1, part - BUCKETS * heads), single))
    rel = jnp.broadcast_to(jnp.concatenate(found, axis=1), (16, part))
    router = (router0[...] + router1[...]).astype(bfloat)
    for lane in range(len(outs)):
        columns = slice(lane * part, (lane + 1) * part)
        grad[lane, :count, :] = total[:, columns]
        mine = jnp.where(order[0] == lane, 1.0, 0.0)
        grad[lane, count : count + 16, :] = (rel * mine).astype(bfloat)
        terms = jnp.broadcast_to(gain_terms[:, columns], (16, part))
        grad[lane, count + 16 : count + 32, :] = terms.astype(bfloat)
        begin = count + 32 + router.shape[0]
        grad[lane, count + 32 : begin, :] = router[:, columns]
        if begin < grad.shape[1]:
            grad[lane, begin:, :] = jnp.zeros((grad.shape[1] - begin, part), bfloat)


def settle(order, dq0, late, behind, normed, sums, hot, gain_terms, routers, multiple):
    lanes, rows, width = normed.shape
    tall = 3 * width // lanes
    count = tall + 32 + routers[0].shape[0]
    count = -(-count // multiple) * multiple
    (dq1, dkv1), (dq2, dkv2) = late
    return once(
        settle_kernel,
        "settle",
        (order, dq0, dq1, dq2, dkv1, dkv2, behind, normed, *sums, hot, gain_terms, *routers),
        [((tall, rows), bfloat)] * lanes + [((lanes, count, width // lanes), bfloat)],
    )


def middle_kernel(o0, o1, o2, o3, w0, w1, w2, w3, x, gain, code, y_out, send0, send1):
    y = x[...].astype(single)
    for ref, weight in ((o0, w0), (o1, w1), (o2, w2), (o3, w3)):
        y = y + dot(ref[...], weight[...], TN)
    y_out[...] = y
    inverse = lax.rsqrt(jnp.mean(y * y, axis=-1, keepdims=True) + epsilon)
    normed = (y * inverse * gain[...]).astype(bfloat)
    slots = send0.shape[0]
    for number, ref in enumerate((send0, send1)):
        slot = lax.broadcasted_iota(jnp.int32, (slots, y.shape[0]), 0) + number * slots
        pick = ((slot == code[0:1, :]) | (slot == code[1:2, :])).astype(bfloat)
        ref[...] = dot(pick, normed).astype(bfloat)


def middle(ots, w_out, x, gain, code, slots):
    rows, width = x.shape
    return once(
        middle_kernel,
        "middle",
        (*ots, *w_out, x, gain, code),
        [((rows, width), single), ((slots, width), bfloat), ((slots, width), bfloat)],
    )


NOTES = 16


def send_kernel(code, value, *outs):
    blocks, count = outs[0].shape[:2]
    slot = lax.broadcasted_iota(jnp.int32, (count, value.shape[0]), 0)
    for block in range(blocks):
        for number, out in enumerate(outs):
            here = slot + ((number // 2 * blocks + block) * 2 + number % 2) * count
            pick = ((here == code[0:1, :]) | (here == code[1:2, :])).astype(bfloat)
            out[block] = dot(pick, value[...]).astype(bfloat)


def send_rows(code, value, blocks, slot_rows):
    shape = (blocks, slot_rows // 2, value.shape[1])
    return once(send_kernel, "send_rows", (code, value), [(shape, bfloat)] * 4)


def send_noted_kernel(part, notes, out):
    for block in range(part.shape[0]):
        out[block, NOTES:, :] = part[block]
        out[block, :NOTES, :] = jnp.broadcast_to(notes[...], (NOTES, part.shape[2]))


def send_noted(part, notes):
    blocks, count, width = part.shape
    outputs = [((blocks, count + NOTES, width), bfloat)]
    return once(send_noted_kernel, "send_noted", (part, notes), outputs)[0]


def collect(code, refs):
    total = None
    for number, ref in enumerate(refs):
        slots = ref.shape[0]
        slot = lax.broadcasted_iota(jnp.int32, (code.shape[0], slots), 1) + number * slots
        pick = ((slot == code[:, 0:1]) | (slot == code[:, 1:2])).astype(bfloat)
        part = dot(pick, ref[...])
        total = part if total is None else total + part
    return total


def return_kernel(d0, d1, code, y, gain, cotangent, w0, w1, w2, w3, o0, o1, o2, o3, dy_out, gg_out, *dots):
    dn = collect(code, (d0, d1))
    values = y[...]
    inverse = lax.rsqrt(jnp.mean(values * values, axis=-1, keepdims=True) + epsilon)
    hat = values * inverse
    gg_out[...] = jnp.sum(dn * hat, axis=0, keepdims=True)
    scaled = dn * gain[...]
    dy = cotangent[...].astype(single) + inverse * (scaled - hat * jnp.mean(scaled * hat, axis=-1, keepdims=True))
    dy_out[...] = dy
    low = dy.astype(bfloat)
    for place, (ref, weight) in enumerate(((o0, w0), (o1, w1), (o2, w2), (o3, w3))):
        dots[place][...] = dot(weight[...], low, NT).astype(bfloat)
        dots[place + 4][...] = dot(ref[...], low).astype(bfloat)


def return_rows(d0, d1, code, y, gain, cotangent, w_out, ots):
    rows, width = y.shape
    lanes = len(ots)
    return once(
        return_kernel,
        "return_rows",
        (d0, d1, code, y, gain, cotangent, *w_out, *ots),
        [((rows, width), single), ((1, width), single)]
        + [((width // lanes, rows), bfloat)] * lanes
        + [((width // lanes, width), bfloat)] * lanes,
    )


def finish_kernel(z0, z1, code, y, out):
    out[...] = (y[...] + collect(code, (z0, z1))).astype(bfloat)


def finish(z0, z1, code, y):
    return once(finish_kernel, "finish", (z0, z1, code, y), [(y.shape, bfloat)])[0]


def unpack_kernel(value, wq, wk, wv, gain, q_out, k_out, v_out, other_out, gain_out):
    lanes, _, part = value.shape
    heads = part // HEAD_DIM
    mark = 3 * part
    others = None
    for lane in range(lanes):
        whole = value[lane, :mark, :].astype(single).T
        for head in range(heads):
            at = slice((lane * heads + head) * HEAD_DIM, (lane * heads + head + 1) * HEAD_DIM)
            for number, ref in enumerate((q_out, k_out, v_out)):
                begin = (3 * head + number) * HEAD_DIM
                ref[:, at] = whole[:, begin : begin + HEAD_DIM]
        term = value[lane, mark + 16 : mark + 32 + other_out.shape[0] - 16, :].astype(single)
        others = term if others is None else others + term
    other_out[...] = others
    total = None
    for ref, weight in ((q_out, wq), (k_out, wk), (v_out, wv)):
        term = jnp.sum(ref[...] * weight[...].astype(single), axis=1, keepdims=True)
        total = term if total is None else total + term
    gain_out[...] = total / gain[...].astype(single)


def unpack(value, wq, wk, wv, gain, heads, experts):
    part, width = wq.shape
    outputs = [((part, width), single)] * 3 + [((16 + experts, part), single), ((part, 1), single)]
    return once(unpack_kernel, "unpack", (value, wq, wk, wv, gain), outputs)


def tail_kernel(order, *refs):
    *pieces, wt, x, gain, dy, out = refs
    dn = None
    for number, ref in enumerate(pieces):
        block = order[number % 4]
        tall = ref.shape[0]
        begin = block * tall
        term = dot(ref[...], wt[pl.ds(pl.multiple_of(begin, 64), tall), :], TN)
        dn = term if dn is None else dn + term
    values = x[...].astype(single)
    inverse = lax.rsqrt(jnp.mean(values * values, axis=-1, keepdims=True) + epsilon)
    hat = values * inverse
    scaled = dn * gain[...]
    out[...] = dy[...] + inverse * (scaled - hat * jnp.mean(scaled * hat, axis=-1, keepdims=True))


def tail(order, pieces, wt, x, gain, dy):
    return once(tail_kernel, "tail", (order, *pieces, wt, x, gain, dy), [(x.shape, single)])[0]


GELU_0 = 0.7978845608028654
GELU_1 = 0.7978845608028654 * 0.044715
FF_BLOCK = 512
ROW_BLOCK = 256


def expert_kernel(
    mine, xs, router, other, w1, w2, da, cot, g10, g11, g12, g13, g2, dx_out, z_out, m_out, total, result, dgate, gate, act_all, du_all, xst, dzt
):
    step = pl.program_id(0)
    rows = xs.shape[0]
    experts = router.shape[0]

    def picks():
        lane = lax.broadcasted_iota(jnp.int32, (rows, experts), 1)
        return lane == mine[0], lane == other[...] - 1

    @pl.when(step == 0)
    def _():
        logits = dot(xs[...], router[...], NT)
        own, rest = picks()
        margin = jnp.sum(jnp.where(own, logits, 0.0) - jnp.where(rest, logits, 0.0), axis=1, keepdims=True)
        value = 1.0 / (1.0 + jnp.exp(-margin))
        value = jnp.where(other[...] > 0, value, 0.0)
        gate[...] = jnp.broadcast_to(value, gate.shape)
        dgate[...] = jnp.zeros_like(dgate)
        total[...] = jnp.zeros_like(total)
        result[...] = jnp.zeros_like(result)
        for begin in range(0, rows, ROW_BLOCK):
            at = slice(begin, begin + ROW_BLOCK)
            xst[:, at] = xs[at, :].T
            dzt[:, at] = (cot[at, :].astype(single) * gate[at, 0:1]).astype(bfloat).T

    for begin in range(0, rows, ROW_BLOCK):
        at = slice(begin, begin + ROW_BLOCK)
        u = dot(xs[at, :], w1[...])
        square = u * u
        tan = jnp.tanh(u * (GELU_0 + GELU_1 * square))
        half = 0.5 + 0.5 * tan
        act = u * half
        slope = half + act * (1.0 - half) * (2.0 * GELU_0 + 6.0 * GELU_1 * square)
        back = da[at, :].astype(single)
        product = act * back
        part = product[:, :128]
        for col in range(128, product.shape[1], 128):
            part = part + product[:, col : col + 128]
        dgate[at, :] += part
        act_all[at, :] = act.astype(bfloat)
        du_all[at, :] = (gate[at, 0:1] * back * slope).astype(bfloat)
    total[...] += dot(du_all[...], w1[...], NT)
    result[...] += dot(act_all[...], w2[...])
    grad = dot(xst[...], du_all[...]).astype(bfloat)
    part = g10.shape[0]

    def put(place, lane):
        (g10, g11, g12, g13)[place][...] = grad[lane * part : (lane + 1) * part, :]

    by_lane(mine[1], put)
    g2[...] = dot(dzt[...], act_all[...]).astype(bfloat).T

    @pl.when(step == pl.num_programs(0) - 1)
    def _():
        own, rest = picks()
        value = gate[:, 0:1]
        weight = value * (1.0 - value) * jnp.sum(dgate[...], axis=1, keepdims=True)
        m = (weight * (own.astype(single) - rest.astype(single))).astype(bfloat)
        m_out[...] = dot(m, xs[...], TN)
        dx_out[...] = (total[...] + dot(m, router[...])).astype(bfloat)
        z_out[...] = (result[...] * value).astype(bfloat)


def expert(mine, xs, router, other, w1, w2, da, cot, local):
    rows, width = xs.shape
    inner = w1.shape[2]
    experts = router.shape[0]
    block = FF_BLOCK
    whole = lambda shape: pl.BlockSpec(shape, lambda f: (0,) * len(shape))
    return pl.pallas_call(
        expert_kernel,
        grid=(inner // block,),
        in_specs=[
            SMEM,
            whole((rows, width)),
            whole((experts, width)),
            whole((rows, 1)),
            pl.BlockSpec((None, width, block), lambda f: (local, 0, f)),
            pl.BlockSpec((None, block, width), lambda f: (local, f, 0)),
            pl.BlockSpec((rows, block), lambda f: (0, f)),
            whole((rows, width)),
        ],
        out_specs=[
            *[pl.BlockSpec((width // len(MASKS), block), lambda f: (0, f))] * len(MASKS),
            pl.BlockSpec((block, width), lambda f: (f, 0)),
            whole((rows, width)),
            whole((rows, width)),
            whole((experts, width)),
        ],
        out_shape=[
            *[jax.ShapeDtypeStruct((width // len(MASKS), inner), bfloat)] * len(MASKS),
            jax.ShapeDtypeStruct((inner, width), bfloat),
            jax.ShapeDtypeStruct((rows, width), bfloat),
            jax.ShapeDtypeStruct((rows, width), bfloat),
            jax.ShapeDtypeStruct((experts, width), single),
        ],
        scratch_shapes=[
            pltpu.VMEM((rows, width), single),
            pltpu.VMEM((rows, width), single),
            pltpu.VMEM((rows, 128), single),
            pltpu.VMEM((rows, 128), single),
            pltpu.VMEM((rows, block), bfloat),
            pltpu.VMEM((rows, block), bfloat),
            pltpu.VMEM((width, rows), bfloat),
            pltpu.VMEM((width, rows), bfloat),
        ],
        compiler_params=params(60, 1),
        cost_estimate=cost(20 * rows * width * inner, 8 * rows * inner + 8 * width * inner, rows * inner),
        name="expert",
    )(mine, xs, router, other, w1, w2, da, cot)


def tie(*values):
    return lax.optimization_barrier(values)


def swap(value, axis, mask):
    return lax.ppermute(value, axis, [(i, i ^ mask) for i in range(lax.axis_size(axis))])


def per_device(
    hidden_in,
    norm1_gain,
    w_query,
    w_key,
    w_value,
    w_out,
    rel_bias,
    norm2_gain,
    w_router,
    w_first,
    w_second,
    routes,
    priority,
    segments,
    grad_out,
):
    lanes = lax.axis_size("head")
    blocks = lax.axis_size("seq")
    lane = lax.axis_index("head")
    place = lax.axis_index("seq")
    rows, width = hidden_in.shape[2:]
    x = hidden_in.reshape(rows, width)
    total = rows * lanes
    part = width // lanes
    heads = part // HEAD_DIM
    cotangent = grad_out.reshape(rows, width)
    experts = w_router.shape[1]
    local = w_first.shape[0]
    slot_rows = max(2, 4 * rows // experts)
    slots = blocks * slot_rows
    capacity = 5 * rows * lanes // (2 * local)

    far = swap(x, "head", 2)
    near = swap(x, "head", 1)
    order = jnp.stack([lane, lane ^ 2, lane ^ 1, lane ^ 3]).astype(jnp.int32)
    at = lambda value, mask: lax.dynamic_index_in_dim(value, lane ^ mask, 0, keepdims=False)

    def trade(value):
        return [value[0]] + [swap(value[place], "head", MASKS[place]) for place in range(1, lanes)]

    route_t = routes.reshape(rows, -1).T
    top_count = route_t.shape[0]
    pair_routes = route_t.reshape(-1)
    pair_prio = priority.reshape(rows, -1).T.reshape(-1)
    expert_ids = jnp.arange(experts, dtype=jnp.int32)
    pair_hot = (expert_ids[:, None] == pair_routes[None, :]).astype(jnp.int32)
    earlier = (pair_routes[:, None] == pair_routes[None, :]) & (pair_prio[:, None] < pair_prio[None, :])
    local_rank = jnp.sum(earlier.astype(jnp.int32), axis=0)
    code = (pair_routes % local) * slots + (pair_routes // local) * slot_rows + local_rank
    code_t = code.reshape(top_count, rows)
    code = code_t.T

    def exchange(value):
        return lax.all_to_all(
            value.reshape(blocks, slot_rows, -1), "seq", split_axis=0, concat_axis=0, tiled=True
        ).reshape(slots, -1)


    block_rank = (jnp.min(pair_prio) // (top_count * rows)).reshape(1)
    tally = jnp.concatenate([jnp.sum(pair_hot, axis=1), block_rank, jnp.zeros((part - experts - 1,), jnp.int32)])
    gains = jnp.stack([norm1_gain, norm2_gain, tally.astype(bfloat)])
    gains = jnp.concatenate([gains, jnp.zeros((GAINS - 3, part), bfloat)], axis=0)
    hot, allowed = lane_tables()
    table = rel_bias.reshape(heads, BUCKETS)
    vecs = dot(table, jnp.asarray(hot.T, bfloat)).reshape(heads, CHUNKS, 2 * QB)
    vecs = jnp.where(jnp.asarray(allowed)[None], vecs, MASKED)
    vecs = jnp.concatenate([vecs, jnp.zeros((heads, 8 - CHUNKS, 2 * QB), single)], axis=1)
    base = place * total
    own = lax.dynamic_slice_in_dim(segments, base, total, 0)
    low = jnp.zeros_like(own)
    for number in range(1, 4):
        low = jnp.where(own == number, jnp.sum((segments < number).astype(jnp.int32)), low)
    low = low - base + WINDOW
    need = (jnp.max(low.reshape(-1, QB), axis=1) > jnp.arange(total // QB) * QB).astype(jnp.int32)
    low = low.reshape(1, total)
    packed = pack(order, w_query, w_key, w_value, w_router.T, gains)
    far, near, code_t, low, need, vecs, code, packed = tie(far, near, code_t, low, need, vecs, code, packed)
    packed = trade(packed)
    both = swap(far, "head", 1)
    cot_parts = list(send_rows(code_t, cotangent, blocks, slot_rows))
    spread_out = lambda value: lax.all_to_all(value, "seq", split_axis=0, concat_axis=0, tiled=True)
    cots = [spread_out(cot_parts[0])]
    packed, both, w_second, w_out, cots[0], cot_parts = tie(packed, both, w_second, w_out, cots[0], cot_parts)
    cots.append(spread_out(cot_parts[1]))

    out_far = swap(w_out, "head", 2)
    out_near = swap(w_out, "head", 1)
    second_full = lax.all_gather(w_second, "head", axis=1, tiled=True)

    normed, qt, kv, kv_last, w_rows, router_t, gains = project(order, (x, far, near, both), packed, heads, experts)
    w_rows_full = lax.all_gather(w_rows, "head", axis=0, tiled=True)
    gain_one, gain_two = gains[0:1], gains[1:2]
    kvp = lax.ppermute(kv_last, "seq", [(i, i + 1) for i in range(blocks - 1)])
    early = WINDOW // QB
    later = total // QB - early
    *ot, lse_later = attention_forward(early, later, order, need, low, qt, None, kv, vecs, lanes)
    ot, kvp, cots[1], cot_parts[2] = tie(ot, kvp, cots[1], cot_parts[2])
    cots.append(spread_out(cot_parts[2]))
    *ot, lse_early = attention_forward(0, early, order, need, low, qt, kvp, kv, vecs, lanes, ot)
    ot, out_far, out_near = tie(ot, out_far, out_near)
    w_outs = (w_out, out_far, out_near, swap(out_far, "head", 1))
    ots = trade(ot)
    ots, w_first, cots[2], cot_parts[3] = tie(ots, w_first, cots[2], cot_parts[3])
    noted = spread_out(send_noted(cot_parts[3], gains[2:3].astype(bfloat)))
    first_full = lax.all_gather(w_first, "head", axis=1, tiled=True)

    y, *sends = middle(ots, w_outs, x, gain_two, code_t, slots)
    sends[0], noted = tie(sends[0], noted)
    cots.append(noted[:, NOTES:, :])

    tallies = noted[:, 0, :].reshape(blocks * lanes, part).astype(jnp.int32)
    ahead = (tallies[:, experts : experts + 1] < block_rank[None, :]).astype(jnp.int32)
    offsets = jnp.sum(tallies[:, :experts] * ahead, axis=0)
    kept = (jnp.sum(pair_hot * offsets[:, None], axis=0) + local_rank < capacity).reshape(top_count, rows)
    slot_ids = jnp.arange(local * slots, dtype=jnp.int32)[:, None]
    other = jnp.sum(
        jnp.where(slot_ids == code_t[0:1], jnp.where(kept[0:1], route_t[1:2] + 1, 0), 0)
        + jnp.where(slot_ids == code_t[1:2], jnp.where(kept[1:2], route_t[0:1] + 1, 0), 0),
        axis=1,
    )
    cot_slots = [jnp.concatenate([cots[2 * i], cots[2 * i + 1]], axis=1).reshape(slots, width) for i in range(local)]
    backs = [dot(cot_slots[0], second_full[0], NT).astype(bfloat)]
    other, backs[0] = tie(other, backs[0])
    other = other.reshape(local, blocks, slot_rows)
    far_others = [
        swap(lax.dynamic_index_in_dim(other, place ^ mask, 1, keepdims=False), "seq", mask) for mask in range(1, blocks)
    ]
    mine = jnp.stack([place * local, lane]).astype(jnp.int32)
    backs.append(dot(cot_slots[1], second_full[1], NT).astype(bfloat))
    received = [exchange(sends[0])]
    sends[1], far_others, *backs = tie(sends[1], far_others, *backs)
    received.append(exchange(sends[1]))
    far_others = jnp.concatenate([lax.dynamic_index_in_dim(other, place, 1, keepdims=False)[None], jnp.stack(far_others)])
    other = jnp.stack(
        [lax.dynamic_index_in_dim(far_others, place ^ number, 0, keepdims=False) for number in range(blocks)], axis=1
    ).reshape(local, slots, 1)

    def run_expert(number):
        return expert(
            mine + jnp.asarray([number, 0], jnp.int32),
            received[number],
            router_t,
            other[number],
            first_full,
            second_full,
            backs[number],
            cot_slots[number],
            number,
        )

    received[1], w_rows_full, (*first_parts0, second0, dx0, z0, router0) = tie(
        received[1], w_rows_full, run_expert(0)
    )
    returns = [exchange(dx0)]
    second0 = lax.psum_scatter(second0, "head", scatter_dimension=0, tiled=True)
    returns[0], second0, (*first_parts1, second1, dx1, z1, router1) = tie(returns[0], second0, run_expert(1))
    def near_parts(parts):
        return swap(parts[3], "head", 1), swap(parts[2], "head", 1)

    def add(one, two, kind=single):
        return (one.astype(single) + two.astype(single)).astype(kind)

    def scatter(value):
        return lax.psum_scatter(value, "head", scatter_dimension=0, tiled=True)

    cross0, direct0 = near_parts(first_parts0)
    returns.append(exchange(dx1))
    across0 = swap(add(first_parts0[1], cross0, bfloat), "head", 2)
    cross1, direct1 = near_parts(first_parts1)
    second1 = scatter(second1)

    returns[1], across0 = tie(returns[1], across0)
    first0 = add(add(first_parts0[0], direct0), across0)
    dy, gain_terms, *douts = return_rows(
        returns[0], returns[1], code, y, gain_two, cotangent, w_outs, ots
    )
    douts, outw = trade(douts[:lanes]), douts[lanes:]
    dy, z0 = tie(dy, z0)
    z_back = [exchange(z0)]
    douts, outw, cross1, direct1 = tie(douts, outw, cross1, direct1)
    outw_cross, outw_direct = near_parts(outw)
    across1 = swap(add(first_parts1[1], cross1, bfloat), "head", 2)

    def sum_blocks(value):
        count, last = value.shape[1:]
        value = value.reshape(lanes * blocks, count // blocks, last)
        value = lax.all_to_all(value, ("head", "seq"), split_axis=0, concat_axis=0, tiled=True)
        return jnp.sum(value.reshape(lanes, blocks, -1, last).astype(single), axis=1).astype(bfloat)

    dq_early, behind, dkvt_early, ds_early = attention_backward(
        0, early, (0, heads), order, need, low, qt, kvp, kv, vecs, lse_early, douts
    )
    behind = lax.ppermute(behind, "seq", [(i + 1, i) for i in range(blocks - 1)])
    dq_early, outw_cross, outw_direct, second1 = tie(dq_early, outw_cross, outw_direct, second1)
    outw_across = swap(add(outw[1], outw_cross, bfloat), "head", 2)
    cut = heads - 1

    def later_part(span):
        return attention_backward(
            early, later, span, order, need, low, qt, None, kv, vecs, lse_later, douts, (dkvt_early, ds_early)
        )

    dq_last, dkv_last, sums_last = later_part((cut, heads - cut))
    dkv_last, z_back[0], z1, behind = tie(dkv_last, z_back[0], z1, behind)
    z_back.append(exchange(z1))
    ds_early, dkv_last = tie(ds_early, dkv_last)
    dq_first, dkv_first, sums_first = later_part((0, cut))
    dq_first, outw_across, across1 = tie(dq_first, outw_across, across1)
    grad_outw = add(add(outw[0], outw_direct), outw_across, bfloat)
    grad_outw = spread_out(grad_outw.reshape(blocks, -1, part))
    *parts, grad_part = settle(
        order,
        dq_early,
        ((dq_first, dkv_first), (dq_last, dkv_last)),
        behind,
        normed,
        (sums_first, sums_last),
        jnp.asarray(hot, single),
        gain_terms,
        (router0, router1),
        max(16, blocks),
    )
    pieces = trade(parts)
    first1 = add(add(first_parts1[0], direct1), across1)
    output = finish(z_back[0], z_back[1], code, y).reshape(hidden_in.shape)

    grad_part, z_back[1] = tie(grad_part, z_back[1])
    value = sum_blocks(grad_part)
    value, dy, pieces, grad_outw = tie(value, dy, pieces, grad_outw)
    grad_hidden = tail(order, pieces, w_rows_full, x, gain_one, dy).reshape(hidden_in.shape)
    grad_outw = jnp.sum(grad_outw.astype(single), axis=0).astype(bfloat)
    count = value.shape[1]
    value = jnp.concatenate([value.reshape(-1, part), grad_outw], axis=0)
    value = lax.all_to_all(
        jnp.broadcast_to(value[None], (blocks,) + value.shape), "seq", split_axis=0, concat_axis=0, tiled=True
    )
    grad_outw = value[:, lanes * count :, :].reshape(part, width)
    value = value[:, : lanes * count, :].reshape(blocks, lanes, count, part)
    value = value.transpose(1, 0, 2, 3).reshape(lanes, -1, part)
    mark = 3 * part
    grad_rel = value[:, mark, : heads * BUCKETS].astype(single)
    grad_rel = lax.dynamic_index_in_dim(grad_rel, lane, 0, keepdims=False)
    *grads, others, grad_norm1 = unpack(value, w_query, w_key, w_value, norm1_gain.reshape(part, 1), heads, experts)
    return (
        output,
        grad_hidden,
        grad_norm1.reshape(part),
        grads[0],
        grads[1],
        grads[2],
        grad_outw.astype(single),
        grad_rel,
        others[0],
        others[16:].T,
        jnp.stack([first0, first1]),
        jnp.stack([second0, second1]).astype(single),
    )


def solution(mesh):
    return jax.shard_map(
        per_device,
        mesh=mesh,
        in_specs=(
            P("seq", "head", None, None),
            P("head"),
            P("head", None),
            P("head", None),
            P("head", None),
            P("head", None),
            P("head"),
            P("head"),
            P("head", None),
            P("seq", "head", None),
            P("seq", "head", None),
            P("seq", "head", None, None),
            P("seq", "head", None, None),
            P(),
            P("seq", "head", None, None),
        ),
        out_specs=(
            P("seq", "head", None, None),
            P("seq", "head", None, None),
            P("head"),
            P("head", None),
            P("head", None),
            P("head", None),
            P("head", None),
            P("head"),
            P("head"),
            P("head", None),
            P("seq", "head", None),
            P("seq", "head", None),
        ),
        check_vma=False,
    )
```

```python
import functools

import jax
import jax.numpy as jnp
import numpy as np
from jax import lax
from jax.experimental import pallas as pl
from jax.experimental.pallas import tpu as pltpu
from jax.sharding import PartitionSpec as P

HEAD_DIM = 64
WINDOW = 1024
BUCKETS = 32
QB = 256
CHUNKS = WINDOW // QB + 1
KEYS = CHUNKS * QB
MASKED = -1e30
epsilon = 1e-06
bfloat = jnp.bfloat16
single = jnp.float32
MIB = 1 << 20

VMEM = pl.BlockSpec(memory_space=pltpu.VMEM)
SMEM = pl.BlockSpec(memory_space=pltpu.SMEM)


def dot(a, b, dims=((1,), (0,))):
    return lax.dot_general(a, b, (dims, ((), ())), preferred_element_type=single)


NN = ((1,), (0,))
NT = ((1,), (1,))
TN = ((0,), (0,))


def params(mib, grid=0):
    extra = {"dimension_semantics": ("arbitrary",) * grid} if grid else {}
    return pltpu.CompilerParams(vmem_limit_bytes=mib * MIB, **extra)


def full(shape):
    return pl.BlockSpec(tuple(shape), lambda i: (0,) * len(shape))


def once(kernel, name, inputs, outputs, scratch=()):
    found = pl.pallas_call(
        kernel,
        grid=(1,),
        in_specs=[SMEM if value.ndim == 1 else full(value.shape) for value in inputs],
        out_specs=[full(shape) for shape, _ in outputs],
        out_shape=[jax.ShapeDtypeStruct(shape, kind) for shape, kind in outputs],
        scratch_shapes=list(scratch),
        compiler_params=params(60, 1),
        cost_estimate=light(),
        name=name,
    )(*inputs)
    return found


def cost(flops, moved, trans=0):
    return pl.CostEstimate(flops=int(flops), bytes_accessed=int(moved), transcendentals=int(trans))


def light():
    return cost(1000, 1000)


MASKS = (0, 2, 1, 3)


def by_lane(own, action):
    for lane in range(len(MASKS)):

        @pl.when(own == lane)
        def _():
            for place, mask in enumerate(MASKS):
                action(place, lane ^ mask)


def bucket_edges(window_len, bucket_count):
    middle = bucket_count // 2
    edge_list = []
    for number in range(1, bucket_count):
        if number < middle:
            edge_list.append(number)
        else:
            edge_list.append(int(middle * (window_len / middle) ** ((number - middle) / middle)))
    return edge_list


def lane_tables():
    lane = np.arange(2 * QB)
    offset = np.where(lane < QB, lane, lane - 2 * QB)
    distance = WINDOW - QB * np.arange(CHUNKS)[:, None] + offset[None, :]
    allowed = (distance >= 0) & (distance < WINDOW)
    bucket = np.zeros(distance.shape, np.int32)
    for edge_value in bucket_edges(WINDOW, BUCKETS):
        bucket = bucket + (distance >= edge_value)
    hot = (bucket.reshape(-1)[:, None] == np.arange(BUCKETS)[None, :]) & allowed.reshape(-1)[:, None]
    return hot, allowed


GAINS = 16


def pack_kernel(order, wq, wk, wv, router_t, gains, *outs):
    part = wq.shape[0]
    experts = router_t.shape[0]

    def put(place, lane):
        for number, weight in enumerate((wq, wk, wv)):
            outs[place][:, number * part : (number + 1) * part] = weight[:, lane * part : (lane + 1) * part]

    by_lane(order[0], put)
    rest = outs[0].shape[1] - 3 * part
    for ref in outs:
        ref[:experts, 3 * part :] = router_t[...]
        ref[experts : experts + GAINS, 3 * part :] = gains[...]
        ref[experts + GAINS :, 3 * part :] = jnp.zeros((part - experts - GAINS, rest), bfloat)


def pack(order, wq, wk, wv, router_t, gains):
    part, width = wq.shape
    return once(pack_kernel, "pack", (order, wq, wk, wv, router_t, gains), [((part, width), bfloat)] * len(MASKS))


def project_kernel(
    order, x0, x1, x2, x3, p0, p1, p2, p3, n_out, qt_out, kv_out, kv_last, rows_out, router_out, gain_out, wq, wk, wv
):
    rows, width = x0.shape
    heads = kv_out.shape[0]
    part = heads * HEAD_DIM
    experts = router_out.shape[0]
    packed = (p0, p1, p2, p3)
    for place, ref in enumerate(packed):
        at = pl.ds(pl.multiple_of(order[place] * part, 64), part)
        for number, weight in enumerate((wq, wk, wv)):
            weight[at, :] = ref[:, number * part : (number + 1) * part]

    def spread(skip, count):
        found = []
        for lane in range(len(packed)):
            piece = None
            for place, ref in enumerate(packed):
                value = ref[skip : skip + count, 3 * part :]
                piece = value if piece is None else jnp.where(order[place] == lane, value, piece)
            found.append(piece)
        return jnp.concatenate(found, axis=1)

    router_out[...] = spread(0, experts)
    gains = spread(experts, GAINS).astype(single)
    gain_out[...] = gains[0:8, :]
    wq_t = wq[...].T
    k_t = wk[...].T
    v_t = wv[...].T
    for head in range(heads):
        at = slice(head * HEAD_DIM, (head + 1) * HEAD_DIM)
        for number, value in enumerate((wq_t, k_t, v_t)):
            begin = (3 * head + number) * HEAD_DIM
            rows_out[begin : begin + HEAD_DIM, :] = value[at, :]
    for place, ref in enumerate((x0, x1, x2, x3)):
        block = order[place]
        values = ref[...].astype(single)
        inverse = lax.rsqrt(jnp.mean(values * values, axis=-1, keepdims=True) + epsilon)
        normed = (values * inverse * gain_out[0:1, :]).astype(bfloat)
        n_out[block] = normed
        at = pl.ds(pl.multiple_of(block * rows, 128), rows)
        qt = dot(wq_t, normed, NT).astype(bfloat)
        qt_out[:, at] = qt * bfloat(HEAD_DIM**-0.5)
        for head in range(heads):
            begin = 3 * head * HEAD_DIM + HEAD_DIM
            kv = dot(normed, rows_out[begin : begin + 2 * HEAD_DIM, :], NT)
            kv_out[head, at, :] = kv.astype(bfloat)
    kv_last[...] = kv_out[:, kv_out.shape[1] - WINDOW :, :]


def project(order, pieces, packed, heads, experts):
    rows, width = pieces[0].shape
    lanes = len(MASKS)
    total = rows * lanes
    part = heads * HEAD_DIM
    return once(
        project_kernel,
        "project",
        (order, *pieces, *packed),
        [
            ((lanes, rows, width), bfloat),
            ((part, total), bfloat),
            ((heads, total, 2 * HEAD_DIM), bfloat),
            ((heads, WINDOW, 2 * HEAD_DIM), bfloat),
            ((3 * part, width), bfloat),
            ((experts, width), bfloat),
            ((8, width), single),
        ],
        [pltpu.VMEM((width, part), bfloat)] * 3,
    )


def eye(size):
    return (
        lax.broadcasted_iota(jnp.int32, (size, size), 0) == lax.broadcasted_iota(jnp.int32, (size, size), 1)
    ).astype(bfloat)


def stage_attention(kvp, kv, vecs, kv_all, kvt_all, bias):
    heads = kv_all.shape[0]
    unit = eye(2 * HEAD_DIM)
    for head in range(heads):
        if kvp is None:
            kv_all[head] = kv[head]
        else:
            kv_all[head, :WINDOW, :] = kvp[head]
            kv_all[head, WINDOW:, :] = kv[head]
        kvt_all[head] = dot(unit, kv_all[head], NT).astype(bfloat)
        for chunk in range(CHUNKS):
            row = jnp.broadcast_to(vecs[head, chunk : chunk + 1, :], (QB, 2 * QB))
            tile = pltpu.roll(row, 0, 1, stride=1, stride_axis=0)
            bias[head, chunk * QB : (chunk + 1) * QB, :] = tile[:, :QB]


def keep_rows(scores, step, low):
    key = lax.broadcasted_iota(jnp.int32, scores.shape, 0) + step * QB
    return jnp.where(key >= low, scores, MASKED)


def query_tile(step, first, pieces):
    found = []
    for half in range(QB // 128):
        piece = (step + first) * (QB // 128) + half
        found.append((piece // pieces, pl.ds(pl.multiple_of((piece % pieces) * 128, 128), 128)))
    return found


def forward_kernel(first, order, need, low, qt, keys_in, vecs, *rest):
    *more, out0, out1, out2, out3, lse, kv_all, kvt_all, bias = rest
    outs = (out0, out1, out2, out3)
    step = pl.program_id(0)
    heads = kv_all.shape[0]
    pieces = out0.shape[1] // 128

    @pl.when(step == 0)
    def _():
        if more:
            stage_attention(more[0], keys_in, vecs, kv_all, kvt_all, bias)
            for ref, begun in zip(outs, more[1:]):
                ref[...] = begun[...]
        else:
            stage_attention(None, keys_in, vecs, kv_all, kvt_all, bias)

    start = pl.multiple_of(step * QB, QB)

    def run(masked):
        found = []
        for head in range(heads):
            keys = kv_all[head, pl.ds(start, KEYS), :]
            query = qt[head * HEAD_DIM : (head + 1) * HEAD_DIM, :]
            query = jnp.concatenate([query, jnp.zeros_like(query)], axis=0)
            scores = dot(keys, query) + bias[head]
            if masked:
                scores = keep_rows(scores, step + first, low[...])
            peak = jnp.max(scores, axis=0, keepdims=True)
            expo = jnp.exp(scores - peak)
            total = jnp.sum(expo, axis=0, keepdims=True)
            values = kvt_all[head, HEAD_DIM:, pl.ds(start, KEYS)]
            mixed = dot(values, expo.astype(bfloat)) * (1.0 / total)
            found.append(mixed.astype(bfloat))
            lse[0, head : head + 1, :] = peak + jnp.log(total)
        whole = jnp.concatenate(found, axis=0)
        for half, (owner, spot) in enumerate(query_tile(step, first, pieces)):
            for mask, ref in zip(MASKS, outs):

                @pl.when(jnp.bitwise_xor(owner, order[0]) == mask)
                def _():
                    ref[:, spot] = whole[:, half * 128 : (half + 1) * 128]

    pl.when(need[step + first] > 0)(lambda: run(True))
    pl.when(need[step + first] <= 0)(lambda: run(False))


def attention_forward(first, steps, order, need, low, qt, kvp, kv, vecs, lanes, begun=None):
    heads, total, packed = kv.shape
    width = heads * HEAD_DIM
    held = KEYS + (steps - 1) * QB
    own = held - (0 if kvp is None else WINDOW)
    more = [] if kvp is None else [kvp, *begun]
    return pl.pallas_call(
        functools.partial(forward_kernel, first),
        grid=(steps,),
        in_specs=[
            SMEM,
            SMEM,
            pl.BlockSpec((1, QB), lambda i: (0, i + first)),
            pl.BlockSpec((width, QB), lambda i: (0, i + first)),
            pl.BlockSpec((heads, own, packed), lambda i: (0, 0, 0)),
            full(vecs.shape),
        ]
        + [full(value.shape) for value in more],
        out_specs=[full((width, total // lanes))] * lanes + [pl.BlockSpec((1, 8, QB), lambda i: (i, 0, 0))],
        out_shape=[jax.ShapeDtypeStruct((width, total // lanes), bfloat)] * lanes
        + [jax.ShapeDtypeStruct((steps, 8, QB), single)],
        scratch_shapes=[
            pltpu.VMEM((heads, held, packed), bfloat),
            pltpu.VMEM((heads, packed, held), bfloat),
            pltpu.VMEM((heads, KEYS, QB), single),
        ],
        compiler_params=params(60, 1),
        cost_estimate=light(),
        name="attend",
    )(order, need, low, qt, kv, vecs, *more)


def diagonal_sums(tile):
    wide = jnp.concatenate([tile, jnp.zeros_like(tile)], axis=1)
    row = lax.broadcasted_iota(jnp.int32, wide.shape, 0)
    bit = 1
    while bit < QB:
        wide = jnp.where((row & bit) != 0, pltpu.roll(wide, 2 * QB - bit, 1), wide)
        bit *= 2
    return jnp.sum(wide, axis=0, keepdims=True)


def backward_kernel(first, ends, order, need, low, qt, keys_in, vecs, lse, d0, d1, d2, d3, *rest):
    if ends:
        dkvt_in, ds_in, dqt, dkvt, sums, kv_all, kvt_all, bias, dout_all, ds_all = rest
        kvp = None
    else:
        kvp, dqt, behind, dkv_own, ds_all, kv_all, kvt_all, bias, dout_all, dkvt = rest
    step = pl.program_id(0)
    heads = kv_all.shape[0]
    rows = d0.shape[1]

    @pl.when(step == 0)
    def _():
        stage_attention(kvp, keys_in, vecs, kv_all, kvt_all, bias)
        for place, ref in enumerate((d0, d1, d2, d3)):
            dout_all[:, pl.ds(pl.multiple_of(order[place] * rows, 128), rows)] = ref[...]
        if ends:
            ds_all[...] = ds_in[...]
            dkvt[:, :, :WINDOW] = dkvt_in[...]
            dkvt[:, :, WINDOW:] = jnp.zeros_like(dkvt[:, :, WINDOW:])
        else:
            ds_all[...] = jnp.zeros_like(ds_all)
            dkvt[...] = jnp.zeros_like(dkvt)

    start = pl.multiple_of(step * QB, QB)

    def run(masked):
        for head in range(heads):
            at = slice(head * HEAD_DIM, (head + 1) * HEAD_DIM)
            keys = kv_all[head, pl.ds(start, KEYS), :]
            query = qt[at, :]
            none = jnp.zeros_like(query)
            scores = dot(keys, jnp.concatenate([query, none], axis=0)) + bias[head]
            if masked:
                scores = keep_rows(scores, step + first, low[...])
            probs = jnp.exp(scores - lse[0, pl.ds(order[4] + head, 1), :])
            dout = dout_all[at, pl.ds(pl.multiple_of((step + first) * QB, QB), QB)]
            dprobs = dot(keys, jnp.concatenate([none, dout], axis=0))
            delta = jnp.sum(probs * dprobs, axis=0, keepdims=True)
            dscores = probs * (dprobs - delta)
            ds_all[head] += dscores
            dscores = dscores.astype(bfloat)
            probs = probs.astype(bfloat)
            window = pl.ds(start, KEYS)
            dqt[at, :] = (dot(kvt_all[head, :HEAD_DIM, window], dscores) * HEAD_DIM**-0.5).astype(bfloat)
            dkvt[head, :HEAD_DIM, window] += dot(query, dscores, NT)
            dkvt[head, HEAD_DIM:, window] += dot(dout, probs, NT)

    pl.when(need[step + first] > 0)(lambda: run(True))
    pl.when(need[step + first] <= 0)(lambda: run(False))

    @pl.when(step == pl.num_programs(0) - 1)
    def _():
        if not ends:
            behind[...] = dkvt[:, :, :WINDOW].astype(bfloat)
            dkv_own[...] = dkvt[:, :, WINDOW:]
        else:
            for head in range(heads):
                for chunk in range(CHUNKS):
                    sums[head, chunk : chunk + 1, :] = diagonal_sums(ds_all[head, chunk * QB : (chunk + 1) * QB, :])


def attention_backward(first, steps, span, order, need, low, qt, kvp, kv, vecs, lse, douts, begun=()):
    total, packed = kv.shape[1:]
    begin, heads = span
    pick = begin // heads
    width = heads * HEAD_DIM
    held = KEYS + (steps - 1) * QB
    ends = kvp is None
    own = held if ends else held - WINDOW
    scores = (heads, KEYS, QB)
    order = jnp.concatenate([order, jnp.full((1,), begin, jnp.int32)])
    kernel = functools.partial(backward_kernel, first, ends)
    specs = [
        SMEM,
        SMEM,
        pl.BlockSpec((1, QB), lambda i: (0, i + first)),
        pl.BlockSpec((width, QB), lambda i: (pick, i + first)),
        pl.BlockSpec((heads, own, packed), lambda i: (pick, 0, 0)),
        pl.BlockSpec((heads,) + vecs.shape[1:], lambda i: (pick, 0, 0)),
        pl.BlockSpec((1, 8, QB), lambda i: (i, 0, 0)),
    ] + [pl.BlockSpec((width, douts[0].shape[1]), lambda i: (pick, 0))] * 4
    inputs = [order, need, low, qt, kv, vecs, lse, *douts]
    out_specs = [pl.BlockSpec((width, QB), lambda i: (0, i))]
    out_shape = [jax.ShapeDtypeStruct((width, steps * QB), bfloat)]
    scratch = [
        pltpu.VMEM((heads, held, packed), bfloat),
        pltpu.VMEM((heads, packed, held), bfloat),
        pltpu.VMEM(scores, single),
        pltpu.VMEM((width, total), bfloat),
    ]
    if ends:
        specs += [
            pl.BlockSpec((heads, packed, WINDOW), lambda i: (pick, 0, 0)),
            pl.BlockSpec(scores, lambda i: (pick, 0, 0)),
        ]
        inputs += list(begun)
        shapes = [((heads, packed, held), single), ((heads, 8, 2 * QB), single)]
        scratch.append(pltpu.VMEM(scores, single))
    else:
        specs.append(full(kvp.shape))
        inputs.append(kvp)
        shapes = [((heads, packed, WINDOW), bfloat), ((heads, packed, held - WINDOW), single), (scores, single)]
        scratch.append(pltpu.VMEM((heads, packed, held), single))
    out_specs += [full(shape) for shape, _ in shapes]
    out_shape += [jax.ShapeDtypeStruct(shape, kind) for shape, kind in shapes]
    return pl.pallas_call(
        kernel,
        grid=(steps,),
        in_specs=specs,
        out_specs=out_specs,
        out_shape=out_shape,
        scratch_shapes=scratch,
        compiler_params=params(60, 1),
        cost_estimate=light(),
        name="attend_back",
    )(*inputs)


def settle_kernel(
    order, dq0, dq1, dq2, dkv1, dkv2, behind, normed, sums1, sums2, hot, gain_terms, router0, router1,
    out0, out1, out2, out3, grad,
):
    heads = behind.shape[0]
    rows = out0.shape[1]
    outs = (out0, out1, out2, out3)
    edge = dkv1.shape[2] - WINDOW
    held = [(dq1, dkv1, sums1, number) for number in range(dkv1.shape[0])]
    held += [(dq2, dkv2, sums2, number) for number in range(dkv2.shape[0])]
    parts = []
    for head, (dq, dkvt, _, number) in enumerate(held):
        at = slice(number * HEAD_DIM, (number + 1) * HEAD_DIM)
        last = dkvt[number, :, edge:] + behind[head].astype(single)
        parts.append(jnp.concatenate([dq0[head * HEAD_DIM : (head + 1) * HEAD_DIM, :], dq[at, :]], axis=1))
        parts.append(jnp.concatenate([dkvt[number, :, :edge], last], axis=1).astype(bfloat))
    whole = jnp.concatenate(parts, axis=0)

    def put(place, lane):
        outs[place][...] = whole[:, lane * rows : (lane + 1) * rows]

    by_lane(order[0], put)
    total = None
    for lane in range(len(outs)):
        term = dot(whole[:, lane * rows : (lane + 1) * rows], normed[lane])
        total = term if total is None else total + term
    total = total.astype(bfloat)
    part = grad.shape[2]
    count = total.shape[0]
    found = []
    for _, _, ref, number in held:
        value = None
        for chunk in range(CHUNKS):
            term = lax.dot_general(
                jnp.broadcast_to(ref[number, chunk : chunk + 1, :], (8, 2 * QB)),
                hot[chunk * 2 * QB : (chunk + 1) * 2 * QB, :],
                (NN, ((), ())),
                precision=lax.Precision.HIGHEST,
                preferred_element_type=single,
            )
            value = term if value is None else value + term
        found.append(value[0:1, :])
    found.append(jnp.zeros((1, part - BUCKETS * heads), single))
    rel = jnp.broadcast_to(jnp.concatenate(found, axis=1), (16, part))
    router = (router0[...] + router1[...]).astype(bfloat)
    for lane in range(len(outs)):
        columns = slice(lane * part, (lane + 1) * part)
        grad[lane, :count, :] = total[:, columns]
        mine = jnp.where(order[0] == lane, 1.0, 0.0)
        grad[lane, count : count + 16, :] = (rel * mine).astype(bfloat)
        terms = jnp.broadcast_to(gain_terms[:, columns], (16, part))
        grad[lane, count + 16 : count + 32, :] = terms.astype(bfloat)
        begin = count + 32 + router.shape[0]
        grad[lane, count + 32 : begin, :] = router[:, columns]
        if begin < grad.shape[1]:
            grad[lane, begin:, :] = jnp.zeros((grad.shape[1] - begin, part), bfloat)


def settle(order, dq0, late, behind, normed, sums, hot, gain_terms, routers, multiple):
    lanes, rows, width = normed.shape
    tall = 3 * width // lanes
    count = tall + 32 + routers[0].shape[0]
    count = -(-count // multiple) * multiple
    (dq1, dkv1), (dq2, dkv2) = late
    return once(
        settle_kernel,
        "settle",
        (order, dq0, dq1, dq2, dkv1, dkv2, behind, normed, *sums, hot, gain_terms, *routers),
        [((tall, rows), bfloat)] * lanes + [((lanes, count, width // lanes), bfloat)],
    )


def middle_kernel(o0, o1, o2, o3, w0, w1, w2, w3, x, gain, code, y_out, send0, send1):
    y = x[...].astype(single)
    for ref, weight in ((o0, w0), (o1, w1), (o2, w2), (o3, w3)):
        y = y + dot(ref[...], weight[...], TN)
    y_out[...] = y
    inverse = lax.rsqrt(jnp.mean(y * y, axis=-1, keepdims=True) + epsilon)
    normed = (y * inverse * gain[...]).astype(bfloat)
    slots = send0.shape[0]
    for number, ref in enumerate((send0, send1)):
        slot = lax.broadcasted_iota(jnp.int32, (slots, y.shape[0]), 0) + number * slots
        pick = ((slot == code[0:1, :]) | (slot == code[1:2, :])).astype(bfloat)
        ref[...] = dot(pick, normed).astype(bfloat)


def middle(ots, w_out, x, gain, code, slots):
    rows, width = x.shape
    return once(
        middle_kernel,
        "middle",
        (*ots, *w_out, x, gain, code),
        [((rows, width), single), ((slots, width), bfloat), ((slots, width), bfloat)],
    )


NOTES = 16


def send_kernel(place, value, *outs):
    begin = 0
    for out in outs:
        count = out.shape[0]
        here = lax.broadcasted_iota(jnp.int32, (count, value.shape[0]), 0) + begin
        pick = ((here == place[0:1, :]) | (here == place[1:2, :])).astype(bfloat)
        out[...] = dot(pick, value[...]).astype(bfloat)
        begin += count


def send_rows(place, value, blocks, counts):
    shapes = [((blocks * count, value.shape[1]), bfloat) for count in counts]
    found = once(send_kernel, "send_rows", (place, value), shapes)
    return [part.reshape(blocks, count, -1) for part, count in zip(found, counts)]


def send_noted_kernel(part, notes, out):
    for block in range(part.shape[0]):
        out[block, NOTES:, :] = part[block]
        out[block, :NOTES, :] = jnp.broadcast_to(notes[...], (NOTES, part.shape[2]))


def send_noted(part, notes):
    blocks, count, width = part.shape
    outputs = [((blocks, count + NOTES, width), bfloat)]
    return once(send_noted_kernel, "send_noted", (part, notes), outputs)[0]


def collect(code, refs):
    total = None
    for number, ref in enumerate(refs):
        slots = ref.shape[0]
        slot = lax.broadcasted_iota(jnp.int32, (code.shape[0], slots), 1) + number * slots
        pick = ((slot == code[:, 0:1]) | (slot == code[:, 1:2])).astype(bfloat)
        part = dot(pick, ref[...])
        total = part if total is None else total + part
    return total


def return_kernel(d0, d1, code, y, gain, cotangent, w0, w1, w2, w3, o0, o1, o2, o3, dy_out, gg_out, *dots):
    dn = collect(code, (d0, d1))
    values = y[...]
    inverse = lax.rsqrt(jnp.mean(values * values, axis=-1, keepdims=True) + epsilon)
    hat = values * inverse
    gg_out[...] = jnp.sum(dn * hat, axis=0, keepdims=True)
    scaled = dn * gain[...]
    dy = cotangent[...].astype(single) + inverse * (scaled - hat * jnp.mean(scaled * hat, axis=-1, keepdims=True))
    dy_out[...] = dy
    low = dy.astype(bfloat)
    for place, (ref, weight) in enumerate(((o0, w0), (o1, w1), (o2, w2), (o3, w3))):
        dots[place][...] = dot(weight[...], low, NT).astype(bfloat)
        dots[place + 4][...] = dot(ref[...], low).astype(bfloat)


def return_rows(d0, d1, code, y, gain, cotangent, w_out, ots):
    rows, width = y.shape
    lanes = len(ots)
    return once(
        return_kernel,
        "return_rows",
        (d0, d1, code, y, gain, cotangent, *w_out, *ots),
        [((rows, width), single), ((1, width), single)]
        + [((width // lanes, rows), bfloat)] * lanes
        + [((width // lanes, width), bfloat)] * lanes,
    )


def finish_kernel(z0, z1, code, y, out):
    out[...] = (y[...] + collect(code, (z0, z1))).astype(bfloat)


def finish(z0, z1, code, y):
    return once(finish_kernel, "finish", (z0, z1, code, y), [(y.shape, bfloat)])[0]


def unpack_kernel(value, wq, wk, wv, gain, q_out, k_out, v_out, router_out, norm_out, rel_out, gain_out):
    blocks, lanes, count, part = value.shape
    heads = part // HEAD_DIM
    mark = 3 * part
    others = None
    for lane in range(lanes):
        rows = jnp.concatenate([value[block, lane] for block in range(blocks)], axis=0)
        whole = rows[:mark, :].astype(single).T
        for head in range(heads):
            at = slice((lane * heads + head) * HEAD_DIM, (lane * heads + head + 1) * HEAD_DIM)
            for number, ref in enumerate((q_out, k_out, v_out)):
                begin = (3 * head + number) * HEAD_DIM
                ref[:, at] = whole[:, begin : begin + HEAD_DIM]
        term = rows[mark : mark + 32 + router_out.shape[1], :].astype(single)
        rel_out[lane : lane + 1, :] = term[0:1, :]
        others = term if others is None else others + term
    norm_out[...] = others[16:17, :]
    router_out[...] = others[32:, :].T
    total = None
    for ref, weight in ((q_out, wq), (k_out, wk), (v_out, wv)):
        term = jnp.sum(ref[...] * weight[...].astype(single), axis=1, keepdims=True)
        total = term if total is None else total + term
    total = jnp.broadcast_to(total / gain[...].astype(single), (part, 128))
    gain_out[...] = total.T[0:1, :]


def unpack(value, wq, wk, wv, gain, experts):
    part, width = wq.shape
    outputs = [((part, width), single)] * 3
    outputs += [((part, experts), single), ((1, part), single), ((value.shape[1], part), single), ((1, part), single)]
    return once(unpack_kernel, "unpack", (value, wq, wk, wv, gain), outputs)


def tail_kernel(order, *refs):
    *pieces, wt, x, gain, dy, out = refs
    dn = None
    for number, ref in enumerate(pieces):
        block = order[number % 4]
        tall = ref.shape[0]
        begin = block * tall
        term = dot(ref[...], wt[pl.ds(pl.multiple_of(begin, 64), tall), :], TN)
        dn = term if dn is None else dn + term
    values = x[...].astype(single)
    inverse = lax.rsqrt(jnp.mean(values * values, axis=-1, keepdims=True) + epsilon)
    hat = values * inverse
    scaled = dn * gain[...]
    out[...] = dy[...] + inverse * (scaled - hat * jnp.mean(scaled * hat, axis=-1, keepdims=True))


def tail(order, pieces, wt, x, gain, dy):
    return once(tail_kernel, "tail", (order, *pieces, wt, x, gain, dy), [(x.shape, single)])[0]


GELU_0 = 0.7978845608028654
GELU_1 = 0.7978845608028654 * 0.044715
FF_BLOCK = 512
ROW_BLOCK = 256


def expert_kernel(
    mine, xs, router, other, w1, w2, da, cot, g10, g11, g12, g13, g2, dx_out, z_out, m_out, total, result, dgate, gate, act_all, du_all, xst, dzt
):
    step = pl.program_id(0)
    rows = xs.shape[0]
    experts = router.shape[0]

    def picks():
        lane = lax.broadcasted_iota(jnp.int32, (rows, experts), 1)
        return lane == mine[0], lane == other[...] - 1

    @pl.when(step == 0)
    def _():
        logits = dot(xs[...], router[...], NT)
        own, rest = picks()
        margin = jnp.sum(jnp.where(own, logits, 0.0) - jnp.where(rest, logits, 0.0), axis=1, keepdims=True)
        value = 1.0 / (1.0 + jnp.exp(-margin))
        value = jnp.where(other[...] > 0, value, 0.0)
        gate[...] = jnp.broadcast_to(value, gate.shape)
        dgate[...] = jnp.zeros_like(dgate)
        total[...] = jnp.zeros_like(total)
        result[...] = jnp.zeros_like(result)
        for begin in range(0, rows, ROW_BLOCK):
            at = slice(begin, begin + ROW_BLOCK)
            xst[:, at] = xs[at, :].T
            dzt[:, at] = (cot[at, :].astype(single) * gate[at, 0:1]).astype(bfloat).T

    for begin in range(0, rows, ROW_BLOCK):
        at = slice(begin, begin + ROW_BLOCK)
        u = dot(xs[at, :], w1[...])
        square = u * u
        tan = jnp.tanh(u * (GELU_0 + GELU_1 * square))
        half = 0.5 + 0.5 * tan
        act = u * half
        slope = half + act * (1.0 - half) * (2.0 * GELU_0 + 6.0 * GELU_1 * square)
        back = da[at, :].astype(single)
        product = act * back
        part = product[:, :128]
        for col in range(128, product.shape[1], 128):
            part = part + product[:, col : col + 128]
        dgate[at, :] += part
        act_all[at, :] = act.astype(bfloat)
        du_all[at, :] = (gate[at, 0:1] * back * slope).astype(bfloat)
    total[...] += dot(du_all[...], w1[...], NT)
    result[...] += dot(act_all[...], w2[...])
    grad = dot(xst[...], du_all[...]).astype(bfloat)
    part = g10.shape[0]

    def put(place, lane):
        (g10, g11, g12, g13)[place][...] = grad[lane * part : (lane + 1) * part, :]

    by_lane(mine[1], put)
    g2[...] = dot(dzt[...], act_all[...]).astype(bfloat).T

    @pl.when(step == pl.num_programs(0) - 1)
    def _():
        own, rest = picks()
        value = gate[:, 0:1]
        weight = value * (1.0 - value) * jnp.sum(dgate[...], axis=1, keepdims=True)
        m = (weight * (own.astype(single) - rest.astype(single))).astype(bfloat)
        m_out[...] = dot(m, xs[...], TN)
        dx_out[...] = (total[...] + dot(m, router[...])).astype(bfloat)
        z_out[...] = (result[...] * value).astype(bfloat)


def expert(mine, xs, router, other, w1, w2, da, cot, local):
    rows, width = xs.shape
    inner = w1.shape[2]
    experts = router.shape[0]
    block = FF_BLOCK
    whole = lambda shape: pl.BlockSpec(shape, lambda f: (0,) * len(shape))
    return pl.pallas_call(
        expert_kernel,
        grid=(inner // block,),
        in_specs=[
            SMEM,
            whole((rows, width)),
            whole((experts, width)),
            whole((rows, 1)),
            pl.BlockSpec((None, width, block), lambda f: (local, 0, f)),
            pl.BlockSpec((None, block, width), lambda f: (local, f, 0)),
            pl.BlockSpec((rows, block), lambda f: (0, f)),
            whole((rows, width)),
        ],
        out_specs=[
            *[pl.BlockSpec((width // len(MASKS), block), lambda f: (0, f))] * len(MASKS),
            pl.BlockSpec((block, width), lambda f: (f, 0)),
            whole((rows, width)),
            whole((rows, width)),
            whole((experts, width)),
        ],
        out_shape=[
            *[jax.ShapeDtypeStruct((width // len(MASKS), inner), bfloat)] * len(MASKS),
            jax.ShapeDtypeStruct((inner, width), bfloat),
            jax.ShapeDtypeStruct((rows, width), bfloat),
            jax.ShapeDtypeStruct((rows, width), bfloat),
            jax.ShapeDtypeStruct((experts, width), single),
        ],
        scratch_shapes=[
            pltpu.VMEM((rows, width), single),
            pltpu.VMEM((rows, width), single),
            pltpu.VMEM((rows, 128), single),
            pltpu.VMEM((rows, 128), single),
            pltpu.VMEM((rows, block), bfloat),
            pltpu.VMEM((rows, block), bfloat),
            pltpu.VMEM((width, rows), bfloat),
            pltpu.VMEM((width, rows), bfloat),
        ],
        compiler_params=params(60, 1),
        cost_estimate=cost(20 * rows * width * inner, 8 * rows * inner + 8 * width * inner, rows * inner),
        name="expert",
    )(mine, xs, router, other, w1, w2, da, cot)


def tie(*values):
    return lax.optimization_barrier(values)


def swap(value, axis, mask):
    return lax.ppermute(value, axis, [(i, i ^ mask) for i in range(lax.axis_size(axis))])


def per_device(
    hidden_in,
    norm1_gain,
    w_query,
    w_key,
    w_value,
    w_out,
    rel_bias,
    norm2_gain,
    w_router,
    w_first,
    w_second,
    routes,
    priority,
    segments,
    grad_out,
):
    lanes = lax.axis_size("head")
    blocks = lax.axis_size("seq")
    lane = lax.axis_index("head")
    place = lax.axis_index("seq")
    rows, width = hidden_in.shape[2:]
    x = hidden_in.reshape(rows, width)
    total = rows * lanes
    part = width // lanes
    heads = part // HEAD_DIM
    cotangent = grad_out.reshape(rows, width)
    experts = w_router.shape[1]
    local = w_first.shape[0]
    slot_rows = max(2, 4 * rows // experts)
    slots = blocks * slot_rows
    capacity = 5 * rows * lanes // (2 * local)

    far = swap(x, "head", 2)
    near = swap(x, "head", 1)
    order = jnp.stack([lane, lane ^ 2, lane ^ 1, lane ^ 3]).astype(jnp.int32)
    at = lambda value, mask: lax.dynamic_index_in_dim(value, lane ^ mask, 0, keepdims=False)

    def trade(value):
        return [value[0]] + [swap(value[place], "head", MASKS[place]) for place in range(1, lanes)]

    route_t = routes.reshape(rows, -1).T
    top_count = route_t.shape[0]
    pair_routes = route_t.reshape(-1)
    pair_prio = priority.reshape(rows, -1).T.reshape(-1)
    expert_ids = jnp.arange(experts, dtype=jnp.int32)
    pair_hot = (expert_ids[:, None] == pair_routes[None, :]).astype(jnp.int32)
    earlier = (pair_routes[:, None] == pair_routes[None, :]) & (pair_prio[:, None] < pair_prio[None, :])
    local_rank = jnp.sum(earlier.astype(jnp.int32), axis=0)
    code = (pair_routes % local) * slots + (pair_routes // local) * slot_rows + local_rank
    code_t = code.reshape(top_count, rows)
    code = code_t.T
    third, half = slot_rows * 3 // 10, slot_rows // 2
    second = slot_rows - third
    counts = (third, second - third, third + half, slot_rows - half)
    held = ((0, 0, third, 0, 0), (0, third, second, 1, 0), (0, second, slot_rows, 2, 0), (1, 0, half, 2, third))
    send_place = jnp.zeros_like(local_rank)
    for owner, lowest, highest, number, skip in held + ((1, half, slot_rows, 3, 0),):
        inside = (pair_routes % local == owner) & (local_rank >= lowest) & (local_rank < highest)
        row = blocks * sum(counts[:number]) + (pair_routes // local) * counts[number] + skip
        send_place = send_place + jnp.where(inside, row + local_rank - lowest, 0)
    send_place = send_place.reshape(top_count, rows)

    def exchange(value):
        return lax.all_to_all(
            value.reshape(blocks, slot_rows, -1), "seq", split_axis=0, concat_axis=0, tiled=True
        ).reshape(slots, -1)


    block_rank = (jnp.min(pair_prio) // (top_count * rows)).reshape(1)
    tally = jnp.concatenate([jnp.sum(pair_hot, axis=1), block_rank, jnp.zeros((part - experts - 1,), jnp.int32)])
    gains = jnp.stack([norm1_gain, norm2_gain, tally.astype(bfloat)])
    gains = jnp.concatenate([gains, jnp.zeros((GAINS - 3, part), bfloat)], axis=0)
    hot, allowed = lane_tables()
    table = rel_bias.reshape(heads, BUCKETS)
    vecs = dot(table, jnp.asarray(hot.T, bfloat)).reshape(heads, CHUNKS, 2 * QB)
    vecs = jnp.where(jnp.asarray(allowed)[None], vecs, MASKED)
    vecs = jnp.concatenate([vecs, jnp.zeros((heads, 8 - CHUNKS, 2 * QB), single)], axis=1)
    base = place * total
    own = lax.dynamic_slice_in_dim(segments, base, total, 0)
    low = jnp.zeros_like(own)
    for number in range(1, 4):
        low = jnp.where(own == number, jnp.sum((segments < number).astype(jnp.int32)), low)
    low = low - base + WINDOW
    need = (jnp.max(low.reshape(-1, QB), axis=1) > jnp.arange(total // QB) * QB).astype(jnp.int32)
    low = low.reshape(1, total)
    packed = trade(pack(order, w_query, w_key, w_value, w_router.T, gains))
    cot_parts = send_rows(send_place, cotangent, blocks, counts)
    spread_out = lambda value: lax.all_to_all(value, "seq", split_axis=0, concat_axis=0, tiled=True)
    cots = [spread_out(cot_parts[0])]
    far, near, packed, cots, cot_parts, low, need, vecs, code = tie(
        far, near, packed, cots, cot_parts, low, need, vecs, code
    )
    both = swap(far, "head", 1)
    cots.append(spread_out(cot_parts[1]))
    both, w_second, w_out = tie(both, w_second, w_out)

    out_far = swap(w_out, "head", 2)
    out_near = swap(w_out, "head", 1)
    second_full = lax.all_gather(w_second, "head", axis=1, tiled=True)

    normed, qt, kv, kv_last, w_rows, router_t, gains = project(order, (x, far, near, both), packed, heads, experts)
    w_rows_full = lax.all_gather(w_rows, "head", axis=0, tiled=True)
    gain_one, gain_two = gains[0:1], gains[1:2]
    kvp = lax.ppermute(kv_last, "seq", [(i, i + 1) for i in range(blocks - 1)])
    early = WINDOW // QB
    later = total // QB - early
    *ot, lse_later = attention_forward(early, later, order, need, low, qt, None, kv, vecs, lanes)
    ot, kvp, cots[1], cot_parts[2] = tie(ot, kvp, cots[1], cot_parts[2])
    cots.append(spread_out(cot_parts[2]))
    *ot, lse_early = attention_forward(0, early, order, need, low, qt, kvp, kv, vecs, lanes, ot)
    ot, out_far, out_near = tie(ot, out_far, out_near)
    w_outs = (w_out, out_far, out_near, swap(out_far, "head", 1))
    ots = trade(ot)
    ots, w_first, cots[2] = tie(ots, w_first, cots[2])
    noted = spread_out(send_noted(cot_parts[3], gains[2:3].astype(bfloat)))
    first_full = lax.all_gather(w_first, "head", axis=1, tiled=True)

    y, *sends = middle(ots, w_outs, x, gain_two, code_t, slots)
    sends[0], noted = tie(sends[0], noted)

    tallies = noted[:, 0, :].reshape(blocks * lanes, part).astype(jnp.int32)
    ahead = (tallies[:, experts : experts + 1] < block_rank[None, :]).astype(jnp.int32)
    offsets = jnp.sum(tallies[:, :experts] * ahead, axis=0)
    kept = (jnp.sum(pair_hot * offsets[:, None], axis=0) + local_rank < capacity).reshape(top_count, rows)
    slot_ids = jnp.arange(local * slots, dtype=jnp.int32)[:, None]
    other = jnp.sum(
        jnp.where(slot_ids == code_t[0:1], jnp.where(kept[0:1], route_t[1:2] + 1, 0), 0)
        + jnp.where(slot_ids == code_t[1:2], jnp.where(kept[1:2], route_t[0:1] + 1, 0), 0),
        axis=1,
    )
    cot_slots = [[cots[0], cots[1], cots[2][:, :third]], [cots[2][:, third:], noted[:, NOTES:, :]]]
    cot_slots = [jnp.concatenate(value, axis=1).reshape(slots, width) for value in cot_slots]
    backs = [dot(cot_slots[0], second_full[0], NT).astype(bfloat)]
    other, backs[0] = tie(other, backs[0])
    other = other.reshape(local, blocks, slot_rows)
    far_others = [
        swap(lax.dynamic_index_in_dim(other, place ^ mask, 1, keepdims=False), "seq", mask) for mask in range(1, blocks)
    ]
    mine = jnp.stack([place * local, lane]).astype(jnp.int32)
    backs.append(dot(cot_slots[1], second_full[1], NT).astype(bfloat))
    received = [exchange(sends[0])]
    sends[1], far_others, *backs = tie(sends[1], far_others, *backs)
    received.append(exchange(sends[1]))
    far_others = jnp.concatenate([lax.dynamic_index_in_dim(other, place, 1, keepdims=False)[None], jnp.stack(far_others)])
    other = jnp.stack(
        [lax.dynamic_index_in_dim(far_others, place ^ number, 0, keepdims=False) for number in range(blocks)], axis=1
    ).reshape(local, slots, 1)

    def run_expert(number):
        return expert(
            mine + jnp.asarray([number, 0], jnp.int32),
            received[number],
            router_t,
            other[number],
            first_full,
            second_full,
            backs[number],
            cot_slots[number],
            number,
        )

    received[1], w_rows_full, (*first_parts0, second0, dx0, z0, router0) = tie(
        received[1], w_rows_full, run_expert(0)
    )
    returns = [exchange(dx0)]
    second0 = lax.psum_scatter(second0, "head", scatter_dimension=0, tiled=True)
    returns[0], second0, (*first_parts1, second1, dx1, z1, router1) = tie(returns[0], second0, run_expert(1))
    def near_parts(parts):
        return swap(parts[3], "head", 1), swap(parts[2], "head", 1)

    def add(one, two, kind=single):
        return (one.astype(single) + two.astype(single)).astype(kind)

    def scatter(value):
        return lax.psum_scatter(value, "head", scatter_dimension=0, tiled=True)

    cross0, direct0 = near_parts(first_parts0)
    returns.append(exchange(dx1))
    across0 = swap(add(first_parts0[1], cross0, bfloat), "head", 2)
    cross1, direct1 = near_parts(first_parts1)
    second1 = scatter(second1)

    returns[1], across0 = tie(returns[1], across0)
    first0 = add(add(first_parts0[0], direct0), across0)
    dy, gain_terms, *douts = return_rows(
        returns[0], returns[1], code, y, gain_two, cotangent, w_outs, ots
    )
    douts, outw = trade(douts[:lanes]), douts[lanes:]
    outw_cross, outw_direct = near_parts(outw)
    dy, z0 = tie(dy, z0)
    z_back = [exchange(z0)]
    douts, outw_cross, outw_direct, cross1, direct1 = tie(douts, outw_cross, outw_direct, cross1, direct1)

    def sum_blocks(value):
        count, last = value.shape[1:]
        value = value.reshape(lanes * blocks, count // blocks, last)
        value = lax.all_to_all(value, ("head", "seq"), split_axis=0, concat_axis=0, tiled=True)
        return jnp.sum(value.reshape(lanes, blocks, -1, last).astype(single), axis=1).astype(bfloat)

    dq_early, behind, dkvt_early, ds_early = attention_backward(
        0, early, (0, heads), order, need, low, qt, kvp, kv, vecs, lse_early, douts
    )
    behind = lax.ppermute(behind, "seq", [(i + 1, i) for i in range(blocks - 1)])
    dq_early, second1 = tie(dq_early, second1)
    outw_across = swap(add(outw[1], outw_cross, bfloat), "head", 2)
    hops = [1 << bit for bit in range(blocks.bit_length() - 1)]

    def hop(value, masks):
        for mask in masks:
            value = add(value, swap(value, "seq", mask), bfloat)
        return value

    cut = heads - 1

    def later_part(span):
        return attention_backward(
            early, later, span, order, need, low, qt, None, kv, vecs, lse_later, douts, (dkvt_early, ds_early)
        )

    dq_last, dkv_last, sums_last = later_part((cut, heads - cut))
    dkv_last, z_back[0], z1, behind, outw_across, cross1 = tie(
        dkv_last, z_back[0], z1, behind, outw_across, cross1
    )
    across1 = swap(add(first_parts1[1], cross1, bfloat), "head", 2)
    grad_outw = add(add(outw[0], outw_direct), outw_across, bfloat)
    grad_outw = hop(grad_outw, hops[:-2])
    z_back.append(exchange(z1))
    ds_early, dkv_last = tie(ds_early, dkv_last)
    dq_first, dkv_first, sums_first = later_part((0, cut))
    dq_first, grad_outw, across1 = tie(dq_first, grad_outw, across1)
    grad_outw = hop(grad_outw, hops[-2:-1])
    *parts, grad_part = settle(
        order,
        dq_early,
        ((dq_first, dkv_first), (dq_last, dkv_last)),
        behind,
        normed,
        (sums_first, sums_last),
        jnp.asarray(hot, single),
        gain_terms,
        (router0, router1),
        max(16, blocks),
    )
    pieces = trade(parts)
    first1 = add(add(first_parts1[0], direct1), across1)
    grad_part, z_back[1] = tie(grad_part, z_back[1])
    value = sum_blocks(grad_part)
    output = finish(z_back[0], z_back[1], code, y).reshape(hidden_in.shape)
    value, grad_outw, pieces[1], pieces[2], output = tie(value, grad_outw, pieces[1], pieces[2], output)
    grad_outw = hop(grad_outw, hops[-1:])
    count = value.shape[1]
    value = lax.all_to_all(
        jnp.broadcast_to(value[None], (blocks,) + value.shape), "seq", split_axis=0, concat_axis=0, tiled=True
    )
    grad_hidden = tail(order, pieces, w_rows_full, x, gain_one, dy).reshape(hidden_in.shape)
    value, grad_hidden = tie(value, grad_hidden)
    if count % 16:
        value = value.transpose(1, 0, 2, 3).reshape(1, lanes, -1, part)
    *grads, grad_router, grad_norm2, rels, grad_norm1 = unpack(value, w_query, w_key, w_value, norm1_gain.reshape(part, 1), experts)
    grad_rel = lax.dynamic_index_in_dim(rels, lane, 0, keepdims=False)[: heads * BUCKETS]
    return (
        output,
        grad_hidden,
        grad_norm1.reshape(part),
        grads[0],
        grads[1],
        grads[2],
        grad_outw.astype(single),
        grad_rel,
        grad_norm2.reshape(part),
        grad_router,
        jnp.stack([first0, first1]),
        jnp.stack([second0, second1]).astype(single),
    )


def solution(mesh):
    return jax.shard_map(
        per_device,
        mesh=mesh,
        in_specs=(
            P("seq", "head", None, None),
            P("head"),
            P("head", None),
            P("head", None),
            P("head", None),
            P("head", None),
            P("head"),
            P("head"),
            P("head", None),
            P("seq", "head", None),
            P("seq", "head", None),
            P("seq", "head", None, None),
            P("seq", "head", None, None),
            P(),
            P("seq", "head", None, None),
        ),
        out_specs=(
            P("seq", "head", None, None),
            P("seq", "head", None, None),
            P("head"),
            P("head", None),
            P("head", None),
            P("head", None),
            P("head", None),
            P("head"),
            P("head"),
            P("head", None),
            P("seq", "head", None),
            P("seq", "head", None),
        ),
        check_vma=False,
    )
```

```python
import functools

import jax
import jax.numpy as jnp
import numpy as np
from jax import lax
from jax.experimental import pallas as pl
from jax.experimental.pallas import tpu as pltpu
from jax.sharding import PartitionSpec as P

HEAD_DIM = 64
WINDOW = 1024
BUCKETS = 32
QB = 256
CHUNKS = WINDOW // QB + 1
KEYS = CHUNKS * QB
MASKED = -1e30
epsilon = 1e-06
bfloat = jnp.bfloat16
single = jnp.float32
MIB = 1 << 20

VMEM = pl.BlockSpec(memory_space=pltpu.VMEM)
SMEM = pl.BlockSpec(memory_space=pltpu.SMEM)


def dot(a, b, dims=((1,), (0,))):
    return lax.dot_general(a, b, (dims, ((), ())), preferred_element_type=single)


NN = ((1,), (0,))
NT = ((1,), (1,))
TN = ((0,), (0,))


def params(mib, grid=0):
    extra = {"dimension_semantics": ("arbitrary",) * grid} if grid else {}
    return pltpu.CompilerParams(vmem_limit_bytes=mib * MIB, **extra)


def full(shape):
    return pl.BlockSpec(tuple(shape), lambda i: (0,) * len(shape))


def once(kernel, name, inputs, outputs, scratch=()):
    found = pl.pallas_call(
        kernel,
        grid=(1,),
        in_specs=[SMEM if value.ndim == 1 else full(value.shape) for value in inputs],
        out_specs=[full(shape) for shape, _ in outputs],
        out_shape=[jax.ShapeDtypeStruct(shape, kind) for shape, kind in outputs],
        scratch_shapes=list(scratch),
        compiler_params=params(60, 1),
        cost_estimate=light(),
        name=name,
    )(*inputs)
    return found


def cost(flops, moved, trans=0):
    return pl.CostEstimate(flops=int(flops), bytes_accessed=int(moved), transcendentals=int(trans))


def light():
    return cost(1000, 1000)


MASKS = (0, 2, 1, 3)


def by_lane(own, action):
    for lane in range(len(MASKS)):

        @pl.when(own == lane)
        def _():
            for place, mask in enumerate(MASKS):
                action(place, lane ^ mask)


def bucket_edges(window_len, bucket_count):
    middle = bucket_count // 2
    edge_list = []
    for number in range(1, bucket_count):
        if number < middle:
            edge_list.append(number)
        else:
            edge_list.append(int(middle * (window_len / middle) ** ((number - middle) / middle)))
    return edge_list


def lane_tables():
    lane = np.arange(2 * QB)
    offset = np.where(lane < QB, lane, lane - 2 * QB)
    distance = WINDOW - QB * np.arange(CHUNKS)[:, None] + offset[None, :]
    allowed = (distance >= 0) & (distance < WINDOW)
    bucket = np.zeros(distance.shape, np.int32)
    for edge_value in bucket_edges(WINDOW, BUCKETS):
        bucket = bucket + (distance >= edge_value)
    hot = (bucket.reshape(-1)[:, None] == np.arange(BUCKETS)[None, :]) & allowed.reshape(-1)[:, None]
    return hot, allowed


GAINS = 16


def pack_kernel(order, wq, wk, wv, router_t, gains, *outs):
    part = wq.shape[0]
    experts = router_t.shape[0]

    def put(place, lane):
        for number, weight in enumerate((wq, wk, wv)):
            outs[place][:, number * part : (number + 1) * part] = weight[:, lane * part : (lane + 1) * part]

    by_lane(order[0], put)
    rest = outs[0].shape[1] - 3 * part
    for ref in outs:
        ref[:experts, 3 * part :] = router_t[...]
        ref[experts : experts + GAINS, 3 * part :] = gains[...]
        ref[experts + GAINS :, 3 * part :] = jnp.zeros((part - experts - GAINS, rest), bfloat)


def pack(order, wq, wk, wv, router_t, gains):
    part, width = wq.shape
    return once(pack_kernel, "pack", (order, wq, wk, wv, router_t, gains), [((part, width), bfloat)] * len(MASKS))


def project_kernel(
    order, x0, x1, x2, x3, p0, p1, p2, p3, n_out, qt_out, kv_out, kv_last, rows_out, router_out, gain_out, wq, wk, wv
):
    rows, width = x0.shape
    heads = kv_out.shape[0]
    part = heads * HEAD_DIM
    experts = router_out.shape[0]
    packed = (p0, p1, p2, p3)
    for place, ref in enumerate(packed):
        at = pl.ds(pl.multiple_of(order[place] * part, 64), part)
        for number, weight in enumerate((wq, wk, wv)):
            weight[at, :] = ref[:, number * part : (number + 1) * part]

    def spread(skip, count):
        found = []
        for lane in range(len(packed)):
            piece = None
            for place, ref in enumerate(packed):
                value = ref[skip : skip + count, 3 * part :]
                piece = value if piece is None else jnp.where(order[place] == lane, value, piece)
            found.append(piece)
        return jnp.concatenate(found, axis=1)

    router_out[...] = spread(0, experts)
    gains = spread(experts, GAINS).astype(single)
    gain_out[...] = gains[0:8, :]
    wq_t = wq[...].T
    k_t = wk[...].T
    v_t = wv[...].T
    for head in range(heads):
        at = slice(head * HEAD_DIM, (head + 1) * HEAD_DIM)
        for number, value in enumerate((wq_t, k_t, v_t)):
            begin = (3 * head + number) * HEAD_DIM
            rows_out[begin : begin + HEAD_DIM, :] = value[at, :]
    for place, ref in enumerate((x0, x1, x2, x3)):
        block = order[place]
        values = ref[...].astype(single)
        inverse = lax.rsqrt(jnp.mean(values * values, axis=-1, keepdims=True) + epsilon)
        normed = (values * inverse * gain_out[0:1, :]).astype(bfloat)
        n_out[block] = normed
        at = pl.ds(pl.multiple_of(block * rows, 128), rows)
        qt = dot(wq_t, normed, NT).astype(bfloat)
        qt_out[:, at] = qt * bfloat(HEAD_DIM**-0.5)
        for head in range(heads):
            begin = 3 * head * HEAD_DIM + HEAD_DIM
            kv = dot(normed, rows_out[begin : begin + 2 * HEAD_DIM, :], NT)
            kv_out[head, at, :] = kv.astype(bfloat)
    kv_last[...] = kv_out[:, kv_out.shape[1] - WINDOW :, :]


def project(order, pieces, packed, heads, experts):
    rows, width = pieces[0].shape
    lanes = len(MASKS)
    total = rows * lanes
    part = heads * HEAD_DIM
    return once(
        project_kernel,
        "project",
        (order, *pieces, *packed),
        [
            ((lanes, rows, width), bfloat),
            ((part, total), bfloat),
            ((heads, total, 2 * HEAD_DIM), bfloat),
            ((heads, WINDOW, 2 * HEAD_DIM), bfloat),
            ((3 * part, width), bfloat),
            ((experts, width), bfloat),
            ((8, width), single),
        ],
        [pltpu.VMEM((width, part), bfloat)] * 3,
    )


def eye(size):
    return (
        lax.broadcasted_iota(jnp.int32, (size, size), 0) == lax.broadcasted_iota(jnp.int32, (size, size), 1)
    ).astype(bfloat)


def stage_attention(kvp, kv, vecs, kv_all, kvt_all, bias):
    heads = kv_all.shape[0]
    unit = eye(2 * HEAD_DIM)
    for head in range(heads):
        if kvp is None:
            kv_all[head] = kv[head]
        else:
            kv_all[head, :WINDOW, :] = kvp[head]
            kv_all[head, WINDOW:, :] = kv[head]
        kvt_all[head] = dot(unit, kv_all[head], NT).astype(bfloat)
        for chunk in range(CHUNKS):
            row = jnp.broadcast_to(vecs[head, chunk : chunk + 1, :], (QB, 2 * QB))
            tile = pltpu.roll(row, 0, 1, stride=1, stride_axis=0)
            bias[head, chunk * QB : (chunk + 1) * QB, :] = tile[:, :QB]


def keep_rows(scores, step, low):
    key = lax.broadcasted_iota(jnp.int32, scores.shape, 0) + step * QB
    return jnp.where(key >= low, scores, MASKED)


def query_tile(step, first, pieces):
    found = []
    for half in range(QB // 128):
        piece = (step + first) * (QB // 128) + half
        found.append((piece // pieces, pl.ds(pl.multiple_of((piece % pieces) * 128, 128), 128)))
    return found


def forward_kernel(first, order, need, low, qt, keys_in, vecs, *rest):
    *more, out0, out1, out2, out3, lse, kv_all, kvt_all, bias = rest
    outs = (out0, out1, out2, out3)
    step = pl.program_id(0)
    heads = kv_all.shape[0]
    pieces = out0.shape[1] // 128

    @pl.when(step == 0)
    def _():
        if more:
            stage_attention(more[0], keys_in, vecs, kv_all, kvt_all, bias)
            for ref, begun in zip(outs, more[1:]):
                ref[...] = begun[...]
        else:
            stage_attention(None, keys_in, vecs, kv_all, kvt_all, bias)

    start = pl.multiple_of(step * QB, QB)

    def run(masked):
        found = []
        for head in range(heads):
            keys = kv_all[head, pl.ds(start, KEYS), :]
            query = qt[head * HEAD_DIM : (head + 1) * HEAD_DIM, :]
            query = jnp.concatenate([query, jnp.zeros_like(query)], axis=0)
            scores = dot(keys, query) + bias[head]
            if masked:
                scores = keep_rows(scores, step + first, low[...])
            peak = jnp.max(scores, axis=0, keepdims=True)
            expo = jnp.exp(scores - peak)
            total = jnp.sum(expo, axis=0, keepdims=True)
            values = kvt_all[head, HEAD_DIM:, pl.ds(start, KEYS)]
            mixed = dot(values, expo.astype(bfloat)) * (1.0 / total)
            found.append(mixed.astype(bfloat))
            lse[0, head : head + 1, :] = peak + jnp.log(total)
        whole = jnp.concatenate(found, axis=0)
        for half, (owner, spot) in enumerate(query_tile(step, first, pieces)):
            for mask, ref in zip(MASKS, outs):

                @pl.when(jnp.bitwise_xor(owner, order[0]) == mask)
                def _():
                    ref[:, spot] = whole[:, half * 128 : (half + 1) * 128]

    pl.when(need[step + first] > 0)(lambda: run(True))
    pl.when(need[step + first] <= 0)(lambda: run(False))


def attention_forward(first, steps, order, need, low, qt, kvp, kv, vecs, lanes, begun=None):
    heads, total, packed = kv.shape
    width = heads * HEAD_DIM
    held = KEYS + (steps - 1) * QB
    own = held - (0 if kvp is None else WINDOW)
    more = [] if kvp is None else [kvp, *begun]
    return pl.pallas_call(
        functools.partial(forward_kernel, first),
        grid=(steps,),
        in_specs=[
            SMEM,
            SMEM,
            pl.BlockSpec((1, QB), lambda i: (0, i + first)),
            pl.BlockSpec((width, QB), lambda i: (0, i + first)),
            pl.BlockSpec((heads, own, packed), lambda i: (0, 0, 0)),
            full(vecs.shape),
        ]
        + [full(value.shape) for value in more],
        out_specs=[full((width, total // lanes))] * lanes + [pl.BlockSpec((1, 8, QB), lambda i: (i, 0, 0))],
        out_shape=[jax.ShapeDtypeStruct((width, total // lanes), bfloat)] * lanes
        + [jax.ShapeDtypeStruct((steps, 8, QB), single)],
        scratch_shapes=[
            pltpu.VMEM((heads, held, packed), bfloat),
            pltpu.VMEM((heads, packed, held), bfloat),
            pltpu.VMEM((heads, KEYS, QB), single),
        ],
        compiler_params=params(60, 1),
        cost_estimate=light(),
        name="attend",
    )(order, need, low, qt, kv, vecs, *more)


def diagonal_sums(tile):
    wide = jnp.concatenate([tile, jnp.zeros_like(tile)], axis=1)
    row = lax.broadcasted_iota(jnp.int32, wide.shape, 0)
    bit = 1
    while bit < QB:
        wide = jnp.where((row & bit) != 0, pltpu.roll(wide, 2 * QB - bit, 1), wide)
        bit *= 2
    return jnp.sum(wide, axis=0, keepdims=True)


def backward_kernel(first, ends, order, need, low, qt, keys_in, vecs, lse, d0, d1, d2, d3, *rest):
    if ends:
        dkvt_in, ds_in, dqt, dkvt, sums, kv_all, kvt_all, bias, dout_all, ds_all = rest
        kvp = None
    else:
        kvp, dqt, behind, dkv_own, ds_all, kv_all, kvt_all, bias, dout_all, dkvt = rest
    step = pl.program_id(0)
    heads = kv_all.shape[0]
    rows = d0.shape[1]

    @pl.when(step == 0)
    def _():
        stage_attention(kvp, keys_in, vecs, kv_all, kvt_all, bias)
        for place, ref in enumerate((d0, d1, d2, d3)):
            dout_all[:, pl.ds(pl.multiple_of(order[place] * rows, 128), rows)] = ref[...]
        if ends:
            ds_all[...] = ds_in[...]
            dkvt[:, :, :WINDOW] = dkvt_in[...]
            dkvt[:, :, WINDOW:] = jnp.zeros_like(dkvt[:, :, WINDOW:])
        else:
            ds_all[...] = jnp.zeros_like(ds_all)
            dkvt[...] = jnp.zeros_like(dkvt)

    start = pl.multiple_of(step * QB, QB)

    def run(masked):
        for head in range(heads):
            at = slice(head * HEAD_DIM, (head + 1) * HEAD_DIM)
            keys = kv_all[head, pl.ds(start, KEYS), :]
            query = qt[at, :]
            none = jnp.zeros_like(query)
            scores = dot(keys, jnp.concatenate([query, none], axis=0)) + bias[head]
            if masked:
                scores = keep_rows(scores, step + first, low[...])
            probs = jnp.exp(scores - lse[0, pl.ds(order[4] + head, 1), :])
            dout = dout_all[at, pl.ds(pl.multiple_of((step + first) * QB, QB), QB)]
            dprobs = dot(keys, jnp.concatenate([none, dout], axis=0))
            delta = jnp.sum(probs * dprobs, axis=0, keepdims=True)
            dscores = probs * (dprobs - delta)
            ds_all[head] += dscores
            dscores = dscores.astype(bfloat)
            probs = probs.astype(bfloat)
            window = pl.ds(start, KEYS)
            dqt[at, :] = (dot(kvt_all[head, :HEAD_DIM, window], dscores) * HEAD_DIM**-0.5).astype(bfloat)
            dkvt[head, :HEAD_DIM, window] += dot(query, dscores, NT)
            dkvt[head, HEAD_DIM:, window] += dot(dout, probs, NT)

    pl.when(need[step + first] > 0)(lambda: run(True))
    pl.when(need[step + first] <= 0)(lambda: run(False))

    @pl.when(step == pl.num_programs(0) - 1)
    def _():
        if not ends:
            behind[...] = dkvt[:, :, :WINDOW].astype(bfloat)
            dkv_own[...] = dkvt[:, :, WINDOW:]
        else:
            for head in range(heads):
                for chunk in range(CHUNKS):
                    sums[head, chunk : chunk + 1, :] = diagonal_sums(ds_all[head, chunk * QB : (chunk + 1) * QB, :])


def attention_backward(first, steps, span, order, need, low, qt, kvp, kv, vecs, lse, douts, begun=()):
    total, packed = kv.shape[1:]
    begin, heads = span
    pick = begin // heads
    width = heads * HEAD_DIM
    held = KEYS + (steps - 1) * QB
    ends = kvp is None
    own = held if ends else held - WINDOW
    scores = (heads, KEYS, QB)
    order = jnp.concatenate([order, jnp.full((1,), begin, jnp.int32)])
    kernel = functools.partial(backward_kernel, first, ends)
    specs = [
        SMEM,
        SMEM,
        pl.BlockSpec((1, QB), lambda i: (0, i + first)),
        pl.BlockSpec((width, QB), lambda i: (pick, i + first)),
        pl.BlockSpec((heads, own, packed), lambda i: (pick, 0, 0)),
        pl.BlockSpec((heads,) + vecs.shape[1:], lambda i: (pick, 0, 0)),
        pl.BlockSpec((1, 8, QB), lambda i: (i, 0, 0)),
    ] + [pl.BlockSpec((width, douts[0].shape[1]), lambda i: (pick, 0))] * 4
    inputs = [order, need, low, qt, kv, vecs, lse, *douts]
    out_specs = [pl.BlockSpec((width, QB), lambda i: (0, i))]
    out_shape = [jax.ShapeDtypeStruct((width, steps * QB), bfloat)]
    scratch = [
        pltpu.VMEM((heads, held, packed), bfloat),
        pltpu.VMEM((heads, packed, held), bfloat),
        pltpu.VMEM(scores, single),
        pltpu.VMEM((width, total), bfloat),
    ]
    if ends:
        specs += [
            pl.BlockSpec((heads, packed, WINDOW), lambda i: (pick, 0, 0)),
            pl.BlockSpec(scores, lambda i: (pick, 0, 0)),
        ]
        inputs += list(begun)
        shapes = [((heads, packed, held), single), ((heads, 8, 2 * QB), single)]
        scratch.append(pltpu.VMEM(scores, single))
    else:
        specs.append(full(kvp.shape))
        inputs.append(kvp)
        shapes = [((heads, packed, WINDOW), bfloat), ((heads, packed, held - WINDOW), single), (scores, single)]
        scratch.append(pltpu.VMEM((heads, packed, held), single))
    out_specs += [full(shape) for shape, _ in shapes]
    out_shape += [jax.ShapeDtypeStruct(shape, kind) for shape, kind in shapes]
    return pl.pallas_call(
        kernel,
        grid=(steps,),
        in_specs=specs,
        out_specs=out_specs,
        out_shape=out_shape,
        scratch_shapes=scratch,
        compiler_params=params(60, 1),
        cost_estimate=light(),
        name="attend_back",
    )(*inputs)


def settle_kernel(
    order, dq0, dq1, dq2, dkv1, dkv2, behind, normed, sums1, sums2, hot, gain_terms, router0, router1,
    out0, out1, out2, out3, grad,
):
    heads = behind.shape[0]
    rows = out0.shape[1]
    outs = (out0, out1, out2, out3)
    edge = dkv1.shape[2] - WINDOW
    held = [(dq1, dkv1, sums1, number) for number in range(dkv1.shape[0])]
    held += [(dq2, dkv2, sums2, number) for number in range(dkv2.shape[0])]
    parts = []
    for head, (dq, dkvt, _, number) in enumerate(held):
        at = slice(number * HEAD_DIM, (number + 1) * HEAD_DIM)
        last = dkvt[number, :, edge:] + behind[head].astype(single)
        parts.append(jnp.concatenate([dq0[head * HEAD_DIM : (head + 1) * HEAD_DIM, :], dq[at, :]], axis=1))
        parts.append(jnp.concatenate([dkvt[number, :, :edge], last], axis=1).astype(bfloat))
    whole = jnp.concatenate(parts, axis=0)

    def put(place, lane):
        outs[place][...] = whole[:, lane * rows : (lane + 1) * rows]

    by_lane(order[0], put)
    total = None
    for lane in range(len(outs)):
        term = dot(whole[:, lane * rows : (lane + 1) * rows], normed[lane])
        total = term if total is None else total + term
    total = total.astype(bfloat)
    part = grad.shape[2]
    count = total.shape[0]
    found = []
    for _, _, ref, number in held:
        value = None
        for chunk in range(CHUNKS):
            term = lax.dot_general(
                jnp.broadcast_to(ref[number, chunk : chunk + 1, :], (8, 2 * QB)),
                hot[chunk * 2 * QB : (chunk + 1) * 2 * QB, :],
                (NN, ((), ())),
                precision=lax.Precision.HIGHEST,
                preferred_element_type=single,
            )
            value = term if value is None else value + term
        found.append(value[0:1, :])
    found.append(jnp.zeros((1, part - BUCKETS * heads), single))
    rel = jnp.broadcast_to(jnp.concatenate(found, axis=1), (16, part))
    router = (router0[...] + router1[...]).astype(bfloat)
    for lane in range(len(outs)):
        columns = slice(lane * part, (lane + 1) * part)
        grad[lane, :count, :] = total[:, columns]
        mine = jnp.where(order[0] == lane, 1.0, 0.0)
        grad[lane, count : count + 16, :] = (rel * mine).astype(bfloat)
        terms = jnp.broadcast_to(gain_terms[:, columns], (16, part))
        grad[lane, count + 16 : count + 32, :] = terms.astype(bfloat)
        begin = count + 32 + router.shape[0]
        grad[lane, count + 32 : begin, :] = router[:, columns]
        if begin < grad.shape[1]:
            grad[lane, begin:, :] = jnp.zeros((grad.shape[1] - begin, part), bfloat)


def settle(order, dq0, late, behind, normed, sums, hot, gain_terms, routers, multiple):
    lanes, rows, width = normed.shape
    tall = 3 * width // lanes
    count = tall + 32 + routers[0].shape[0]
    count = -(-count // multiple) * multiple
    (dq1, dkv1), (dq2, dkv2) = late
    return once(
        settle_kernel,
        "settle",
        (order, dq0, dq1, dq2, dkv1, dkv2, behind, normed, *sums, hot, gain_terms, *routers),
        [((tall, rows), bfloat)] * lanes + [((lanes, count, width // lanes), bfloat)],
    )


def middle_kernel(o0, o1, o2, o3, w0, w1, w2, w3, x, gain, code, y_out, send0, send1):
    y = x[...].astype(single)
    for ref, weight in ((o0, w0), (o1, w1), (o2, w2), (o3, w3)):
        y = y + dot(ref[...], weight[...], TN)
    y_out[...] = y
    inverse = lax.rsqrt(jnp.mean(y * y, axis=-1, keepdims=True) + epsilon)
    normed = (y * inverse * gain[...]).astype(bfloat)
    slots = send0.shape[0]
    for number, ref in enumerate((send0, send1)):
        slot = lax.broadcasted_iota(jnp.int32, (slots, y.shape[0]), 0) + number * slots
        pick = ((slot == code[0:1, :]) | (slot == code[1:2, :])).astype(bfloat)
        ref[...] = dot(pick, normed).astype(bfloat)


def middle(ots, w_out, x, gain, code, slots):
    rows, width = x.shape
    return once(
        middle_kernel,
        "middle",
        (*ots, *w_out, x, gain, code),
        [((rows, width), single), ((slots, width), bfloat), ((slots, width), bfloat)],
    )


NOTES = 16


def send_kernel(place, value, *outs):
    begin = 0
    for out in outs:
        count = out.shape[0]
        here = lax.broadcasted_iota(jnp.int32, (count, value.shape[0]), 0) + begin
        pick = ((here == place[0:1, :]) | (here == place[1:2, :])).astype(bfloat)
        out[...] = dot(pick, value[...]).astype(bfloat)
        begin += count


def send_rows(place, value, blocks, counts):
    shapes = [((blocks * count, value.shape[1]), bfloat) for count in counts]
    found = once(send_kernel, "send_rows", (place, value), shapes)
    return [part.reshape(blocks, count, -1) for part, count in zip(found, counts)]


def send_noted_kernel(part, notes, out):
    for block in range(part.shape[0]):
        out[block, NOTES:, :] = part[block]
        out[block, :NOTES, :] = jnp.broadcast_to(notes[...], (NOTES, part.shape[2]))


def send_noted(part, notes):
    blocks, count, width = part.shape
    outputs = [((blocks, count + NOTES, width), bfloat)]
    return once(send_noted_kernel, "send_noted", (part, notes), outputs)[0]


def collect(code, refs):
    total = None
    for number, ref in enumerate(refs):
        slots = ref.shape[0]
        slot = lax.broadcasted_iota(jnp.int32, (code.shape[0], slots), 1) + number * slots
        pick = ((slot == code[:, 0:1]) | (slot == code[:, 1:2])).astype(bfloat)
        part = dot(pick, ref[...])
        total = part if total is None else total + part
    return total


def return_kernel(d0, d1, code, y, gain, cotangent, w0, w1, w2, w3, o0, o1, o2, o3, dy_out, gg_out, *dots):
    dn = collect(code, (d0, d1))
    values = y[...]
    inverse = lax.rsqrt(jnp.mean(values * values, axis=-1, keepdims=True) + epsilon)
    hat = values * inverse
    gg_out[...] = jnp.sum(dn * hat, axis=0, keepdims=True)
    scaled = dn * gain[...]
    dy = cotangent[...].astype(single) + inverse * (scaled - hat * jnp.mean(scaled * hat, axis=-1, keepdims=True))
    dy_out[...] = dy
    low = dy.astype(bfloat)
    for place, (ref, weight) in enumerate(((o0, w0), (o1, w1), (o2, w2), (o3, w3))):
        dots[place][...] = dot(weight[...], low, NT).astype(bfloat)
        dots[place + 4][...] = dot(ref[...], low).astype(bfloat)


def return_rows(d0, d1, code, y, gain, cotangent, w_out, ots):
    rows, width = y.shape
    lanes = len(ots)
    return once(
        return_kernel,
        "return_rows",
        (d0, d1, code, y, gain, cotangent, *w_out, *ots),
        [((rows, width), single), ((1, width), single)]
        + [((width // lanes, rows), bfloat)] * lanes
        + [((width // lanes, width), bfloat)] * lanes,
    )


def finish_kernel(z0, z1, code, y, out):
    out[...] = (y[...] + collect(code, (z0, z1))).astype(bfloat)


def finish(z0, z1, code, y):
    return once(finish_kernel, "finish", (z0, z1, code, y), [(y.shape, bfloat)])[0]


def unpack_kernel(value, wq, wk, wv, gain, q_out, k_out, v_out, router_out, norm_out, rel_out, gain_out):
    blocks, lanes, count, part = value.shape
    heads = part // HEAD_DIM
    mark = 3 * part
    others = None
    for lane in range(lanes):
        rows = jnp.concatenate([value[block, lane] for block in range(blocks)], axis=0)
        whole = rows[:mark, :].astype(single).T
        for head in range(heads):
            at = slice((lane * heads + head) * HEAD_DIM, (lane * heads + head + 1) * HEAD_DIM)
            for number, ref in enumerate((q_out, k_out, v_out)):
                begin = (3 * head + number) * HEAD_DIM
                ref[:, at] = whole[:, begin : begin + HEAD_DIM]
        term = rows[mark : mark + 32 + router_out.shape[1], :].astype(single)
        rel_out[lane : lane + 1, :] = term[0:1, :]
        others = term if others is None else others + term
    norm_out[...] = others[16:17, :]
    router_out[...] = others[32:, :].T
    total = None
    for ref, weight in ((q_out, wq), (k_out, wk), (v_out, wv)):
        term = jnp.sum(ref[...] * weight[...].astype(single), axis=1, keepdims=True)
        total = term if total is None else total + term
    total = jnp.broadcast_to(total / gain[...].astype(single), (part, 128))
    gain_out[...] = total.T[0:1, :]


def unpack(value, wq, wk, wv, gain, experts):
    part, width = wq.shape
    outputs = [((part, width), single)] * 3
    outputs += [((part, experts), single), ((1, part), single), ((value.shape[1], part), single), ((1, part), single)]
    return once(unpack_kernel, "unpack", (value, wq, wk, wv, gain), outputs)


def tail_kernel(order, *refs):
    *pieces, wt, x, gain, dy, out = refs
    dn = None
    for number, ref in enumerate(pieces):
        block = order[number % 4]
        tall = ref.shape[0]
        begin = block * tall
        term = dot(ref[...], wt[pl.ds(pl.multiple_of(begin, 64), tall), :], TN)
        dn = term if dn is None else dn + term
    values = x[...].astype(single)
    inverse = lax.rsqrt(jnp.mean(values * values, axis=-1, keepdims=True) + epsilon)
    hat = values * inverse
    scaled = dn * gain[...]
    out[...] = dy[...] + inverse * (scaled - hat * jnp.mean(scaled * hat, axis=-1, keepdims=True))


def tail(order, pieces, wt, x, gain, dy):
    return once(tail_kernel, "tail", (order, *pieces, wt, x, gain, dy), [(x.shape, single)])[0]


GELU_0 = 0.7978845608028654
GELU_1 = 0.7978845608028654 * 0.044715
FF_BLOCK = 512
ROW_BLOCK = 256


def expert_kernel(
    mine, xs, router, other, w1, da, cot, g10, g11, g12, g13, g2, dx_out, a_out, m_out, total, dgate, gate, act_all, du_all, xst, dzt
):
    step = pl.program_id(0)
    rows = xs.shape[0]
    experts = router.shape[0]

    def picks():
        lane = lax.broadcasted_iota(jnp.int32, (rows, experts), 1)
        return lane == mine[0], lane == other[...] - 1

    @pl.when(step == 0)
    def _():
        logits = dot(xs[...], router[...], NT)
        own, rest = picks()
        margin = jnp.sum(jnp.where(own, logits, 0.0) - jnp.where(rest, logits, 0.0), axis=1, keepdims=True)
        value = 1.0 / (1.0 + jnp.exp(-margin))
        value = jnp.where(other[...] > 0, value, 0.0)
        gate[...] = jnp.broadcast_to(value, gate.shape)
        dgate[...] = jnp.zeros_like(dgate)
        total[...] = jnp.zeros_like(total)
        for begin in range(0, rows, ROW_BLOCK):
            at = slice(begin, begin + ROW_BLOCK)
            xst[:, at] = xs[at, :].T
            dzt[:, at] = (cot[at, :].astype(single) * gate[at, 0:1]).astype(bfloat).T

    for begin in range(0, rows, ROW_BLOCK):
        at = slice(begin, begin + ROW_BLOCK)
        u = dot(xs[at, :], w1[...])
        square = u * u
        tan = jnp.tanh(u * (GELU_0 + GELU_1 * square))
        half = 0.5 + 0.5 * tan
        act = u * half
        slope = half + act * (1.0 - half) * (2.0 * GELU_0 + 6.0 * GELU_1 * square)
        back = da[at, :].astype(single)
        product = act * back
        part = product[:, :128]
        for col in range(128, product.shape[1], 128):
            part = part + product[:, col : col + 128]
        dgate[at, :] += part
        act_all[at, :] = act.astype(bfloat)
        a_out[at, :] = (act * gate[at, 0:1]).astype(bfloat)
        du_all[at, :] = (gate[at, 0:1] * back * slope).astype(bfloat)
    total[...] += dot(du_all[...], w1[...], NT)
    grad = dot(xst[...], du_all[...]).astype(bfloat)
    part = g10.shape[0]

    def put(place, lane):
        (g10, g11, g12, g13)[place][...] = grad[lane * part : (lane + 1) * part, :]

    by_lane(mine[1], put)
    g2[...] = dot(dzt[...], act_all[...]).astype(bfloat).T

    @pl.when(step == pl.num_programs(0) - 1)
    def _():
        own, rest = picks()
        value = gate[:, 0:1]
        weight = value * (1.0 - value) * jnp.sum(dgate[...], axis=1, keepdims=True)
        m = (weight * (own.astype(single) - rest.astype(single))).astype(bfloat)
        m_out[...] = dot(m, xs[...], TN)
        dx_out[...] = (total[...] + dot(m, router[...])).astype(bfloat)


def expert(mine, xs, router, other, w1, da, cot, local):
    rows, width = xs.shape
    inner = w1.shape[2]
    experts = router.shape[0]
    block = FF_BLOCK
    whole = lambda shape: pl.BlockSpec(shape, lambda f: (0,) * len(shape))
    return pl.pallas_call(
        expert_kernel,
        grid=(inner // block,),
        in_specs=[
            SMEM,
            whole((rows, width)),
            whole((experts, width)),
            whole((rows, 1)),
            pl.BlockSpec((None, width, block), lambda f: (local, 0, f)),
            pl.BlockSpec((rows, block), lambda f: (0, f)),
            whole((rows, width)),
        ],
        out_specs=[
            *[pl.BlockSpec((width // len(MASKS), block), lambda f: (0, f))] * len(MASKS),
            pl.BlockSpec((block, width), lambda f: (f, 0)),
            whole((rows, width)),
            pl.BlockSpec((rows, block), lambda f: (0, f)),
            whole((experts, width)),
        ],
        out_shape=[
            *[jax.ShapeDtypeStruct((width // len(MASKS), inner), bfloat)] * len(MASKS),
            jax.ShapeDtypeStruct((inner, width), bfloat),
            jax.ShapeDtypeStruct((rows, width), bfloat),
            jax.ShapeDtypeStruct((rows, inner), bfloat),
            jax.ShapeDtypeStruct((experts, width), single),
        ],
        scratch_shapes=[
            pltpu.VMEM((rows, width), single),
            pltpu.VMEM((rows, 128), single),
            pltpu.VMEM((rows, 128), single),
            pltpu.VMEM((rows, block), bfloat),
            pltpu.VMEM((rows, block), bfloat),
            pltpu.VMEM((width, rows), bfloat),
            pltpu.VMEM((width, rows), bfloat),
        ],
        compiler_params=params(60, 1),
        cost_estimate=cost(20 * rows * width * inner, 8 * rows * inner + 8 * width * inner, rows * inner),
        name="expert",
    )(mine, xs, router, other, w1, da, cot)


def tie(*values):
    return lax.optimization_barrier(values)


def swap(value, axis, mask):
    return lax.ppermute(value, axis, [(i, i ^ mask) for i in range(lax.axis_size(axis))])


def per_device(
    hidden_in,
    norm1_gain,
    w_query,
    w_key,
    w_value,
    w_out,
    rel_bias,
    norm2_gain,
    w_router,
    w_first,
    w_second,
    routes,
    priority,
    segments,
    grad_out,
):
    lanes = lax.axis_size("head")
    blocks = lax.axis_size("seq")
    lane = lax.axis_index("head")
    place = lax.axis_index("seq")
    rows, width = hidden_in.shape[2:]
    x = hidden_in.reshape(rows, width)
    total = rows * lanes
    part = width // lanes
    heads = part // HEAD_DIM
    cotangent = grad_out.reshape(rows, width)
    experts = w_router.shape[1]
    local = w_first.shape[0]
    slot_rows = max(2, 4 * rows // experts)
    slots = blocks * slot_rows
    capacity = 5 * rows * lanes // (2 * local)

    far = swap(x, "head", 2)
    near = swap(x, "head", 1)
    order = jnp.stack([lane, lane ^ 2, lane ^ 1, lane ^ 3]).astype(jnp.int32)
    at = lambda value, mask: lax.dynamic_index_in_dim(value, lane ^ mask, 0, keepdims=False)

    def trade(value):
        return [value[0]] + [swap(value[place], "head", MASKS[place]) for place in range(1, lanes)]

    route_t = routes.reshape(rows, -1).T
    top_count = route_t.shape[0]
    pair_routes = route_t.reshape(-1)
    pair_prio = priority.reshape(rows, -1).T.reshape(-1)
    expert_ids = jnp.arange(experts, dtype=jnp.int32)
    pair_hot = (expert_ids[:, None] == pair_routes[None, :]).astype(jnp.int32)
    earlier = (pair_routes[:, None] == pair_routes[None, :]) & (pair_prio[:, None] < pair_prio[None, :])
    local_rank = jnp.sum(earlier.astype(jnp.int32), axis=0)
    code = (pair_routes % local) * slots + (pair_routes // local) * slot_rows + local_rank
    code_t = code.reshape(top_count, rows)
    code = code_t.T
    one, two, three = slot_rows * 3 // 10, slot_rows * 7 // 10, slot_rows // 2
    counts = (one, two - one, slot_rows - two + three, slot_rows - three)
    held = ((0, 0, one, 0, 0), (0, one, two, 1, 0), (0, two, slot_rows, 2, 0), (1, 0, three, 2, slot_rows - two))
    send_place = jnp.zeros_like(local_rank)
    for owner, lowest, highest, number, skip in held + ((1, three, slot_rows, 3, 0),):
        inside = (pair_routes % local == owner) & (local_rank >= lowest) & (local_rank < highest)
        row = blocks * sum(counts[:number]) + (pair_routes // local) * counts[number] + skip
        send_place = send_place + jnp.where(inside, row + local_rank - lowest, 0)
    send_place = send_place.reshape(top_count, rows)

    def exchange(value):
        return lax.all_to_all(
            value.reshape(blocks, slot_rows, -1), "seq", split_axis=0, concat_axis=0, tiled=True
        ).reshape(slots, -1)


    block_rank = (jnp.min(pair_prio) // (top_count * rows)).reshape(1)
    tally = jnp.concatenate([jnp.sum(pair_hot, axis=1), block_rank, jnp.zeros((part - experts - 1,), jnp.int32)])
    gains = jnp.stack([norm1_gain, norm2_gain, tally.astype(bfloat)])
    gains = jnp.concatenate([gains, jnp.zeros((GAINS - 3, part), bfloat)], axis=0)
    hot, allowed = lane_tables()
    table = rel_bias.reshape(heads, BUCKETS)
    vecs = dot(table, jnp.asarray(hot.T, bfloat)).reshape(heads, CHUNKS, 2 * QB)
    vecs = jnp.where(jnp.asarray(allowed)[None], vecs, MASKED)
    vecs = jnp.concatenate([vecs, jnp.zeros((heads, 8 - CHUNKS, 2 * QB), single)], axis=1)
    base = place * total
    own = lax.dynamic_slice_in_dim(segments, base, total, 0)
    low = jnp.zeros_like(own)
    for number in range(1, 4):
        low = jnp.where(own == number, jnp.sum((segments < number).astype(jnp.int32)), low)
    low = low - base + WINDOW
    need = (jnp.max(low.reshape(-1, QB), axis=1) > jnp.arange(total // QB) * QB).astype(jnp.int32)
    low = low.reshape(1, total)
    packed = trade(pack(order, w_query, w_key, w_value, w_router.T, gains))
    cot_parts = send_rows(send_place, cotangent, blocks, counts)
    spread_out = lambda value: lax.all_to_all(value, "seq", split_axis=0, concat_axis=0, tiled=True)
    cots = [spread_out(cot_parts[0])]
    far, near, packed, cots, cot_parts, low, need, vecs, code = tie(
        far, near, packed, cots, cot_parts, low, need, vecs, code
    )
    both = swap(far, "head", 1)
    cots.append(spread_out(cot_parts[1]))
    both, w_second, w_out = tie(both, w_second, w_out)

    out_far = swap(w_out, "head", 2)
    out_near = swap(w_out, "head", 1)
    second_full = lax.all_gather(w_second, "head", axis=1, tiled=True)

    normed, qt, kv, kv_last, w_rows, router_t, gains = project(order, (x, far, near, both), packed, heads, experts)
    w_rows_full = lax.all_gather(w_rows, "head", axis=0, tiled=True)
    gain_one, gain_two = gains[0:1], gains[1:2]
    kvp = lax.ppermute(kv_last, "seq", [(i, i + 1) for i in range(blocks - 1)])
    early = WINDOW // QB
    later = total // QB - early
    *ot, lse_later = attention_forward(early, later, order, need, low, qt, None, kv, vecs, lanes)
    ot, kvp, cots[1], cot_parts[2] = tie(ot, kvp, cots[1], cot_parts[2])
    cots.append(spread_out(cot_parts[2]))
    *ot, lse_early = attention_forward(0, early, order, need, low, qt, kvp, kv, vecs, lanes, ot)
    ot, out_far, out_near = tie(ot, out_far, out_near)
    w_outs = (w_out, out_far, out_near, swap(out_far, "head", 1))
    ots = trade(ot)
    ots, w_first, cots[2] = tie(ots, w_first, cots[2])
    noted = spread_out(send_noted(cot_parts[3], gains[2:3].astype(bfloat)))
    first_full = lax.all_gather(w_first, "head", axis=1, tiled=True)

    y, *sends = middle(ots, w_outs, x, gain_two, code_t, slots)
    sends[0], noted = tie(sends[0], noted)

    tallies = noted[:, 0, :].reshape(blocks * lanes, part).astype(jnp.int32)
    ahead = (tallies[:, experts : experts + 1] < block_rank[None, :]).astype(jnp.int32)
    offsets = jnp.sum(tallies[:, :experts] * ahead, axis=0)
    kept = (jnp.sum(pair_hot * offsets[:, None], axis=0) + local_rank < capacity).reshape(top_count, rows)
    slot_ids = jnp.arange(local * slots, dtype=jnp.int32)[:, None]
    other = jnp.sum(
        jnp.where(slot_ids == code_t[0:1], jnp.where(kept[0:1], route_t[1:2] + 1, 0), 0)
        + jnp.where(slot_ids == code_t[1:2], jnp.where(kept[1:2], route_t[0:1] + 1, 0), 0),
        axis=1,
    )
    last = slot_rows - two
    cot_slots = [[cots[0], cots[1], cots[2][:, :last]], [cots[2][:, last:], noted[:, NOTES:, :]]]
    cot_slots = [jnp.concatenate(value, axis=1).reshape(slots, width) for value in cot_slots]
    backs = [dot(cot_slots[0], second_full[0], NT).astype(bfloat)]
    other, backs[0] = tie(other, backs[0])
    other = other.reshape(local, blocks, slot_rows)
    far_others = [
        swap(lax.dynamic_index_in_dim(other, place ^ mask, 1, keepdims=False), "seq", mask) for mask in range(1, blocks)
    ]
    mine = jnp.stack([place * local, lane]).astype(jnp.int32)
    backs.append(dot(cot_slots[1], second_full[1], NT).astype(bfloat))
    received = [exchange(sends[0])]
    sends[1], far_others, *backs = tie(sends[1], far_others, *backs)
    received.append(exchange(sends[1]))
    far_others = jnp.concatenate([lax.dynamic_index_in_dim(other, place, 1, keepdims=False)[None], jnp.stack(far_others)])
    other = jnp.stack(
        [lax.dynamic_index_in_dim(far_others, place ^ number, 0, keepdims=False) for number in range(blocks)], axis=1
    ).reshape(local, slots, 1)

    def run_expert(number):
        return expert(
            mine + jnp.asarray([number, 0], jnp.int32),
            received[number],
            router_t,
            other[number],
            first_full,
            backs[number],
            cot_slots[number],
            number,
        )

    received[1], w_rows_full, (*first_parts0, second0, dx0, act0, router0) = tie(
        received[1], w_rows_full, run_expert(0)
    )
    returns = [exchange(dx0)]
    second0 = lax.psum_scatter(second0, "head", scatter_dimension=0, tiled=True)
    returns[0], second0, (*first_parts1, second1, dx1, act1, router1) = tie(returns[0], second0, run_expert(1))
    def near_parts(parts):
        return swap(parts[3], "head", 1), swap(parts[2], "head", 1)

    def add(one, two, kind=single):
        return (one.astype(single) + two.astype(single)).astype(kind)

    def scatter(value):
        return lax.psum_scatter(value, "head", scatter_dimension=0, tiled=True)

    cross0, direct0 = near_parts(first_parts0)
    returns.append(exchange(dx1))
    away0, act0, act1 = tie(add(first_parts0[1], cross0, bfloat), act0, act1)
    across0 = swap(away0, "head", 2)
    cross1, direct1 = near_parts(first_parts1)
    second1 = scatter(second1)

    z0, z1 = (dot(act, second_full[i]).astype(bfloat) for i, act in enumerate((act0, act1)))
    returns[1], across0, z0, z1 = tie(returns[1], across0, z0, z1)
    first0 = add(add(first_parts0[0], direct0), across0)
    dy, gain_terms, *douts = return_rows(
        returns[0], returns[1], code, y, gain_two, cotangent, w_outs, ots
    )
    douts, outw = trade(douts[:lanes]), douts[lanes:]
    outw_cross, outw_direct = near_parts(outw)
    dy, z0 = tie(dy, z0)
    z_back = [exchange(z0)]
    douts, outw_cross, outw_direct, cross1, direct1 = tie(douts, outw_cross, outw_direct, cross1, direct1)

    def sum_blocks(value):
        count, last = value.shape[1:]
        value = value.reshape(lanes * blocks, count // blocks, last)
        value = lax.all_to_all(value, ("head", "seq"), split_axis=0, concat_axis=0, tiled=True)
        return jnp.sum(value.reshape(lanes, blocks, -1, last).astype(single), axis=1).astype(bfloat)

    dq_early, behind, dkvt_early, ds_early = attention_backward(
        0, early, (0, heads), order, need, low, qt, kvp, kv, vecs, lse_early, douts
    )
    behind = lax.ppermute(behind, "seq", [(i + 1, i) for i in range(blocks - 1)])
    dq_early, second1 = tie(dq_early, second1)
    outw_across = swap(add(outw[1], outw_cross, bfloat), "head", 2)
    hops = [1 << bit for bit in range(blocks.bit_length() - 1)]

    def hop(value, masks):
        for mask in masks:
            value = add(value, swap(value, "seq", mask), bfloat)
        return value

    cut = heads - 1

    def later_part(span):
        return attention_backward(
            early, later, span, order, need, low, qt, None, kv, vecs, lse_later, douts, (dkvt_early, ds_early)
        )

    dq_last, dkv_last, sums_last = later_part((cut, heads - cut))
    dkv_last, z_back[0], z1, behind, outw_across, cross1 = tie(
        dkv_last, z_back[0], z1, behind, outw_across, cross1
    )
    across1 = swap(add(first_parts1[1], cross1, bfloat), "head", 2)
    grad_outw = add(add(outw[0], outw_direct), outw_across, bfloat)
    grad_outw = hop(grad_outw, hops[:-2])
    z_back.append(exchange(z1))
    ds_early, dkv_last = tie(ds_early, dkv_last)
    dq_first, dkv_first, sums_first = later_part((0, cut))
    dq_first, grad_outw, across1 = tie(dq_first, grad_outw, across1)
    grad_outw = hop(grad_outw, hops[-2:-1])
    *parts, grad_part = settle(
        order,
        dq_early,
        ((dq_first, dkv_first), (dq_last, dkv_last)),
        behind,
        normed,
        (sums_first, sums_last),
        jnp.asarray(hot, single),
        gain_terms,
        (router0, router1),
        max(16, blocks),
    )
    pieces = trade(parts)
    first1 = add(add(first_parts1[0], direct1), across1)
    grad_part, z_back[1] = tie(grad_part, z_back[1])
    value = sum_blocks(grad_part)
    output = finish(z_back[0], z_back[1], code, y).reshape(hidden_in.shape)
    value, grad_outw, pieces[1], pieces[2] = tie(value, grad_outw, pieces[1], pieces[2])
    grad_outw = hop(grad_outw, hops[-1:])
    count = value.shape[1]
    value = lax.all_to_all(
        jnp.broadcast_to(value[None], (blocks,) + value.shape), "seq", split_axis=0, concat_axis=0, tiled=True
    )
    grad_hidden = tail(order, pieces, w_rows_full, x, gain_one, dy).reshape(hidden_in.shape)
    value, grad_hidden, output = tie(value, grad_hidden, output)
    if count % 16:
        value = value.transpose(1, 0, 2, 3).reshape(1, lanes, -1, part)
    *grads, grad_router, grad_norm2, rels, grad_norm1 = unpack(value, w_query, w_key, w_value, norm1_gain.reshape(part, 1), experts)
    grad_rel = lax.dynamic_index_in_dim(rels, lane, 0, keepdims=False)[: heads * BUCKETS]
    return (
        output,
        grad_hidden,
        grad_norm1.reshape(part),
        grads[0],
        grads[1],
        grads[2],
        grad_outw.astype(single),
        grad_rel,
        grad_norm2.reshape(part),
        grad_router,
        jnp.stack([first0, first1]),
        jnp.stack([second0, second1]).astype(single),
    )


def solution(mesh):
    return jax.shard_map(
        per_device,
        mesh=mesh,
        in_specs=(
            P("seq", "head", None, None),
            P("head"),
            P("head", None),
            P("head", None),
            P("head", None),
            P("head", None),
            P("head"),
            P("head"),
            P("head", None),
            P("seq", "head", None),
            P("seq", "head", None),
            P("seq", "head", None, None),
            P("seq", "head", None, None),
            P(),
            P("seq", "head", None, None),
        ),
        out_specs=(
            P("seq", "head", None, None),
            P("seq", "head", None, None),
            P("head"),
            P("head", None),
            P("head", None),
            P("head", None),
            P("head", None),
            P("head"),
            P("head"),
            P("head", None),
            P("seq", "head", None),
            P("seq", "head", None),
        ),
        check_vma=False,
    )
```

```python
import functools

import jax
import jax.numpy as jnp
import numpy as np
from jax import lax
from jax.experimental import pallas as pl
from jax.experimental.pallas import tpu as pltpu
from jax.sharding import PartitionSpec as P

HEAD_DIM = 64
WINDOW = 1024
BUCKETS = 32
QB = 256
CHUNKS = WINDOW // QB + 1
KEYS = CHUNKS * QB
MASKED = -1e30
epsilon = 1e-06
bfloat = jnp.bfloat16
single = jnp.float32
MIB = 1 << 20

VMEM = pl.BlockSpec(memory_space=pltpu.VMEM)
SMEM = pl.BlockSpec(memory_space=pltpu.SMEM)


def dot(a, b, dims=((1,), (0,))):
    return lax.dot_general(a, b, (dims, ((), ())), preferred_element_type=single)


NN = ((1,), (0,))
NT = ((1,), (1,))
TN = ((0,), (0,))


def params(mib, grid=0):
    extra = {"dimension_semantics": ("arbitrary",) * grid} if grid else {}
    return pltpu.CompilerParams(vmem_limit_bytes=mib * MIB, **extra)


def full(shape):
    return pl.BlockSpec(tuple(shape), lambda i: (0,) * len(shape))


def once(kernel, name, inputs, outputs, scratch=()):
    found = pl.pallas_call(
        kernel,
        grid=(1,),
        in_specs=[SMEM if value.ndim == 1 else full(value.shape) for value in inputs],
        out_specs=[full(shape) for shape, _ in outputs],
        out_shape=[jax.ShapeDtypeStruct(shape, kind) for shape, kind in outputs],
        scratch_shapes=list(scratch),
        compiler_params=params(60, 1),
        cost_estimate=light(),
        name=name,
    )(*inputs)
    return found


def cost(flops, moved, trans=0):
    return pl.CostEstimate(flops=int(flops), bytes_accessed=int(moved), transcendentals=int(trans))


def light():
    return cost(1000, 1000)


MASKS = (0, 2, 1, 3)


def by_lane(own, action):
    for lane in range(len(MASKS)):

        @pl.when(own == lane)
        def _():
            for place, mask in enumerate(MASKS):
                action(place, lane ^ mask)


def bucket_edges(window_len, bucket_count):
    middle = bucket_count // 2
    edge_list = []
    for number in range(1, bucket_count):
        if number < middle:
            edge_list.append(number)
        else:
            edge_list.append(int(middle * (window_len / middle) ** ((number - middle) / middle)))
    return edge_list


def lane_tables():
    lane = np.arange(2 * QB)
    offset = np.where(lane < QB, lane, lane - 2 * QB)
    distance = WINDOW - QB * np.arange(CHUNKS)[:, None] + offset[None, :]
    allowed = (distance >= 0) & (distance < WINDOW)
    bucket = np.zeros(distance.shape, np.int32)
    for edge_value in bucket_edges(WINDOW, BUCKETS):
        bucket = bucket + (distance >= edge_value)
    hot = (bucket.reshape(-1)[:, None] == np.arange(BUCKETS)[None, :]) & allowed.reshape(-1)[:, None]
    return hot, allowed


GAINS = 16


def pack_kernel(order, wq, wk, wv, router_t, gains, *outs):
    part = wq.shape[0]
    experts = router_t.shape[0]

    def put(place, lane):
        for number, weight in enumerate((wq, wk, wv)):
            outs[place][:, number * part : (number + 1) * part] = weight[:, lane * part : (lane + 1) * part]

    by_lane(order[0], put)
    rest = outs[0].shape[1] - 3 * part
    for ref in outs:
        ref[:experts, 3 * part :] = router_t[...]
        ref[experts : experts + GAINS, 3 * part :] = gains[...]
        ref[experts + GAINS :, 3 * part :] = jnp.zeros((part - experts - GAINS, rest), bfloat)


def pack(order, wq, wk, wv, router_t, gains):
    part, width = wq.shape
    return once(pack_kernel, "pack", (order, wq, wk, wv, router_t, gains), [((part, width), bfloat)] * len(MASKS))


def project_kernel(
    order, x0, x1, x2, x3, p0, p1, p2, p3, n_out, qt_out, kv_out, kv_last, rows_out, router_out, gain_out, wq, wk, wv
):
    rows, width = x0.shape
    heads = kv_out.shape[0]
    part = heads * HEAD_DIM
    experts = router_out.shape[0]
    packed = (p0, p1, p2, p3)
    for place, ref in enumerate(packed):
        at = pl.ds(pl.multiple_of(order[place] * part, 64), part)
        for number, weight in enumerate((wq, wk, wv)):
            weight[at, :] = ref[:, number * part : (number + 1) * part]

    def spread(skip, count):
        found = []
        for lane in range(len(packed)):
            piece = None
            for place, ref in enumerate(packed):
                value = ref[skip : skip + count, 3 * part :]
                piece = value if piece is None else jnp.where(order[place] == lane, value, piece)
            found.append(piece)
        return jnp.concatenate(found, axis=1)

    router_out[...] = spread(0, experts)
    gains = spread(experts, GAINS).astype(single)
    gain_out[...] = gains[0:8, :]
    wq_t = wq[...].T
    k_t = wk[...].T
    v_t = wv[...].T
    for head in range(heads):
        at = slice(head * HEAD_DIM, (head + 1) * HEAD_DIM)
        for number, value in enumerate((wq_t, k_t, v_t)):
            begin = (3 * head + number) * HEAD_DIM
            rows_out[begin : begin + HEAD_DIM, :] = value[at, :]
    for place, ref in enumerate((x0, x1, x2, x3)):
        block = order[place]
        values = ref[...].astype(single)
        inverse = lax.rsqrt(jnp.mean(values * values, axis=-1, keepdims=True) + epsilon)
        normed = (values * inverse * gain_out[0:1, :]).astype(bfloat)
        n_out[block] = normed
        at = pl.ds(pl.multiple_of(block * rows, 128), rows)
        qt = dot(wq_t, normed, NT).astype(bfloat)
        qt_out[:, at] = qt * bfloat(HEAD_DIM**-0.5)
        for head in range(heads):
            begin = 3 * head * HEAD_DIM + HEAD_DIM
            kv = dot(normed, rows_out[begin : begin + 2 * HEAD_DIM, :], NT)
            kv_out[head, at, :] = kv.astype(bfloat)
    kv_last[...] = kv_out[:, kv_out.shape[1] - WINDOW :, :]


def project(order, pieces, packed, heads, experts):
    rows, width = pieces[0].shape
    lanes = len(MASKS)
    total = rows * lanes
    part = heads * HEAD_DIM
    return once(
        project_kernel,
        "project",
        (order, *pieces, *packed),
        [
            ((lanes, rows, width), bfloat),
            ((part, total), bfloat),
            ((heads, total, 2 * HEAD_DIM), bfloat),
            ((heads, WINDOW, 2 * HEAD_DIM), bfloat),
            ((3 * part, width), bfloat),
            ((experts, width), bfloat),
            ((8, width), single),
        ],
        [pltpu.VMEM((width, part), bfloat)] * 3,
    )


def eye(size):
    return (
        lax.broadcasted_iota(jnp.int32, (size, size), 0) == lax.broadcasted_iota(jnp.int32, (size, size), 1)
    ).astype(bfloat)


def stage_attention(kvp, kv, vecs, kv_all, kvt_all, bias):
    heads = kv_all.shape[0]
    unit = eye(2 * HEAD_DIM)
    for head in range(heads):
        if kvp is None:
            kv_all[head] = kv[head]
        else:
            kv_all[head, :WINDOW, :] = kvp[head]
            kv_all[head, WINDOW:, :] = kv[head]
        kvt_all[head] = dot(unit, kv_all[head], NT).astype(bfloat)
        for chunk in range(CHUNKS):
            row = jnp.broadcast_to(vecs[head, chunk : chunk + 1, :], (QB, 2 * QB))
            tile = pltpu.roll(row, 0, 1, stride=1, stride_axis=0)
            bias[head, chunk * QB : (chunk + 1) * QB, :] = tile[:, :QB]


def keep_rows(scores, step, low):
    key = lax.broadcasted_iota(jnp.int32, scores.shape, 0) + step * QB
    return jnp.where(key >= low, scores, MASKED)


def query_tile(step, first, pieces):
    found = []
    for half in range(QB // 128):
        piece = (step + first) * (QB // 128) + half
        found.append((piece // pieces, pl.ds(pl.multiple_of((piece % pieces) * 128, 128), 128)))
    return found


def forward_kernel(first, order, need, low, qt, keys_in, vecs, *rest):
    *more, out0, out1, out2, out3, lse, kv_all, kvt_all, bias = rest
    outs = (out0, out1, out2, out3)
    step = pl.program_id(0)
    heads = kv_all.shape[0]
    pieces = out0.shape[1] // 128

    @pl.when(step == 0)
    def _():
        if more:
            stage_attention(more[0], keys_in, vecs, kv_all, kvt_all, bias)
            for ref, begun in zip(outs, more[1:]):
                ref[...] = begun[...]
        else:
            stage_attention(None, keys_in, vecs, kv_all, kvt_all, bias)

    start = pl.multiple_of(step * QB, QB)

    def run(masked):
        found = []
        for head in range(heads):
            keys = kv_all[head, pl.ds(start, KEYS), :]
            query = qt[head * HEAD_DIM : (head + 1) * HEAD_DIM, :]
            query = jnp.concatenate([query, jnp.zeros_like(query)], axis=0)
            scores = dot(keys, query) + bias[head]
            if masked:
                scores = keep_rows(scores, step + first, low[...])
            peak = jnp.max(scores, axis=0, keepdims=True)
            expo = jnp.exp(scores - peak)
            total = jnp.sum(expo, axis=0, keepdims=True)
            values = kvt_all[head, HEAD_DIM:, pl.ds(start, KEYS)]
            mixed = dot(values, expo.astype(bfloat)) * (1.0 / total)
            found.append(mixed.astype(bfloat))
            lse[0, head : head + 1, :] = peak + jnp.log(total)
        whole = jnp.concatenate(found, axis=0)
        for half, (owner, spot) in enumerate(query_tile(step, first, pieces)):
            for mask, ref in zip(MASKS, outs):

                @pl.when(jnp.bitwise_xor(owner, order[0]) == mask)
                def _():
                    ref[:, spot] = whole[:, half * 128 : (half + 1) * 128]

    pl.when(need[step + first] > 0)(lambda: run(True))
    pl.when(need[step + first] <= 0)(lambda: run(False))


def attention_forward(first, steps, order, need, low, qt, kvp, kv, vecs, lanes, begun=None):
    heads, total, packed = kv.shape
    width = heads * HEAD_DIM
    held = KEYS + (steps - 1) * QB
    own = held - (0 if kvp is None else WINDOW)
    more = [] if kvp is None else [kvp, *begun]
    return pl.pallas_call(
        functools.partial(forward_kernel, first),
        grid=(steps,),
        in_specs=[
            SMEM,
            SMEM,
            pl.BlockSpec((1, QB), lambda i: (0, i + first)),
            pl.BlockSpec((width, QB), lambda i: (0, i + first)),
            pl.BlockSpec((heads, own, packed), lambda i: (0, 0, 0)),
            full(vecs.shape),
        ]
        + [full(value.shape) for value in more],
        out_specs=[full((width, total // lanes))] * lanes + [pl.BlockSpec((1, 8, QB), lambda i: (i, 0, 0))],
        out_shape=[jax.ShapeDtypeStruct((width, total // lanes), bfloat)] * lanes
        + [jax.ShapeDtypeStruct((steps, 8, QB), single)],
        scratch_shapes=[
            pltpu.VMEM((heads, held, packed), bfloat),
            pltpu.VMEM((heads, packed, held), bfloat),
            pltpu.VMEM((heads, KEYS, QB), single),
        ],
        compiler_params=params(60, 1),
        cost_estimate=light(),
        name="attend",
    )(order, need, low, qt, kv, vecs, *more)


def diagonal_sums(tile):
    wide = jnp.concatenate([tile, jnp.zeros_like(tile)], axis=1)
    row = lax.broadcasted_iota(jnp.int32, wide.shape, 0)
    bit = 1
    while bit < QB:
        wide = jnp.where((row & bit) != 0, pltpu.roll(wide, 2 * QB - bit, 1), wide)
        bit *= 2
    return jnp.sum(wide, axis=0, keepdims=True)


def backward_kernel(first, ends, order, need, low, qt, keys_in, vecs, lse, d0, d1, d2, d3, *rest):
    if ends:
        dkvt_in, ds_in, dqt, dkvt, sums, kv_all, kvt_all, bias, dout_all, ds_all = rest
        kvp = None
    else:
        kvp, dqt, behind, dkv_own, ds_all, kv_all, kvt_all, bias, dout_all, dkvt = rest
    step = pl.program_id(0)
    heads = kv_all.shape[0]
    rows = d0.shape[1]

    @pl.when(step == 0)
    def _():
        stage_attention(kvp, keys_in, vecs, kv_all, kvt_all, bias)
        for place, ref in enumerate((d0, d1, d2, d3)):
            dout_all[:, pl.ds(pl.multiple_of(order[place] * rows, 128), rows)] = ref[...]
        if ends:
            ds_all[...] = ds_in[...]
            dkvt[:, :, :WINDOW] = dkvt_in[...]
            dkvt[:, :, WINDOW:] = jnp.zeros_like(dkvt[:, :, WINDOW:])
        else:
            ds_all[...] = jnp.zeros_like(ds_all)
            dkvt[...] = jnp.zeros_like(dkvt)

    start = pl.multiple_of(step * QB, QB)

    def run(masked):
        for head in range(heads):
            at = slice(head * HEAD_DIM, (head + 1) * HEAD_DIM)
            keys = kv_all[head, pl.ds(start, KEYS), :]
            query = qt[at, :]
            none = jnp.zeros_like(query)
            scores = dot(keys, jnp.concatenate([query, none], axis=0)) + bias[head]
            if masked:
                scores = keep_rows(scores, step + first, low[...])
            probs = jnp.exp(scores - lse[0, pl.ds(order[4] + head, 1), :])
            dout = dout_all[at, pl.ds(pl.multiple_of((step + first) * QB, QB), QB)]
            dprobs = dot(keys, jnp.concatenate([none, dout], axis=0))
            delta = jnp.sum(probs * dprobs, axis=0, keepdims=True)
            dscores = probs * (dprobs - delta)
            ds_all[head] += dscores
            dscores = dscores.astype(bfloat)
            probs = probs.astype(bfloat)
            window = pl.ds(start, KEYS)
            dqt[at, :] = (dot(kvt_all[head, :HEAD_DIM, window], dscores) * HEAD_DIM**-0.5).astype(bfloat)
            dkvt[head, :HEAD_DIM, window] += dot(query, dscores, NT)
            dkvt[head, HEAD_DIM:, window] += dot(dout, probs, NT)

    pl.when(need[step + first] > 0)(lambda: run(True))
    pl.when(need[step + first] <= 0)(lambda: run(False))

    @pl.when(step == pl.num_programs(0) - 1)
    def _():
        if not ends:
            behind[...] = dkvt[:, :, :WINDOW].astype(bfloat)
            dkv_own[...] = dkvt[:, :, WINDOW:]
        else:
            for head in range(heads):
                for chunk in range(CHUNKS):
                    sums[head, chunk : chunk + 1, :] = diagonal_sums(ds_all[head, chunk * QB : (chunk + 1) * QB, :])


def attention_backward(first, steps, span, order, need, low, qt, kvp, kv, vecs, lse, douts, begun=()):
    total, packed = kv.shape[1:]
    begin, heads = span
    pick = begin // heads
    width = heads * HEAD_DIM
    held = KEYS + (steps - 1) * QB
    ends = kvp is None
    own = held if ends else held - WINDOW
    scores = (heads, KEYS, QB)
    order = jnp.concatenate([order, jnp.full((1,), begin, jnp.int32)])
    kernel = functools.partial(backward_kernel, first, ends)
    specs = [
        SMEM,
        SMEM,
        pl.BlockSpec((1, QB), lambda i: (0, i + first)),
        pl.BlockSpec((width, QB), lambda i: (pick, i + first)),
        pl.BlockSpec((heads, own, packed), lambda i: (pick, 0, 0)),
        pl.BlockSpec((heads,) + vecs.shape[1:], lambda i: (pick, 0, 0)),
        pl.BlockSpec((1, 8, QB), lambda i: (i, 0, 0)),
    ] + [pl.BlockSpec((width, douts[0].shape[1]), lambda i: (pick, 0))] * 4
    inputs = [order, need, low, qt, kv, vecs, lse, *douts]
    out_specs = [pl.BlockSpec((width, QB), lambda i: (0, i))]
    out_shape = [jax.ShapeDtypeStruct((width, steps * QB), bfloat)]
    scratch = [
        pltpu.VMEM((heads, held, packed), bfloat),
        pltpu.VMEM((heads, packed, held), bfloat),
        pltpu.VMEM(scores, single),
        pltpu.VMEM((width, total), bfloat),
    ]
    if ends:
        specs += [
            pl.BlockSpec((heads, packed, WINDOW), lambda i: (pick, 0, 0)),
            pl.BlockSpec(scores, lambda i: (pick, 0, 0)),
        ]
        inputs += list(begun)
        shapes = [((heads, packed, held), single), ((heads, 8, 2 * QB), single)]
        scratch.append(pltpu.VMEM(scores, single))
    else:
        specs.append(full(kvp.shape))
        inputs.append(kvp)
        shapes = [((heads, packed, WINDOW), bfloat), ((heads, packed, held - WINDOW), single), (scores, single)]
        scratch.append(pltpu.VMEM((heads, packed, held), single))
    out_specs += [full(shape) for shape, _ in shapes]
    out_shape += [jax.ShapeDtypeStruct(shape, kind) for shape, kind in shapes]
    return pl.pallas_call(
        kernel,
        grid=(steps,),
        in_specs=specs,
        out_specs=out_specs,
        out_shape=out_shape,
        scratch_shapes=scratch,
        compiler_params=params(60, 1),
        cost_estimate=light(),
        name="attend_back",
    )(*inputs)


def settle_kernel(
    order, dq0, dq1, dq2, dkv1, dkv2, behind, normed, sums1, sums2, hot, gain_terms, router0, router1,
    out0, out1, out2, out3, grad,
):
    heads = behind.shape[0]
    rows = out0.shape[1]
    outs = (out0, out1, out2, out3)
    edge = dkv1.shape[2] - WINDOW
    held = [(dq1, dkv1, sums1, number) for number in range(dkv1.shape[0])]
    held += [(dq2, dkv2, sums2, number) for number in range(dkv2.shape[0])]
    parts = []
    for head, (dq, dkvt, _, number) in enumerate(held):
        at = slice(number * HEAD_DIM, (number + 1) * HEAD_DIM)
        last = dkvt[number, :, edge:] + behind[head].astype(single)
        parts.append(jnp.concatenate([dq0[head * HEAD_DIM : (head + 1) * HEAD_DIM, :], dq[at, :]], axis=1))
        parts.append(jnp.concatenate([dkvt[number, :, :edge], last], axis=1).astype(bfloat))
    whole = jnp.concatenate(parts, axis=0)

    def put(place, lane):
        outs[place][...] = whole[:, lane * rows : (lane + 1) * rows]

    by_lane(order[0], put)
    total = None
    for lane in range(len(outs)):
        term = dot(whole[:, lane * rows : (lane + 1) * rows], normed[lane])
        total = term if total is None else total + term
    total = total.astype(bfloat)
    part = grad.shape[2]
    count = total.shape[0]
    found = []
    for _, _, ref, number in held:
        value = None
        for chunk in range(CHUNKS):
            term = lax.dot_general(
                jnp.broadcast_to(ref[number, chunk : chunk + 1, :], (8, 2 * QB)),
                hot[chunk * 2 * QB : (chunk + 1) * 2 * QB, :],
                (NN, ((), ())),
                precision=lax.Precision.HIGHEST,
                preferred_element_type=single,
            )
            value = term if value is None else value + term
        found.append(value[0:1, :])
    found.append(jnp.zeros((1, part - BUCKETS * heads), single))
    rel = jnp.broadcast_to(jnp.concatenate(found, axis=1), (16, part))
    router = (router0[...] + router1[...]).astype(bfloat)
    chunk = grad.shape[1]
    blocks = grad.shape[0] // len(outs)
    for lane in range(len(outs)):
        columns = slice(lane * part, (lane + 1) * part)
        mine = jnp.where(order[0] == lane, 1.0, 0.0)
        terms = jnp.broadcast_to(gain_terms[:, columns], (16, part))
        rows_out = [total[:, columns], (rel * mine).astype(bfloat), terms.astype(bfloat), router[:, columns]]
        left = blocks * chunk - sum(value.shape[0] for value in rows_out)
        if left:
            rows_out.append(jnp.zeros((left, part), bfloat))
        rows_out = jnp.concatenate(rows_out, axis=0)
        for block in range(blocks):
            grad[lane * blocks + block] = rows_out[block * chunk : (block + 1) * chunk, :]


def settle(order, dq0, late, behind, normed, sums, hot, gain_terms, routers, blocks):
    lanes, rows, width = normed.shape
    tall = 3 * width // lanes
    count = tall + 32 + routers[0].shape[0]
    count = -(-count // max(16, blocks)) * max(16, blocks)
    cut = blocks if count // blocks % 16 == 0 else 1
    (dq1, dkv1), (dq2, dkv2) = late
    return once(
        settle_kernel,
        "settle",
        (order, dq0, dq1, dq2, dkv1, dkv2, behind, normed, *sums, hot, gain_terms, *routers),
        [((tall, rows), bfloat)] * lanes + [((lanes * cut, count // cut, width // lanes), bfloat)],
    )


def middle_kernel(o0, o1, o2, o3, w0, w1, w2, w3, x, gain, code, y_out, send0, send1):
    y = x[...].astype(single)
    for ref, weight in ((o0, w0), (o1, w1), (o2, w2), (o3, w3)):
        y = y + dot(ref[...], weight[...], TN)
    y_out[...] = y
    inverse = lax.rsqrt(jnp.mean(y * y, axis=-1, keepdims=True) + epsilon)
    normed = (y * inverse * gain[...]).astype(bfloat)
    slots = send0.shape[0]
    for number, ref in enumerate((send0, send1)):
        slot = lax.broadcasted_iota(jnp.int32, (slots, y.shape[0]), 0) + number * slots
        pick = ((slot == code[0:1, :]) | (slot == code[1:2, :])).astype(bfloat)
        ref[...] = dot(pick, normed).astype(bfloat)


def middle(ots, w_out, x, gain, code, slots):
    rows, width = x.shape
    return once(
        middle_kernel,
        "middle",
        (*ots, *w_out, x, gain, code),
        [((rows, width), single), ((slots, width), bfloat), ((slots, width), bfloat)],
    )


NOTES = 16


def send_kernel(place, value, *outs):
    begin = 0
    for out in outs:
        count = out.shape[0]
        here = lax.broadcasted_iota(jnp.int32, (count, value.shape[0]), 0) + begin
        pick = ((here == place[0:1, :]) | (here == place[1:2, :])).astype(bfloat)
        out[...] = dot(pick, value[...]).astype(bfloat)
        begin += count


def send_rows(place, value, blocks, counts):
    shapes = [((blocks * count, value.shape[1]), bfloat) for count in counts]
    found = once(send_kernel, "send_rows", (place, value), shapes)
    return [part.reshape(blocks, count, -1) for part, count in zip(found, counts)]


def send_noted_kernel(part, notes, out):
    for block in range(part.shape[0]):
        out[block, NOTES:, :] = part[block]
        out[block, :NOTES, :] = jnp.broadcast_to(notes[...], (NOTES, part.shape[2]))


def send_noted(part, notes):
    blocks, count, width = part.shape
    outputs = [((blocks, count + NOTES, width), bfloat)]
    return once(send_noted_kernel, "send_noted", (part, notes), outputs)[0]


def collect(code, refs):
    total = None
    for number, ref in enumerate(refs):
        slots = ref.shape[0]
        slot = lax.broadcasted_iota(jnp.int32, (code.shape[0], slots), 1) + number * slots
        pick = ((slot == code[:, 0:1]) | (slot == code[:, 1:2])).astype(bfloat)
        part = dot(pick, ref[...])
        total = part if total is None else total + part
    return total


def return_kernel(d0, d1, code, y, gain, cotangent, w0, w1, w2, w3, o0, o1, o2, o3, dy_out, gg_out, *dots):
    dn = collect(code, (d0, d1))
    values = y[...]
    inverse = lax.rsqrt(jnp.mean(values * values, axis=-1, keepdims=True) + epsilon)
    hat = values * inverse
    gg_out[...] = jnp.sum(dn * hat, axis=0, keepdims=True)
    scaled = dn * gain[...]
    dy = cotangent[...].astype(single) + inverse * (scaled - hat * jnp.mean(scaled * hat, axis=-1, keepdims=True))
    dy_out[...] = dy
    low = dy.astype(bfloat)
    for place, (ref, weight) in enumerate(((o0, w0), (o1, w1), (o2, w2), (o3, w3))):
        dots[place][...] = dot(weight[...], low, NT).astype(bfloat)
        dots[place + 4][...] = dot(ref[...], low).astype(bfloat)


def return_rows(d0, d1, code, y, gain, cotangent, w_out, ots):
    rows, width = y.shape
    lanes = len(ots)
    return once(
        return_kernel,
        "return_rows",
        (d0, d1, code, y, gain, cotangent, *w_out, *ots),
        [((rows, width), single), ((1, width), single)]
        + [((width // lanes, rows), bfloat)] * lanes
        + [((width // lanes, width), bfloat)] * lanes,
    )


def finish_kernel(z0, z1, code, y, out):
    out[...] = (y[...] + collect(code, (z0, z1))).astype(bfloat)


def finish(z0, z1, code, y):
    return once(finish_kernel, "finish", (z0, z1, code, y), [(y.shape, bfloat)])[0]


def unpack_kernel(value, wq, wk, wv, gain, q_out, k_out, v_out, router_out, norm_out, rel_out, gain_out):
    blocks, lanes, count, part = value.shape
    heads = part // HEAD_DIM
    mark = 3 * part
    others = None
    for lane in range(lanes):
        rows = jnp.concatenate([value[block, lane] for block in range(blocks)], axis=0)
        whole = rows[:mark, :].astype(single).T
        for head in range(heads):
            at = slice((lane * heads + head) * HEAD_DIM, (lane * heads + head + 1) * HEAD_DIM)
            for number, ref in enumerate((q_out, k_out, v_out)):
                begin = (3 * head + number) * HEAD_DIM
                ref[:, at] = whole[:, begin : begin + HEAD_DIM]
        term = rows[mark : mark + 32 + router_out.shape[1], :].astype(single)
        rel_out[lane : lane + 1, :] = term[0:1, :]
        others = term if others is None else others + term
    norm_out[...] = others[16:17, :]
    router_out[...] = others[32:, :].T
    total = None
    for ref, weight in ((q_out, wq), (k_out, wk), (v_out, wv)):
        term = jnp.sum(ref[...] * weight[...].astype(single), axis=1, keepdims=True)
        total = term if total is None else total + term
    total = jnp.broadcast_to(total / gain[...].astype(single), (part, 128))
    gain_out[...] = total.T[0:1, :]


def unpack(value, wq, wk, wv, gain, experts):
    part, width = wq.shape
    outputs = [((part, width), single)] * 3
    outputs += [((part, experts), single), ((1, part), single), ((value.shape[1], part), single), ((1, part), single)]
    return once(unpack_kernel, "unpack", (value, wq, wk, wv, gain), outputs)


def tail_kernel(order, *refs):
    *pieces, wt, x, gain, dy, out = refs
    dn = None
    for number, ref in enumerate(pieces):
        block = order[number % 4]
        tall = ref.shape[0]
        begin = block * tall
        term = dot(ref[...], wt[pl.ds(pl.multiple_of(begin, 64), tall), :], TN)
        dn = term if dn is None else dn + term
    values = x[...].astype(single)
    inverse = lax.rsqrt(jnp.mean(values * values, axis=-1, keepdims=True) + epsilon)
    hat = values * inverse
    scaled = dn * gain[...]
    out[...] = dy[...] + inverse * (scaled - hat * jnp.mean(scaled * hat, axis=-1, keepdims=True))


def tail(order, pieces, wt, x, gain, dy):
    return once(tail_kernel, "tail", (order, *pieces, wt, x, gain, dy), [(x.shape, single)])[0]


GELU_0 = 0.7978845608028654
GELU_1 = 0.7978845608028654 * 0.044715
FF_BLOCK = 512
ROW_BLOCK = 256


def expert_kernel(
    mine, xs, router, other, w1, da, cot, g10, g11, g12, g13, g2, dx_out, a_out, m_out, total, dgate, gate, act_all, du_all, xst, dzt
):
    step = pl.program_id(0)
    rows = xs.shape[0]
    experts = router.shape[0]

    def picks():
        lane = lax.broadcasted_iota(jnp.int32, (rows, experts), 1)
        return lane == mine[0], lane == other[...] - 1

    @pl.when(step == 0)
    def _():
        logits = dot(xs[...], router[...], NT)
        own, rest = picks()
        margin = jnp.sum(jnp.where(own, logits, 0.0) - jnp.where(rest, logits, 0.0), axis=1, keepdims=True)
        value = 1.0 / (1.0 + jnp.exp(-margin))
        value = jnp.where(other[...] > 0, value, 0.0)
        gate[...] = jnp.broadcast_to(value, gate.shape)
        dgate[...] = jnp.zeros_like(dgate)
        total[...] = jnp.zeros_like(total)
        for begin in range(0, rows, ROW_BLOCK):
            at = slice(begin, begin + ROW_BLOCK)
            xst[:, at] = xs[at, :].T
            dzt[:, at] = (cot[at, :].astype(single) * gate[at, 0:1]).astype(bfloat).T

    for begin in range(0, rows, ROW_BLOCK):
        at = slice(begin, begin + ROW_BLOCK)
        u = dot(xs[at, :], w1[...])
        square = u * u
        tan = jnp.tanh(u * (GELU_0 + GELU_1 * square))
        half = 0.5 + 0.5 * tan
        act = u * half
        slope = half + act * (1.0 - half) * (2.0 * GELU_0 + 6.0 * GELU_1 * square)
        back = da[at, :].astype(single)
        product = act * back
        part = product[:, :128]
        for col in range(128, product.shape[1], 128):
            part = part + product[:, col : col + 128]
        dgate[at, :] += part
        act_all[at, :] = act.astype(bfloat)
        a_out[at, :] = (act * gate[at, 0:1]).astype(bfloat)
        du_all[at, :] = (gate[at, 0:1] * back * slope).astype(bfloat)
    total[...] += dot(du_all[...], w1[...], NT)
    grad = dot(xst[...], du_all[...]).astype(bfloat)
    part = g10.shape[0]

    def put(place, lane):
        (g10, g11, g12, g13)[place][...] = grad[lane * part : (lane + 1) * part, :]

    by_lane(mine[1], put)
    g2[...] = dot(dzt[...], act_all[...]).astype(bfloat).T

    @pl.when(step == pl.num_programs(0) - 1)
    def _():
        own, rest = picks()
        value = gate[:, 0:1]
        weight = value * (1.0 - value) * jnp.sum(dgate[...], axis=1, keepdims=True)
        m = (weight * (own.astype(single) - rest.astype(single))).astype(bfloat)
        m_out[...] = dot(m, xs[...], TN)
        dx_out[...] = (total[...] + dot(m, router[...])).astype(bfloat)


def expert(mine, xs, router, other, w1, da, cot, local):
    rows, width = xs.shape
    inner = w1.shape[2]
    experts = router.shape[0]
    block = FF_BLOCK
    whole = lambda shape: pl.BlockSpec(shape, lambda f: (0,) * len(shape))
    return pl.pallas_call(
        expert_kernel,
        grid=(inner // block,),
        in_specs=[
            SMEM,
            whole((rows, width)),
            whole((experts, width)),
            whole((rows, 1)),
            pl.BlockSpec((None, width, block), lambda f: (local, 0, f)),
            pl.BlockSpec((rows, block), lambda f: (0, f)),
            whole((rows, width)),
        ],
        out_specs=[
            *[pl.BlockSpec((width // len(MASKS), block), lambda f: (0, f))] * len(MASKS),
            pl.BlockSpec((block, width), lambda f: (f, 0)),
            whole((rows, width)),
            pl.BlockSpec((rows, block), lambda f: (0, f)),
            whole((experts, width)),
        ],
        out_shape=[
            *[jax.ShapeDtypeStruct((width // len(MASKS), inner), bfloat)] * len(MASKS),
            jax.ShapeDtypeStruct((inner, width), bfloat),
            jax.ShapeDtypeStruct((rows, width), bfloat),
            jax.ShapeDtypeStruct((rows, inner), bfloat),
            jax.ShapeDtypeStruct((experts, width), single),
        ],
        scratch_shapes=[
            pltpu.VMEM((rows, width), single),
            pltpu.VMEM((rows, 128), single),
            pltpu.VMEM((rows, 128), single),
            pltpu.VMEM((rows, block), bfloat),
            pltpu.VMEM((rows, block), bfloat),
            pltpu.VMEM((width, rows), bfloat),
            pltpu.VMEM((width, rows), bfloat),
        ],
        compiler_params=params(60, 1),
        cost_estimate=cost(20 * rows * width * inner, 8 * rows * inner + 8 * width * inner, rows * inner),
        name="expert",
    )(mine, xs, router, other, w1, da, cot)


def tie(*values):
    return lax.optimization_barrier(values)


def swap(value, axis, mask):
    return lax.ppermute(value, axis, [(i, i ^ mask) for i in range(lax.axis_size(axis))])


def per_device(
    hidden_in,
    norm1_gain,
    w_query,
    w_key,
    w_value,
    w_out,
    rel_bias,
    norm2_gain,
    w_router,
    w_first,
    w_second,
    routes,
    priority,
    segments,
    grad_out,
):
    lanes = lax.axis_size("head")
    blocks = lax.axis_size("seq")
    lane = lax.axis_index("head")
    place = lax.axis_index("seq")
    rows, width = hidden_in.shape[2:]
    x = hidden_in.reshape(rows, width)
    total = rows * lanes
    part = width // lanes
    heads = part // HEAD_DIM
    cotangent = grad_out.reshape(rows, width)
    experts = w_router.shape[1]
    local = w_first.shape[0]
    slot_rows = max(2, 4 * rows // experts)
    slots = blocks * slot_rows
    capacity = 5 * rows * lanes // (2 * local)

    far = swap(x, "head", 2)
    near = swap(x, "head", 1)
    order = jnp.stack([lane, lane ^ 2, lane ^ 1, lane ^ 3]).astype(jnp.int32)
    at = lambda value, mask: lax.dynamic_index_in_dim(value, lane ^ mask, 0, keepdims=False)

    def trade(value):
        return [value[0]] + [swap(value[place], "head", MASKS[place]) for place in range(1, lanes)]

    route_t = routes.reshape(rows, -1).T
    top_count = route_t.shape[0]
    pair_routes = route_t.reshape(-1)
    pair_prio = priority.reshape(rows, -1).T.reshape(-1)
    expert_ids = jnp.arange(experts, dtype=jnp.int32)
    pair_hot = (expert_ids[:, None] == pair_routes[None, :]).astype(jnp.int32)
    earlier = (pair_routes[:, None] == pair_routes[None, :]) & (pair_prio[:, None] < pair_prio[None, :])
    local_rank = jnp.sum(earlier.astype(jnp.int32), axis=0)
    code = (pair_routes % local) * slots + (pair_routes // local) * slot_rows + local_rank
    code_t = code.reshape(top_count, rows)
    code = code_t.T
    one, two, three = slot_rows * 3 // 10, slot_rows * 7 // 10, slot_rows // 2
    counts = (one, two - one, slot_rows - two + three, slot_rows - three)
    held = ((0, 0, one, 0, 0), (0, one, two, 1, 0), (0, two, slot_rows, 2, 0), (1, 0, three, 2, slot_rows - two))
    send_place = jnp.zeros_like(local_rank)
    for owner, lowest, highest, number, skip in held + ((1, three, slot_rows, 3, 0),):
        inside = (pair_routes % local == owner) & (local_rank >= lowest) & (local_rank < highest)
        row = blocks * sum(counts[:number]) + (pair_routes // local) * counts[number] + skip
        send_place = send_place + jnp.where(inside, row + local_rank - lowest, 0)
    send_place = send_place.reshape(top_count, rows)

    def exchange(value):
        return lax.all_to_all(
            value.reshape(blocks, slot_rows, -1), "seq", split_axis=0, concat_axis=0, tiled=True
        ).reshape(slots, -1)


    block_rank = (jnp.min(pair_prio) // (top_count * rows)).reshape(1)
    tally = jnp.concatenate([jnp.sum(pair_hot, axis=1), block_rank, jnp.zeros((part - experts - 1,), jnp.int32)])
    gains = jnp.stack([norm1_gain, norm2_gain, tally.astype(bfloat)])
    gains = jnp.concatenate([gains, jnp.zeros((GAINS - 3, part), bfloat)], axis=0)
    hot, allowed = lane_tables()
    table = rel_bias.reshape(heads, BUCKETS)
    vecs = dot(table, jnp.asarray(hot.T, bfloat)).reshape(heads, CHUNKS, 2 * QB)
    vecs = jnp.where(jnp.asarray(allowed)[None], vecs, MASKED)
    vecs = jnp.concatenate([vecs, jnp.zeros((heads, 8 - CHUNKS, 2 * QB), single)], axis=1)
    base = place * total
    own = lax.dynamic_slice_in_dim(segments, base, total, 0)
    low = jnp.zeros_like(own)
    for number in range(1, 4):
        low = jnp.where(own == number, jnp.sum((segments < number).astype(jnp.int32)), low)
    low = low - base + WINDOW
    need = (jnp.max(low.reshape(-1, QB), axis=1) > jnp.arange(total // QB) * QB).astype(jnp.int32)
    low = low.reshape(1, total)
    packed = trade(pack(order, w_query, w_key, w_value, w_router.T, gains))
    cot_parts = send_rows(send_place, cotangent, blocks, counts)
    spread_out = lambda value: lax.all_to_all(value, "seq", split_axis=0, concat_axis=0, tiled=True)
    cots = [spread_out(cot_parts[0])]
    far, near, packed, cots, cot_parts, low, need, vecs, code = tie(
        far, near, packed, cots, cot_parts, low, need, vecs, code
    )
    both = swap(far, "head", 1)
    cots.append(spread_out(cot_parts[1]))
    both, w_second, w_out = tie(both, w_second, w_out)

    out_far = swap(w_out, "head", 2)
    out_near = swap(w_out, "head", 1)
    second_full = lax.all_gather(w_second, "head", axis=1, tiled=True)

    normed, qt, kv, kv_last, w_rows, router_t, gains = project(order, (x, far, near, both), packed, heads, experts)
    w_rows_full = lax.all_gather(w_rows, "head", axis=0, tiled=True)
    gain_one, gain_two = gains[0:1], gains[1:2]
    kvp = lax.ppermute(kv_last, "seq", [(i, i + 1) for i in range(blocks - 1)])
    early = WINDOW // QB
    later = total // QB - early
    *ot, lse_later = attention_forward(early, later, order, need, low, qt, None, kv, vecs, lanes)
    noted = send_noted(cot_parts[3], gains[2:3].astype(bfloat))
    ot, kvp, cots[1], cot_parts[2], noted = tie(ot, kvp, cots[1], cot_parts[2], noted)
    cots.append(spread_out(cot_parts[2]))
    *ot, lse_early = attention_forward(0, early, order, need, low, qt, kvp, kv, vecs, lanes, ot)
    ot, out_far, out_near = tie(ot, out_far, out_near)
    w_outs = (w_out, out_far, out_near, swap(out_far, "head", 1))
    ots = trade(ot)
    ots, w_first, cots[2] = tie(ots, w_first, cots[2])
    noted = spread_out(noted)
    first_full = lax.all_gather(w_first, "head", axis=1, tiled=True)

    y, *sends = middle(ots, w_outs, x, gain_two, code_t, slots)
    sends[0], noted = tie(sends[0], noted)

    tallies = noted[:, 0, :].reshape(blocks * lanes, part).astype(jnp.int32)
    ahead = (tallies[:, experts : experts + 1] < block_rank[None, :]).astype(jnp.int32)
    offsets = jnp.sum(tallies[:, :experts] * ahead, axis=0)
    kept = (jnp.sum(pair_hot * offsets[:, None], axis=0) + local_rank < capacity).reshape(top_count, rows)
    slot_ids = jnp.arange(local * slots, dtype=jnp.int32)[:, None]
    other = jnp.sum(
        jnp.where(slot_ids == code_t[0:1], jnp.where(kept[0:1], route_t[1:2] + 1, 0), 0)
        + jnp.where(slot_ids == code_t[1:2], jnp.where(kept[1:2], route_t[0:1] + 1, 0), 0),
        axis=1,
    )
    last = slot_rows - two
    cot_slots = [[cots[0], cots[1], cots[2][:, :last]], [cots[2][:, last:], noted[:, NOTES:, :]]]
    cot_slots = [jnp.concatenate(value, axis=1).reshape(slots, width) for value in cot_slots]
    backs = [dot(cot_slots[0], second_full[0], NT).astype(bfloat)]
    other, backs[0] = tie(other, backs[0])
    other = other.reshape(local, blocks, slot_rows)
    far_others = [
        swap(lax.dynamic_index_in_dim(other, place ^ mask, 1, keepdims=False), "seq", mask) for mask in range(1, blocks)
    ]
    mine = jnp.stack([place * local, lane]).astype(jnp.int32)
    backs.append(dot(cot_slots[1], second_full[1], NT).astype(bfloat))
    received = [exchange(sends[0])]
    sends[1], far_others, *backs = tie(sends[1], far_others, *backs)
    received.append(exchange(sends[1]))
    far_others = jnp.concatenate([lax.dynamic_index_in_dim(other, place, 1, keepdims=False)[None], jnp.stack(far_others)])
    other = jnp.stack(
        [lax.dynamic_index_in_dim(far_others, place ^ number, 0, keepdims=False) for number in range(blocks)], axis=1
    ).reshape(local, slots, 1)

    def run_expert(number):
        return expert(
            mine + jnp.asarray([number, 0], jnp.int32),
            received[number],
            router_t,
            other[number],
            first_full,
            backs[number],
            cot_slots[number],
            number,
        )

    received[1], w_rows_full, (*first_parts0, second0, dx0, act0, router0) = tie(
        received[1], w_rows_full, run_expert(0)
    )
    returns = [exchange(dx0)]
    second0 = lax.psum_scatter(second0, "head", scatter_dimension=0, tiled=True)
    returns[0], second0, (*first_parts1, second1, dx1, act1, router1) = tie(returns[0], second0, run_expert(1))
    def near_parts(parts):
        return swap(parts[3], "head", 1), swap(parts[2], "head", 1)

    def add(one, two, kind=single):
        return (one.astype(single) + two.astype(single)).astype(kind)

    def scatter(value):
        return lax.psum_scatter(value, "head", scatter_dimension=0, tiled=True)

    cross0, direct0 = near_parts(first_parts0)
    returns.append(exchange(dx1))
    away0, act0, act1 = tie(add(first_parts0[1], cross0, bfloat), act0, act1)
    across0 = swap(away0, "head", 2)
    cross1, direct1 = near_parts(first_parts1)
    second1 = scatter(second1)

    z0, z1 = (dot(act, second_full[i]).astype(bfloat) for i, act in enumerate((act0, act1)))
    away1 = add(first_parts1[1], cross1, bfloat)
    returns[1], across0, z0, z1, away1 = tie(returns[1], across0, z0, z1, away1)
    first0 = add(add(first_parts0[0], direct0), across0)
    dy, gain_terms, *douts = return_rows(
        returns[0], returns[1], code, y, gain_two, cotangent, w_outs, ots
    )
    douts, outw = trade(douts[:lanes]), douts[lanes:]
    outw_cross, outw_direct = near_parts(outw)
    dy, z0 = tie(dy, z0)
    z_back = [exchange(z0)]
    douts, outw_cross, outw_direct = tie(douts, outw_cross, outw_direct)

    def sum_blocks(value):
        last = value.shape[-1]
        value = value.reshape(lanes * blocks, -1, last)
        value = lax.all_to_all(value, ("head", "seq"), split_axis=0, concat_axis=0, tiled=True)
        return jnp.sum(value.reshape(lanes, blocks, -1, last).astype(single), axis=1).astype(bfloat)

    dq_early, behind, dkvt_early, ds_early = attention_backward(
        0, early, (0, heads), order, need, low, qt, kvp, kv, vecs, lse_early, douts
    )
    behind = lax.ppermute(behind, "seq", [(i + 1, i) for i in range(blocks - 1)])
    dq_early, second1 = tie(dq_early, second1)
    outw_across = swap(add(outw[1], outw_cross, bfloat), "head", 2)
    hops = [1 << bit for bit in range(blocks.bit_length() - 1)]

    def hop(value, masks):
        for mask in masks:
            value = add(value, swap(value, "seq", mask), bfloat)
        return value

    cut = heads - 1

    def later_part(span):
        return attention_backward(
            early, later, span, order, need, low, qt, None, kv, vecs, lse_later, douts, (dkvt_early, ds_early)
        )

    dq_last, dkv_last, sums_last = later_part((cut, heads - cut))
    dkv_last, z_back[0], z1, behind, outw_across, away1 = tie(
        dkv_last, z_back[0], z1, behind, outw_across, away1
    )
    across1 = swap(away1, "head", 2)
    grad_outw = add(add(outw[0], outw_direct), outw_across, bfloat)
    grad_outw = hop(grad_outw, hops[:-2])
    z_back.append(exchange(z1))
    ds_early, dkv_last = tie(ds_early, dkv_last)
    dq_first, dkv_first, sums_first = later_part((0, cut))
    dq_first, grad_outw, across1 = tie(dq_first, grad_outw, across1)
    grad_outw = hop(grad_outw, hops[-2:-1])
    *parts, grad_part = settle(
        order,
        dq_early,
        ((dq_first, dkv_first), (dq_last, dkv_last)),
        behind,
        normed,
        (sums_first, sums_last),
        jnp.asarray(hot, single),
        gain_terms,
        (router0, router1),
        blocks,
    )
    pieces = trade(parts)
    first1 = add(add(first_parts1[0], direct1), across1)
    grad_part, z_back[1] = tie(grad_part, z_back[1])
    value = sum_blocks(grad_part)
    output = finish(z_back[0], z_back[1], code, y).reshape(hidden_in.shape)
    value, grad_outw, pieces[1], pieces[2] = tie(value, grad_outw, pieces[1], pieces[2])
    grad_outw = hop(grad_outw, hops[-1:])
    count = value.shape[1]
    value = lax.all_to_all(
        jnp.broadcast_to(value[None], (blocks,) + value.shape), "seq", split_axis=0, concat_axis=0, tiled=True
    )
    grad_hidden = tail(order, pieces, w_rows_full, x, gain_one, dy).reshape(hidden_in.shape)
    value, grad_hidden, output = tie(value, grad_hidden, output)
    if count % 16:
        value = value.transpose(1, 0, 2, 3).reshape(1, lanes, -1, part)
    *grads, grad_router, grad_norm2, rels, grad_norm1 = unpack(value, w_query, w_key, w_value, norm1_gain.reshape(part, 1), experts)
    grad_rel = lax.dynamic_index_in_dim(rels, lane, 0, keepdims=False)[: heads * BUCKETS]
    return (
        output,
        grad_hidden,
        grad_norm1.reshape(part),
        grads[0],
        grads[1],
        grads[2],
        grad_outw.astype(single),
        grad_rel,
        grad_norm2.reshape(part),
        grad_router,
        jnp.stack([first0, first1]),
        jnp.stack([second0, second1]).astype(single),
    )


def solution(mesh):
    return jax.shard_map(
        per_device,
        mesh=mesh,
        in_specs=(
            P("seq", "head", None, None),
            P("head"),
            P("head", None),
            P("head", None),
            P("head", None),
            P("head", None),
            P("head"),
            P("head"),
            P("head", None),
            P("seq", "head", None),
            P("seq", "head", None),
            P("seq", "head", None, None),
            P("seq", "head", None, None),
            P(),
            P("seq", "head", None, None),
        ),
        out_specs=(
            P("seq", "head", None, None),
            P("seq", "head", None, None),
            P("head"),
            P("head", None),
            P("head", None),
            P("head", None),
            P("head", None),
            P("head"),
            P("head"),
            P("head", None),
            P("seq", "head", None),
            P("seq", "head", None),
        ),
        check_vma=False,
    )
```

```python
import functools

import jax
import jax.numpy as jnp
import numpy as np
from jax import lax
from jax.experimental import pallas as pl
from jax.experimental.pallas import tpu as pltpu
from jax.sharding import PartitionSpec as P

HEAD_DIM = 64
WINDOW = 1024
BUCKETS = 32
QB = 256
CHUNKS = WINDOW // QB + 1
KEYS = CHUNKS * QB
MASKED = -1e30
epsilon = 1e-06
bfloat = jnp.bfloat16
single = jnp.float32
MIB = 1 << 20

VMEM = pl.BlockSpec(memory_space=pltpu.VMEM)
SMEM = pl.BlockSpec(memory_space=pltpu.SMEM)


def dot(a, b, dims=((1,), (0,))):
    return lax.dot_general(a, b, (dims, ((), ())), preferred_element_type=single)


NN = ((1,), (0,))
NT = ((1,), (1,))
TN = ((0,), (0,))


def params(mib, grid=0):
    extra = {"dimension_semantics": ("arbitrary",) * grid} if grid else {}
    return pltpu.CompilerParams(vmem_limit_bytes=mib * MIB, **extra)


def full(shape):
    return pl.BlockSpec(tuple(shape), lambda i: (0,) * len(shape))


def once(kernel, name, inputs, outputs, scratch=()):
    found = pl.pallas_call(
        kernel,
        grid=(1,),
        in_specs=[SMEM if value.ndim == 1 else full(value.shape) for value in inputs],
        out_specs=[full(shape) for shape, _ in outputs],
        out_shape=[jax.ShapeDtypeStruct(shape, kind) for shape, kind in outputs],
        scratch_shapes=list(scratch),
        compiler_params=params(60, 1),
        cost_estimate=light(),
        name=name,
    )(*inputs)
    return found


def cost(flops, moved, trans=0):
    return pl.CostEstimate(flops=int(flops), bytes_accessed=int(moved), transcendentals=int(trans))


def light():
    return cost(1000, 1000)


MASKS = (0, 2, 1, 3)


def by_lane(own, action):
    for lane in range(len(MASKS)):

        @pl.when(own == lane)
        def _():
            for place, mask in enumerate(MASKS):
                action(place, lane ^ mask)


def bucket_edges(window_len, bucket_count):
    middle = bucket_count // 2
    edge_list = []
    for number in range(1, bucket_count):
        if number < middle:
            edge_list.append(number)
        else:
            edge_list.append(int(middle * (window_len / middle) ** ((number - middle) / middle)))
    return edge_list


def lane_tables():
    lane = np.arange(2 * QB)
    offset = np.where(lane < QB, lane, lane - 2 * QB)
    distance = WINDOW - QB * np.arange(CHUNKS)[:, None] + offset[None, :]
    allowed = (distance >= 0) & (distance < WINDOW)
    bucket = np.zeros(distance.shape, np.int32)
    for edge_value in bucket_edges(WINDOW, BUCKETS):
        bucket = bucket + (distance >= edge_value)
    hot = (bucket.reshape(-1)[:, None] == np.arange(BUCKETS)[None, :]) & allowed.reshape(-1)[:, None]
    return hot, allowed


GAINS = 16


def pack_kernel(order, wq, wk, wv, router_t, gains, *outs):
    part = wq.shape[0]
    experts = router_t.shape[0]

    def put(place, lane):
        for number, weight in enumerate((wq, wk, wv)):
            outs[place][:, number * part : (number + 1) * part] = weight[:, lane * part : (lane + 1) * part]

    by_lane(order[0], put)
    rest = outs[0].shape[1] - 3 * part
    for ref in outs:
        ref[:experts, 3 * part :] = router_t[...]
        ref[experts : experts + GAINS, 3 * part :] = gains[...]
        ref[experts + GAINS :, 3 * part :] = jnp.zeros((part - experts - GAINS, rest), bfloat)


def pack(order, wq, wk, wv, router_t, gains):
    part, width = wq.shape
    return once(pack_kernel, "pack", (order, wq, wk, wv, router_t, gains), [((part, width), bfloat)] * len(MASKS))


def project_kernel(
    order, x0, x1, x2, x3, p0, p1, p2, p3, n_out, qt_out, kv_out, kv_last, rows_out, router_out, gain_out, wq, wk, wv
):
    rows, width = x0.shape
    heads = kv_out.shape[0]
    part = heads * HEAD_DIM
    experts = router_out.shape[0]
    packed = (p0, p1, p2, p3)
    for place, ref in enumerate(packed):
        at = pl.ds(pl.multiple_of(order[place] * part, 64), part)
        for number, weight in enumerate((wq, wk, wv)):
            weight[at, :] = ref[:, number * part : (number + 1) * part]

    def spread(skip, count):
        found = []
        for lane in range(len(packed)):
            piece = None
            for place, ref in enumerate(packed):
                value = ref[skip : skip + count, 3 * part :]
                piece = value if piece is None else jnp.where(order[place] == lane, value, piece)
            found.append(piece)
        return jnp.concatenate(found, axis=1)

    router_out[...] = spread(0, experts)
    gains = spread(experts, GAINS).astype(single)
    gain_out[...] = gains[0:8, :]
    wq_t = wq[...].T
    k_t = wk[...].T
    v_t = wv[...].T
    for head in range(heads):
        at = slice(head * HEAD_DIM, (head + 1) * HEAD_DIM)
        for number, value in enumerate((wq_t, k_t, v_t)):
            begin = (3 * head + number) * HEAD_DIM
            rows_out[begin : begin + HEAD_DIM, :] = value[at, :]
    for place, ref in enumerate((x0, x1, x2, x3)):
        block = order[place]
        values = ref[...].astype(single)
        inverse = lax.rsqrt(jnp.mean(values * values, axis=-1, keepdims=True) + epsilon)
        normed = (values * inverse * gain_out[0:1, :]).astype(bfloat)
        n_out[block] = normed
        at = pl.ds(pl.multiple_of(block * rows, 128), rows)
        qt = dot(wq_t, normed, NT).astype(bfloat)
        qt_out[:, at] = qt * bfloat(HEAD_DIM**-0.5)
        for head in range(heads):
            begin = 3 * head * HEAD_DIM + HEAD_DIM
            kv = dot(normed, rows_out[begin : begin + 2 * HEAD_DIM, :], NT)
            kv_out[head, at, :] = kv.astype(bfloat)
    kv_last[...] = kv_out[:, kv_out.shape[1] - WINDOW :, :]


def project(order, pieces, packed, heads, experts):
    rows, width = pieces[0].shape
    lanes = len(MASKS)
    total = rows * lanes
    part = heads * HEAD_DIM
    return once(
        project_kernel,
        "project",
        (order, *pieces, *packed),
        [
            ((lanes, rows, width), bfloat),
            ((part, total), bfloat),
            ((heads, total, 2 * HEAD_DIM), bfloat),
            ((heads, WINDOW, 2 * HEAD_DIM), bfloat),
            ((3 * part, width), bfloat),
            ((experts, width), bfloat),
            ((8, width), single),
        ],
        [pltpu.VMEM((width, part), bfloat)] * 3,
    )


def eye(size):
    return (
        lax.broadcasted_iota(jnp.int32, (size, size), 0) == lax.broadcasted_iota(jnp.int32, (size, size), 1)
    ).astype(bfloat)


def stage_attention(kvp, kv, vecs, kv_all, kvt_all, bias):
    heads = kv_all.shape[0]
    unit = eye(2 * HEAD_DIM)
    for head in range(heads):
        if kvp is None:
            kv_all[head] = kv[head]
        else:
            kv_all[head, :WINDOW, :] = kvp[head]
            kv_all[head, WINDOW:, :] = kv[head]
        kvt_all[head] = dot(unit, kv_all[head], NT).astype(bfloat)
        for chunk in range(CHUNKS):
            row = jnp.broadcast_to(vecs[head, chunk : chunk + 1, :], (QB, 2 * QB))
            tile = pltpu.roll(row, 0, 1, stride=1, stride_axis=0)
            bias[head, chunk * QB : (chunk + 1) * QB, :] = tile[:, :QB]


def keep_rows(scores, step, low):
    key = lax.broadcasted_iota(jnp.int32, scores.shape, 0) + step * QB
    return jnp.where(key >= low, scores, MASKED)


def query_tile(step, first, pieces):
    found = []
    for half in range(QB // 128):
        piece = (step + first) * (QB // 128) + half
        found.append((piece // pieces, pl.ds(pl.multiple_of((piece % pieces) * 128, 128), 128)))
    return found


def forward_kernel(first, order, need, low, qt, keys_in, vecs, *rest):
    *more, out0, out1, out2, out3, lse, kv_all, kvt_all, bias = rest
    outs = (out0, out1, out2, out3)
    step = pl.program_id(0)
    heads = kv_all.shape[0]
    pieces = out0.shape[1] // 128

    @pl.when(step == 0)
    def _():
        if more:
            stage_attention(more[0], keys_in, vecs, kv_all, kvt_all, bias)
            for ref, begun in zip(outs, more[1:]):
                ref[...] = begun[...]
        else:
            stage_attention(None, keys_in, vecs, kv_all, kvt_all, bias)

    start = pl.multiple_of(step * QB, QB)

    def run(masked):
        found = []
        for head in range(heads):
            keys = kv_all[head, pl.ds(start, KEYS), :]
            query = qt[head * HEAD_DIM : (head + 1) * HEAD_DIM, :]
            query = jnp.concatenate([query, jnp.zeros_like(query)], axis=0)
            scores = dot(keys, query) + bias[head]
            if masked:
                scores = keep_rows(scores, step + first, low[...])
            peak = jnp.max(scores, axis=0, keepdims=True)
            expo = jnp.exp(scores - peak)
            total = jnp.sum(expo, axis=0, keepdims=True)
            values = kvt_all[head, HEAD_DIM:, pl.ds(start, KEYS)]
            mixed = dot(values, expo.astype(bfloat)) * (1.0 / total)
            found.append(mixed.astype(bfloat))
            lse[0, head : head + 1, :] = peak + jnp.log(total)
        whole = jnp.concatenate(found, axis=0)
        for half, (owner, spot) in enumerate(query_tile(step, first, pieces)):
            for mask, ref in zip(MASKS, outs):

                @pl.when(jnp.bitwise_xor(owner, order[0]) == mask)
                def _():
                    ref[:, spot] = whole[:, half * 128 : (half + 1) * 128]

    pl.when(need[step + first] > 0)(lambda: run(True))
    pl.when(need[step + first] <= 0)(lambda: run(False))


def attention_forward(first, steps, order, need, low, qt, kvp, kv, vecs, lanes, begun=None):
    heads, total, packed = kv.shape
    width = heads * HEAD_DIM
    held = KEYS + (steps - 1) * QB
    own = held - (0 if kvp is None else WINDOW)
    more = [] if kvp is None else [kvp, *begun]
    return pl.pallas_call(
        functools.partial(forward_kernel, first),
        grid=(steps,),
        in_specs=[
            SMEM,
            SMEM,
            pl.BlockSpec((1, QB), lambda i: (0, i + first)),
            pl.BlockSpec((width, QB), lambda i: (0, i + first)),
            pl.BlockSpec((heads, own, packed), lambda i: (0, 0, 0)),
            full(vecs.shape),
        ]
        + [full(value.shape) for value in more],
        out_specs=[full((width, total // lanes))] * lanes + [pl.BlockSpec((1, 8, QB), lambda i: (i, 0, 0))],
        out_shape=[jax.ShapeDtypeStruct((width, total // lanes), bfloat)] * lanes
        + [jax.ShapeDtypeStruct((steps, 8, QB), single)],
        scratch_shapes=[
            pltpu.VMEM((heads, held, packed), bfloat),
            pltpu.VMEM((heads, packed, held), bfloat),
            pltpu.VMEM((heads, KEYS, QB), single),
        ],
        compiler_params=params(60, 1),
        cost_estimate=light(),
        name="attend",
    )(order, need, low, qt, kv, vecs, *more)


def diagonal_sums(tile):
    wide = jnp.concatenate([tile, jnp.zeros_like(tile)], axis=1)
    row = lax.broadcasted_iota(jnp.int32, wide.shape, 0)
    bit = 1
    while bit < QB:
        wide = jnp.where((row & bit) != 0, pltpu.roll(wide, 2 * QB - bit, 1), wide)
        bit *= 2
    return jnp.sum(wide, axis=0, keepdims=True)


def backward_kernel(first, ends, order, need, low, qt, keys_in, vecs, lse, d0, d1, d2, d3, *rest):
    if ends:
        dkvt_in, ds_in, dqt, dkvt, sums, kv_all, kvt_all, bias, dout_all, ds_all = rest
        kvp = None
    else:
        kvp, dqt, behind, dkv_own, ds_all, kv_all, kvt_all, bias, dout_all, dkvt = rest
    step = pl.program_id(0)
    heads = kv_all.shape[0]
    rows = d0.shape[1]

    @pl.when(step == 0)
    def _():
        stage_attention(kvp, keys_in, vecs, kv_all, kvt_all, bias)
        for place, ref in enumerate((d0, d1, d2, d3)):
            dout_all[:, pl.ds(pl.multiple_of(order[place] * rows, 128), rows)] = ref[...]
        if ends:
            ds_all[...] = ds_in[...]
            dkvt[:, :, :WINDOW] = dkvt_in[...]
            dkvt[:, :, WINDOW:] = jnp.zeros_like(dkvt[:, :, WINDOW:])
        else:
            ds_all[...] = jnp.zeros_like(ds_all)
            dkvt[...] = jnp.zeros_like(dkvt)

    start = pl.multiple_of(step * QB, QB)

    def run(masked):
        for head in range(heads):
            at = slice(head * HEAD_DIM, (head + 1) * HEAD_DIM)
            keys = kv_all[head, pl.ds(start, KEYS), :]
            query = qt[at, :]
            none = jnp.zeros_like(query)
            scores = dot(keys, jnp.concatenate([query, none], axis=0)) + bias[head]
            if masked:
                scores = keep_rows(scores, step + first, low[...])
            probs = jnp.exp(scores - lse[0, pl.ds(order[4] + head, 1), :])
            dout = dout_all[at, pl.ds(pl.multiple_of((step + first) * QB, QB), QB)]
            dprobs = dot(keys, jnp.concatenate([none, dout], axis=0))
            delta = jnp.sum(probs * dprobs, axis=0, keepdims=True)
            dscores = probs * (dprobs - delta)
            ds_all[head] += dscores
            dscores = dscores.astype(bfloat)
            probs = probs.astype(bfloat)
            window = pl.ds(start, KEYS)
            dqt[at, :] = (dot(kvt_all[head, :HEAD_DIM, window], dscores) * HEAD_DIM**-0.5).astype(bfloat)
            dkvt[head, :HEAD_DIM, window] += dot(query, dscores, NT)
            dkvt[head, HEAD_DIM:, window] += dot(dout, probs, NT)

    pl.when(need[step + first] > 0)(lambda: run(True))
    pl.when(need[step + first] <= 0)(lambda: run(False))

    @pl.when(step == pl.num_programs(0) - 1)
    def _():
        if not ends:
            behind[...] = dkvt[:, :, :WINDOW].astype(bfloat)
            dkv_own[...] = dkvt[:, :, WINDOW:]
        else:
            for head in range(heads):
                for chunk in range(CHUNKS):
                    sums[head, chunk : chunk + 1, :] = diagonal_sums(ds_all[head, chunk * QB : (chunk + 1) * QB, :])


def attention_backward(first, steps, span, order, need, low, qt, kvp, kv, vecs, lse, douts, begun=()):
    total, packed = kv.shape[1:]
    begin, heads = span
    pick = begin // heads
    width = heads * HEAD_DIM
    held = KEYS + (steps - 1) * QB
    ends = kvp is None
    own = held if ends else held - WINDOW
    scores = (heads, KEYS, QB)
    order = jnp.concatenate([order, jnp.full((1,), begin, jnp.int32)])
    kernel = functools.partial(backward_kernel, first, ends)
    specs = [
        SMEM,
        SMEM,
        pl.BlockSpec((1, QB), lambda i: (0, i + first)),
        pl.BlockSpec((width, QB), lambda i: (pick, i + first)),
        pl.BlockSpec((heads, own, packed), lambda i: (pick, 0, 0)),
        pl.BlockSpec((heads,) + vecs.shape[1:], lambda i: (pick, 0, 0)),
        pl.BlockSpec((1, 8, QB), lambda i: (i, 0, 0)),
    ] + [pl.BlockSpec((width, douts[0].shape[1]), lambda i: (pick, 0))] * 4
    inputs = [order, need, low, qt, kv, vecs, lse, *douts]
    out_specs = [pl.BlockSpec((width, QB), lambda i: (0, i))]
    out_shape = [jax.ShapeDtypeStruct((width, steps * QB), bfloat)]
    scratch = [
        pltpu.VMEM((heads, held, packed), bfloat),
        pltpu.VMEM((heads, packed, held), bfloat),
        pltpu.VMEM(scores, single),
        pltpu.VMEM((width, total), bfloat),
    ]
    if ends:
        specs += [
            pl.BlockSpec((heads, packed, WINDOW), lambda i: (pick, 0, 0)),
            pl.BlockSpec(scores, lambda i: (pick, 0, 0)),
        ]
        inputs += list(begun)
        shapes = [((heads, packed, held), single), ((heads, 8, 2 * QB), single)]
        scratch.append(pltpu.VMEM(scores, single))
    else:
        specs.append(full(kvp.shape))
        inputs.append(kvp)
        shapes = [((heads, packed, WINDOW), bfloat), ((heads, packed, held - WINDOW), single), (scores, single)]
        scratch.append(pltpu.VMEM((heads, packed, held), single))
    out_specs += [full(shape) for shape, _ in shapes]
    out_shape += [jax.ShapeDtypeStruct(shape, kind) for shape, kind in shapes]
    return pl.pallas_call(
        kernel,
        grid=(steps,),
        in_specs=specs,
        out_specs=out_specs,
        out_shape=out_shape,
        scratch_shapes=scratch,
        compiler_params=params(60, 1),
        cost_estimate=light(),
        name="attend_back",
    )(*inputs)


def settle_kernel(
    order, dq0, dq1, dq2, dkv1, dkv2, behind, normed, sums1, sums2, hot, gain_terms, router0, router1,
    out0, out1, out2, out3, grad,
):
    heads = behind.shape[0]
    rows = out0.shape[1]
    outs = (out0, out1, out2, out3)
    edge = dkv1.shape[2] - WINDOW
    held = [(dq1, dkv1, sums1, number) for number in range(dkv1.shape[0])]
    held += [(dq2, dkv2, sums2, number) for number in range(dkv2.shape[0])]
    parts = []
    for head, (dq, dkvt, _, number) in enumerate(held):
        at = slice(number * HEAD_DIM, (number + 1) * HEAD_DIM)
        last = dkvt[number, :, edge:] + behind[head].astype(single)
        parts.append(jnp.concatenate([dq0[head * HEAD_DIM : (head + 1) * HEAD_DIM, :], dq[at, :]], axis=1))
        parts.append(jnp.concatenate([dkvt[number, :, :edge], last], axis=1).astype(bfloat))
    whole = jnp.concatenate(parts, axis=0)

    def put(place, lane):
        outs[place][...] = whole[:, lane * rows : (lane + 1) * rows]

    by_lane(order[0], put)
    total = None
    for lane in range(len(outs)):
        term = dot(whole[:, lane * rows : (lane + 1) * rows], normed[lane])
        total = term if total is None else total + term
    total = total.astype(bfloat)
    part = grad.shape[2]
    count = total.shape[0]
    found = []
    for _, _, ref, number in held:
        value = None
        for chunk in range(CHUNKS):
            term = lax.dot_general(
                jnp.broadcast_to(ref[number, chunk : chunk + 1, :], (8, 2 * QB)),
                hot[chunk * 2 * QB : (chunk + 1) * 2 * QB, :],
                (NN, ((), ())),
                precision=lax.Precision.HIGHEST,
                preferred_element_type=single,
            )
            value = term if value is None else value + term
        found.append(value[0:1, :])
    found.append(jnp.zeros((1, part - BUCKETS * heads), single))
    rel = jnp.broadcast_to(jnp.concatenate(found, axis=1), (16, part))
    router = (router0[...] + router1[...]).astype(bfloat)
    chunk = grad.shape[1]
    blocks = grad.shape[0] // len(outs)
    for lane in range(len(outs)):
        columns = slice(lane * part, (lane + 1) * part)
        mine = jnp.where(order[0] == lane, 1.0, 0.0)
        terms = jnp.broadcast_to(gain_terms[:, columns], (16, part))
        rows_out = [total[:, columns], (rel * mine).astype(bfloat), terms.astype(bfloat), router[:, columns]]
        left = blocks * chunk - sum(value.shape[0] for value in rows_out)
        if left:
            rows_out.append(jnp.zeros((left, part), bfloat))
        rows_out = jnp.concatenate(rows_out, axis=0)
        for block in range(blocks):
            grad[lane * blocks + block] = rows_out[block * chunk : (block + 1) * chunk, :]


def settle(order, dq0, late, behind, normed, sums, hot, gain_terms, routers, blocks):
    lanes, rows, width = normed.shape
    tall = 3 * width // lanes
    count = tall + 32 + routers[0].shape[0]
    count = -(-count // max(16, blocks)) * max(16, blocks)
    cut = blocks if count // blocks % 16 == 0 else 1
    (dq1, dkv1), (dq2, dkv2) = late
    return once(
        settle_kernel,
        "settle",
        (order, dq0, dq1, dq2, dkv1, dkv2, behind, normed, *sums, hot, gain_terms, *routers),
        [((tall, rows), bfloat)] * lanes + [((lanes * cut, count // cut, width // lanes), bfloat)],
    )


def middle_kernel(o0, o1, o2, o3, w0, w1, w2, w3, x, gain, code, y_out, send0, send1):
    y = x[...].astype(single)
    for ref, weight in ((o0, w0), (o1, w1), (o2, w2), (o3, w3)):
        y = y + dot(ref[...], weight[...], TN)
    y_out[...] = y
    inverse = lax.rsqrt(jnp.mean(y * y, axis=-1, keepdims=True) + epsilon)
    normed = (y * inverse * gain[...]).astype(bfloat)
    slots = send0.shape[0]
    for number, ref in enumerate((send0, send1)):
        slot = lax.broadcasted_iota(jnp.int32, (slots, y.shape[0]), 0) + number * slots
        pick = ((slot == code[0:1, :]) | (slot == code[1:2, :])).astype(bfloat)
        ref[...] = dot(pick, normed).astype(bfloat)


def middle(ots, w_out, x, gain, code, slots):
    rows, width = x.shape
    return once(
        middle_kernel,
        "middle",
        (*ots, *w_out, x, gain, code),
        [((rows, width), single), ((slots, width), bfloat), ((slots, width), bfloat)],
    )


NOTES = 16


def send_kernel(place, value, *outs):
    begin = 0
    for out in outs:
        count = out.shape[0]
        here = lax.broadcasted_iota(jnp.int32, (count, value.shape[0]), 0) + begin
        pick = ((here == place[0:1, :]) | (here == place[1:2, :])).astype(bfloat)
        out[...] = dot(pick, value[...]).astype(bfloat)
        begin += count


def send_rows(place, value, blocks, counts):
    shapes = [((blocks * count, value.shape[1]), bfloat) for count in counts]
    found = once(send_kernel, "send_rows", (place, value), shapes)
    return [part.reshape(blocks, count, -1) for part, count in zip(found, counts)]


def send_noted_kernel(part, notes, out):
    for block in range(part.shape[0]):
        out[block, NOTES:, :] = part[block]
        out[block, :NOTES, :] = jnp.broadcast_to(notes[...], (NOTES, part.shape[2]))


def send_noted(part, notes):
    blocks, count, width = part.shape
    outputs = [((blocks, count + NOTES, width), bfloat)]
    return once(send_noted_kernel, "send_noted", (part, notes), outputs)[0]


def collect(code, refs):
    total = None
    for number, ref in enumerate(refs):
        slots = ref.shape[0]
        slot = lax.broadcasted_iota(jnp.int32, (code.shape[0], slots), 1) + number * slots
        pick = ((slot == code[:, 0:1]) | (slot == code[:, 1:2])).astype(bfloat)
        part = dot(pick, ref[...])
        total = part if total is None else total + part
    return total


def return_kernel(d0, d1, code, y, gain, cotangent, w0, w1, w2, w3, o0, o1, o2, o3, dy_out, gg_out, *dots):
    dn = collect(code, (d0, d1))
    values = y[...]
    inverse = lax.rsqrt(jnp.mean(values * values, axis=-1, keepdims=True) + epsilon)
    hat = values * inverse
    gg_out[...] = jnp.sum(dn * hat, axis=0, keepdims=True)
    scaled = dn * gain[...]
    dy = cotangent[...].astype(single) + inverse * (scaled - hat * jnp.mean(scaled * hat, axis=-1, keepdims=True))
    dy_out[...] = dy
    low = dy.astype(bfloat)
    for place, (ref, weight) in enumerate(((o0, w0), (o1, w1), (o2, w2), (o3, w3))):
        dots[place][...] = dot(weight[...], low, NT).astype(bfloat)
        dots[place + 4][...] = dot(ref[...], low).astype(bfloat)


def return_rows(d0, d1, code, y, gain, cotangent, w_out, ots):
    rows, width = y.shape
    lanes = len(ots)
    return once(
        return_kernel,
        "return_rows",
        (d0, d1, code, y, gain, cotangent, *w_out, *ots),
        [((rows, width), single), ((1, width), single)]
        + [((width // lanes, rows), bfloat)] * lanes
        + [((width // lanes, width), bfloat)] * lanes,
    )


def finish_kernel(z0, z1, code, y, out):
    out[...] = (y[...] + collect(code, (z0, z1))).astype(bfloat)


def finish(z0, z1, code, y):
    return once(finish_kernel, "finish", (z0, z1, code, y), [(y.shape, bfloat)])[0]


def unpack_kernel(value, wq, wk, wv, gain, q_out, k_out, v_out, router_out, norm_out, rel_out, gain_out):
    blocks, lanes, count, part = value.shape
    heads = part // HEAD_DIM
    mark = 3 * part
    others = None
    for lane in range(lanes):
        rows = jnp.concatenate([value[block, lane] for block in range(blocks)], axis=0)
        whole = rows[:mark, :].astype(single).T
        for head in range(heads):
            at = slice((lane * heads + head) * HEAD_DIM, (lane * heads + head + 1) * HEAD_DIM)
            for number, ref in enumerate((q_out, k_out, v_out)):
                begin = (3 * head + number) * HEAD_DIM
                ref[:, at] = whole[:, begin : begin + HEAD_DIM]
        term = rows[mark : mark + 32 + router_out.shape[1], :].astype(single)
        rel_out[lane : lane + 1, :] = term[0:1, :]
        others = term if others is None else others + term
    norm_out[...] = others[16:17, :]
    router_out[...] = others[32:, :].T
    total = None
    for ref, weight in ((q_out, wq), (k_out, wk), (v_out, wv)):
        term = jnp.sum(ref[...] * weight[...].astype(single), axis=1, keepdims=True)
        total = term if total is None else total + term
    total = jnp.broadcast_to(total / gain[...].astype(single), (part, 128))
    gain_out[...] = total.T[0:1, :]


def unpack(value, wq, wk, wv, gain, experts):
    part, width = wq.shape
    outputs = [((part, width), single)] * 3
    outputs += [((part, experts), single), ((1, part), single), ((value.shape[1], part), single), ((1, part), single)]
    return once(unpack_kernel, "unpack", (value, wq, wk, wv, gain), outputs)


def tail_kernel(order, *refs):
    *pieces, wt, x, gain, dy, out = refs
    dn = None
    for number, ref in enumerate(pieces):
        block = order[number % 4]
        tall = ref.shape[0]
        begin = block * tall
        term = dot(ref[...], wt[pl.ds(pl.multiple_of(begin, 64), tall), :], TN)
        dn = term if dn is None else dn + term
    values = x[...].astype(single)
    inverse = lax.rsqrt(jnp.mean(values * values, axis=-1, keepdims=True) + epsilon)
    hat = values * inverse
    scaled = dn * gain[...]
    out[...] = dy[...] + inverse * (scaled - hat * jnp.mean(scaled * hat, axis=-1, keepdims=True))


def tail(order, pieces, wt, x, gain, dy):
    return once(tail_kernel, "tail", (order, *pieces, wt, x, gain, dy), [(x.shape, single)])[0]


GELU_0 = 0.7978845608028654
GELU_1 = 0.7978845608028654 * 0.044715
FF_BLOCK = 512
ROW_BLOCK = 256


def expert_kernel(
    mine, xs, router, other, w1, da, cot, g10, g11, g12, g13, g2, dx_out, a_out, m_out, total, dgate, gate, act_all, du_all, xst, dzt
):
    step = pl.program_id(0)
    rows = xs.shape[0]
    experts = router.shape[0]

    def picks():
        lane = lax.broadcasted_iota(jnp.int32, (rows, experts), 1)
        return lane == mine[0], lane == other[...] - 1

    @pl.when(step == 0)
    def _():
        logits = dot(xs[...], router[...], NT)
        own, rest = picks()
        margin = jnp.sum(jnp.where(own, logits, 0.0) - jnp.where(rest, logits, 0.0), axis=1, keepdims=True)
        value = 1.0 / (1.0 + jnp.exp(-margin))
        value = jnp.where(other[...] > 0, value, 0.0)
        gate[...] = jnp.broadcast_to(value, gate.shape)
        dgate[...] = jnp.zeros_like(dgate)
        total[...] = jnp.zeros_like(total)
        for begin in range(0, rows, ROW_BLOCK):
            at = slice(begin, begin + ROW_BLOCK)
            xst[:, at] = xs[at, :].T
            dzt[:, at] = (cot[at, :].astype(single) * gate[at, 0:1]).astype(bfloat).T

    for begin in range(0, rows, ROW_BLOCK):
        at = slice(begin, begin + ROW_BLOCK)
        u = dot(xs[at, :], w1[...])
        square = u * u
        tan = jnp.tanh(u * (GELU_0 + GELU_1 * square))
        half = 0.5 + 0.5 * tan
        act = u * half
        slope = half + act * (1.0 - half) * (2.0 * GELU_0 + 6.0 * GELU_1 * square)
        back = da[at, :].astype(single)
        product = act * back
        part = product[:, :128]
        for col in range(128, product.shape[1], 128):
            part = part + product[:, col : col + 128]
        dgate[at, :] += part
        act_all[at, :] = act.astype(bfloat)
        a_out[at, :] = (act * gate[at, 0:1]).astype(bfloat)
        du_all[at, :] = (gate[at, 0:1] * back * slope).astype(bfloat)
    total[...] += dot(du_all[...], w1[...], NT)
    grad = dot(xst[...], du_all[...]).astype(bfloat)
    part = g10.shape[0]

    def put(place, lane):
        (g10, g11, g12, g13)[place][...] = grad[lane * part : (lane + 1) * part, :]

    by_lane(mine[1], put)
    g2[...] = dot(dzt[...], act_all[...]).astype(bfloat).T

    @pl.when(step == pl.num_programs(0) - 1)
    def _():
        own, rest = picks()
        value = gate[:, 0:1]
        weight = value * (1.0 - value) * jnp.sum(dgate[...], axis=1, keepdims=True)
        m = (weight * (own.astype(single) - rest.astype(single))).astype(bfloat)
        m_out[...] = dot(m, xs[...], TN)
        dx_out[...] = (total[...] + dot(m, router[...])).astype(bfloat)


def expert(mine, xs, router, other, w1, da, cot, local):
    rows, width = xs.shape
    inner = w1.shape[2]
    experts = router.shape[0]
    block = FF_BLOCK
    whole = lambda shape: pl.BlockSpec(shape, lambda f: (0,) * len(shape))
    return pl.pallas_call(
        expert_kernel,
        grid=(inner // block,),
        in_specs=[
            SMEM,
            whole((rows, width)),
            whole((experts, width)),
            whole((rows, 1)),
            pl.BlockSpec((None, width, block), lambda f: (local, 0, f)),
            pl.BlockSpec((rows, block), lambda f: (0, f)),
            whole((rows, width)),
        ],
        out_specs=[
            *[pl.BlockSpec((width // len(MASKS), block), lambda f: (0, f))] * len(MASKS),
            pl.BlockSpec((block, width), lambda f: (f, 0)),
            whole((rows, width)),
            pl.BlockSpec((rows, block), lambda f: (0, f)),
            whole((experts, width)),
        ],
        out_shape=[
            *[jax.ShapeDtypeStruct((width // len(MASKS), inner), bfloat)] * len(MASKS),
            jax.ShapeDtypeStruct((inner, width), bfloat),
            jax.ShapeDtypeStruct((rows, width), bfloat),
            jax.ShapeDtypeStruct((rows, inner), bfloat),
            jax.ShapeDtypeStruct((experts, width), single),
        ],
        scratch_shapes=[
            pltpu.VMEM((rows, width), single),
            pltpu.VMEM((rows, 128), single),
            pltpu.VMEM((rows, 128), single),
            pltpu.VMEM((rows, block), bfloat),
            pltpu.VMEM((rows, block), bfloat),
            pltpu.VMEM((width, rows), bfloat),
            pltpu.VMEM((width, rows), bfloat),
        ],
        compiler_params=params(60, 1),
        cost_estimate=cost(20 * rows * width * inner, 8 * rows * inner + 8 * width * inner, rows * inner),
        name="expert",
    )(mine, xs, router, other, w1, da, cot)


def tie(*values):
    return lax.optimization_barrier(values)


def swap(value, axis, mask):
    return lax.ppermute(value, axis, [(i, i ^ mask) for i in range(lax.axis_size(axis))])


def per_device(
    hidden_in,
    norm1_gain,
    w_query,
    w_key,
    w_value,
    w_out,
    rel_bias,
    norm2_gain,
    w_router,
    w_first,
    w_second,
    routes,
    priority,
    segments,
    grad_out,
):
    lanes = lax.axis_size("head")
    blocks = lax.axis_size("seq")
    lane = lax.axis_index("head")
    place = lax.axis_index("seq")
    rows, width = hidden_in.shape[2:]
    x = hidden_in.reshape(rows, width)
    total = rows * lanes
    part = width // lanes
    heads = part // HEAD_DIM
    cotangent = grad_out.reshape(rows, width)
    experts = w_router.shape[1]
    local = w_first.shape[0]
    slot_rows = max(2, 4 * rows // experts)
    slots = blocks * slot_rows
    capacity = 5 * rows * lanes // (2 * local)

    far = swap(x, "head", 2)
    near = swap(x, "head", 1)
    order = jnp.stack([lane, lane ^ 2, lane ^ 1, lane ^ 3]).astype(jnp.int32)
    at = lambda value, mask: lax.dynamic_index_in_dim(value, lane ^ mask, 0, keepdims=False)

    def trade(value):
        return [value[0]] + [swap(value[place], "head", MASKS[place]) for place in range(1, lanes)]

    route_t = routes.reshape(rows, -1).T
    top_count = route_t.shape[0]
    pair_routes = route_t.reshape(-1)
    pair_prio = priority.reshape(rows, -1).T.reshape(-1)
    expert_ids = jnp.arange(experts, dtype=jnp.int32)
    pair_hot = (expert_ids[:, None] == pair_routes[None, :]).astype(jnp.int32)
    earlier = (pair_routes[:, None] == pair_routes[None, :]) & (pair_prio[:, None] < pair_prio[None, :])
    local_rank = jnp.sum(earlier.astype(jnp.int32), axis=0)
    code = (pair_routes % local) * slots + (pair_routes // local) * slot_rows + local_rank
    code_t = code.reshape(top_count, rows)
    code = code_t.T
    one, two, three = slot_rows * 3 // 10, slot_rows * 8 // 10, slot_rows // 2
    counts = (one, two - one, slot_rows - two + three, slot_rows - three)
    held = ((0, 0, one, 0, 0), (0, one, two, 1, 0), (0, two, slot_rows, 2, 0), (1, 0, three, 2, slot_rows - two))
    send_place = jnp.zeros_like(local_rank)
    for owner, lowest, highest, number, skip in held + ((1, three, slot_rows, 3, 0),):
        inside = (pair_routes % local == owner) & (local_rank >= lowest) & (local_rank < highest)
        row = blocks * sum(counts[:number]) + (pair_routes // local) * counts[number] + skip
        send_place = send_place + jnp.where(inside, row + local_rank - lowest, 0)
    send_place = send_place.reshape(top_count, rows)

    def exchange(value):
        return lax.all_to_all(
            value.reshape(blocks, slot_rows, -1), "seq", split_axis=0, concat_axis=0, tiled=True
        ).reshape(slots, -1)


    block_rank = (jnp.min(pair_prio) // (top_count * rows)).reshape(1)
    tally = jnp.concatenate([jnp.sum(pair_hot, axis=1), block_rank, jnp.zeros((part - experts - 1,), jnp.int32)])
    gains = jnp.stack([norm1_gain, norm2_gain, tally.astype(bfloat)])
    gains = jnp.concatenate([gains, jnp.zeros((GAINS - 3, part), bfloat)], axis=0)
    hot, allowed = lane_tables()
    table = rel_bias.reshape(heads, BUCKETS)
    vecs = dot(table, jnp.asarray(hot.T, bfloat)).reshape(heads, CHUNKS, 2 * QB)
    vecs = jnp.where(jnp.asarray(allowed)[None], vecs, MASKED)
    vecs = jnp.concatenate([vecs, jnp.zeros((heads, 8 - CHUNKS, 2 * QB), single)], axis=1)
    base = place * total
    own = lax.dynamic_slice_in_dim(segments, base, total, 0)
    low = jnp.zeros_like(own)
    for number in range(1, 4):
        low = jnp.where(own == number, jnp.sum((segments < number).astype(jnp.int32)), low)
    low = low - base + WINDOW
    need = (jnp.max(low.reshape(-1, QB), axis=1) > jnp.arange(total // QB) * QB).astype(jnp.int32)
    low = low.reshape(1, total)
    packed = trade(pack(order, w_query, w_key, w_value, w_router.T, gains))
    cot_parts = send_rows(send_place, cotangent, blocks, counts)
    spread_out = lambda value: lax.all_to_all(value, "seq", split_axis=0, concat_axis=0, tiled=True)
    cots = [spread_out(cot_parts[0])]
    far, near, packed, cots, cot_parts, low, need, vecs, code = tie(
        far, near, packed, cots, cot_parts, low, need, vecs, code
    )
    both = swap(far, "head", 1)
    cots.append(spread_out(cot_parts[1]))
    both, w_second, w_out = tie(both, w_second, w_out)

    out_far = swap(w_out, "head", 2)
    out_near = swap(w_out, "head", 1)
    second_full = lax.all_gather(w_second, "head", axis=1, tiled=True)

    normed, qt, kv, kv_last, w_rows, router_t, gains = project(order, (x, far, near, both), packed, heads, experts)
    w_rows_full = lax.all_gather(w_rows, "head", axis=0, tiled=True)
    gain_one, gain_two = gains[0:1], gains[1:2]
    kvp = lax.ppermute(kv_last, "seq", [(i, i + 1) for i in range(blocks - 1)])
    early = WINDOW // QB
    later = total // QB - early
    *ot, lse_later = attention_forward(early, later, order, need, low, qt, None, kv, vecs, lanes)
    noted = send_noted(cot_parts[3], gains[2:3].astype(bfloat))
    ot, kvp, cots[1], cot_parts[2], noted = tie(ot, kvp, cots[1], cot_parts[2], noted)
    cots.append(spread_out(cot_parts[2]))
    *ot, lse_early = attention_forward(0, early, order, need, low, qt, kvp, kv, vecs, lanes, ot)
    ot, out_far, out_near = tie(ot, out_far, out_near)
    w_outs = (w_out, out_far, out_near, swap(out_far, "head", 1))
    ots = trade(ot)
    ots, w_first, cots[2] = tie(ots, w_first, cots[2])
    noted = spread_out(noted)
    first_full = lax.all_gather(w_first, "head", axis=1, tiled=True)

    y, *sends = middle(ots, w_outs, x, gain_two, code_t, slots)
    sends[0], noted = tie(sends[0], noted)

    tallies = noted[:, 0, :].reshape(blocks * lanes, part).astype(jnp.int32)
    ahead = (tallies[:, experts : experts + 1] < block_rank[None, :]).astype(jnp.int32)
    offsets = jnp.sum(tallies[:, :experts] * ahead, axis=0)
    kept = (jnp.sum(pair_hot * offsets[:, None], axis=0) + local_rank < capacity).reshape(top_count, rows)
    slot_ids = jnp.arange(local * slots, dtype=jnp.int32)[:, None]
    other = jnp.sum(
        jnp.where(slot_ids == code_t[0:1], jnp.where(kept[0:1], route_t[1:2] + 1, 0), 0)
        + jnp.where(slot_ids == code_t[1:2], jnp.where(kept[1:2], route_t[0:1] + 1, 0), 0),
        axis=1,
    )
    last = slot_rows - two
    cot_slots = [[cots[0], cots[1], cots[2][:, :last]], [cots[2][:, last:], noted[:, NOTES:, :]]]
    cot_slots = [jnp.concatenate(value, axis=1).reshape(slots, width) for value in cot_slots]
    backs = [dot(cot_slots[0], second_full[0], NT).astype(bfloat)]
    other, backs[0] = tie(other, backs[0])
    other = other.reshape(local, blocks, slot_rows)
    far_others = [
        swap(lax.dynamic_index_in_dim(other, place ^ mask, 1, keepdims=False), "seq", mask) for mask in range(1, blocks)
    ]
    mine = jnp.stack([place * local, lane]).astype(jnp.int32)
    backs.append(dot(cot_slots[1], second_full[1], NT).astype(bfloat))
    received = [exchange(sends[0])]
    sends[1], far_others, *backs = tie(sends[1], far_others, *backs)
    received.append(exchange(sends[1]))
    far_others = jnp.concatenate([lax.dynamic_index_in_dim(other, place, 1, keepdims=False)[None], jnp.stack(far_others)])
    other = jnp.stack(
        [lax.dynamic_index_in_dim(far_others, place ^ number, 0, keepdims=False) for number in range(blocks)], axis=1
    ).reshape(local, slots, 1)

    def run_expert(number):
        return expert(
            mine + jnp.asarray([number, 0], jnp.int32),
            received[number],
            router_t,
            other[number],
            first_full,
            backs[number],
            cot_slots[number],
            number,
        )

    received[1], w_rows_full, (*first_parts0, second0, dx0, act0, router0) = tie(
        received[1], w_rows_full, run_expert(0)
    )
    returns = [exchange(dx0)]
    second0 = lax.psum_scatter(second0, "head", scatter_dimension=0, tiled=True)
    returns[0], second0, (*first_parts1, second1, dx1, act1, router1) = tie(returns[0], second0, run_expert(1))
    def near_parts(parts):
        return swap(parts[3], "head", 1), swap(parts[2], "head", 1)

    def add(one, two, kind=single):
        return (one.astype(single) + two.astype(single)).astype(kind)

    def scatter(value):
        return lax.psum_scatter(value, "head", scatter_dimension=0, tiled=True)

    cross0, direct0 = near_parts(first_parts0)
    returns.append(exchange(dx1))
    away0, act0, act1 = tie(add(first_parts0[1], cross0, bfloat), act0, act1)
    across0 = swap(away0, "head", 2)
    cross1, direct1 = near_parts(first_parts1)
    second1 = scatter(second1)

    z0, z1 = (dot(act, second_full[i]).astype(bfloat) for i, act in enumerate((act0, act1)))
    away1 = add(first_parts1[1], cross1, bfloat)
    returns[1], across0, z0, z1, away1 = tie(returns[1], across0, z0, z1, away1)
    first0 = add(add(first_parts0[0], direct0), across0)
    dy, gain_terms, *douts = return_rows(
        returns[0], returns[1], code, y, gain_two, cotangent, w_outs, ots
    )
    douts, outw = trade(douts[:lanes]), douts[lanes:]
    outw_cross, outw_direct = near_parts(outw)
    dy, z0 = tie(dy, z0)
    z_back = [exchange(z0)]
    douts, outw_cross, outw_direct = tie(douts, outw_cross, outw_direct)

    def sum_blocks(value):
        last = value.shape[-1]
        value = value.reshape(lanes * blocks, -1, last)
        value = lax.all_to_all(value, ("head", "seq"), split_axis=0, concat_axis=0, tiled=True)
        return jnp.sum(value.reshape(lanes, blocks, -1, last).astype(single), axis=1).astype(bfloat)

    dq_early, behind, dkvt_early, ds_early = attention_backward(
        0, early, (0, heads), order, need, low, qt, kvp, kv, vecs, lse_early, douts
    )
    behind = lax.ppermute(behind, "seq", [(i + 1, i) for i in range(blocks - 1)])
    dq_early, second1 = tie(dq_early, second1)
    outw_across = swap(add(outw[1], outw_cross, bfloat), "head", 2)
    hops = [1 << bit for bit in range(blocks.bit_length() - 1)]

    def hop(value, masks):
        for mask in masks:
            value = add(value, swap(value, "seq", mask), bfloat)
        return value

    cut = heads - 1

    def later_part(span):
        return attention_backward(
            early, later, span, order, need, low, qt, None, kv, vecs, lse_later, douts, (dkvt_early, ds_early)
        )

    dq_last, dkv_last, sums_last = later_part((cut, heads - cut))
    dkv_last, z_back[0], z1, behind, outw_across, away1 = tie(
        dkv_last, z_back[0], z1, behind, outw_across, away1
    )
    across1 = swap(away1, "head", 2)
    grad_outw = add(add(outw[0], outw_direct), outw_across, bfloat)
    grad_outw = hop(grad_outw, hops[:-2])
    z_back.append(exchange(z1))
    ds_early, dkv_last = tie(ds_early, dkv_last)
    dq_first, dkv_first, sums_first = later_part((0, cut))
    dq_first, grad_outw, across1 = tie(dq_first, grad_outw, across1)
    grad_outw = hop(grad_outw, hops[-2:-1])
    *parts, grad_part = settle(
        order,
        dq_early,
        ((dq_first, dkv_first), (dq_last, dkv_last)),
        behind,
        normed,
        (sums_first, sums_last),
        jnp.asarray(hot, single),
        gain_terms,
        (router0, router1),
        blocks,
    )
    pieces = trade(parts)
    first1 = add(add(first_parts1[0], direct1), across1)
    grad_part, z_back[1] = tie(grad_part, z_back[1])
    value = sum_blocks(grad_part)
    output = finish(z_back[0], z_back[1], code, y).reshape(hidden_in.shape)
    value, grad_outw, pieces[1], pieces[2] = tie(value, grad_outw, pieces[1], pieces[2])
    grad_outw = hop(grad_outw, hops[-1:])
    count = value.shape[1]
    value = lax.all_to_all(
        jnp.broadcast_to(value[None], (blocks,) + value.shape), "seq", split_axis=0, concat_axis=0, tiled=True
    )
    grad_hidden = tail(order, pieces, w_rows_full, x, gain_one, dy).reshape(hidden_in.shape)
    value, grad_hidden, output = tie(value, grad_hidden, output)
    if count % 16:
        value = value.transpose(1, 0, 2, 3).reshape(1, lanes, -1, part)
    *grads, grad_router, grad_norm2, rels, grad_norm1 = unpack(value, w_query, w_key, w_value, norm1_gain.reshape(part, 1), experts)
    grad_rel = lax.dynamic_index_in_dim(rels, lane, 0, keepdims=False)[: heads * BUCKETS]
    return (
        output,
        grad_hidden,
        grad_norm1.reshape(part),
        grads[0],
        grads[1],
        grads[2],
        grad_outw.astype(single),
        grad_rel,
        grad_norm2.reshape(part),
        grad_router,
        jnp.stack([first0, first1]),
        jnp.stack([second0, second1]).astype(single),
    )


def solution(mesh):
    return jax.shard_map(
        per_device,
        mesh=mesh,
        in_specs=(
            P("seq", "head", None, None),
            P("head"),
            P("head", None),
            P("head", None),
            P("head", None),
            P("head", None),
            P("head"),
            P("head"),
            P("head", None),
            P("seq", "head", None),
            P("seq", "head", None),
            P("seq", "head", None, None),
            P("seq", "head", None, None),
            P(),
            P("seq", "head", None, None),
        ),
        out_specs=(
            P("seq", "head", None, None),
            P("seq", "head", None, None),
            P("head"),
            P("head", None),
            P("head", None),
            P("head", None),
            P("head", None),
            P("head"),
            P("head"),
            P("head", None),
            P("seq", "head", None),
            P("seq", "head", None),
        ),
        check_vma=False,
    )
```
